32 devices in a mesh: groups: 2 (over y), inst: 4 (over z), tp: 4 (over x, core).
Axes of the slice: x: 2, y: 2, z: 4, core: 2. Of those that a mesh axis runs over, the one named last changes fastest.
Arguments:
- kv_pool: bfloat16 [128, 2, 512, 1024], P(('groups', 'inst'), None, None, 'tp'), parts along dimension 0, may hold values from -16 to 16
- page_table: int32 [64, 8], P(('groups', 'inst')), parts along dimension 0, may hold values from 0 to 15, as said below
- lengths: int32 [64], P(('groups', 'inst')), parts along dimension 0, may hold values from 1 to 4096, as said below
- queries: bfloat16 [64, 2, 8192], P(('groups', 'inst'), None, 'tp'), parts along dimension 0, may hold values from -8 to 8
- new_kv: bfloat16 [64, 2, 2, 1024], P(('groups', 'inst'), None, None, 'tp'), parts along dimension 0, may hold values from -6 to 6
- moves: int32 [8, 2], P('groups'), parts along dimension 0, may hold values from 0 to 31, as said below
Outputs:
- attended: bfloat16 [64, 2, 8192], P(('groups', 'inst'), None, 'tp'), parts along dimension 0
The draws below stay inside these ranges and needn't reach their ends.
There are 2 independent parts, one for each index of `groups`. The reference program is written for one: setup_inputs(seed, part) draws one part's arguments, and reference() takes and returns one part's arrays. A program takes and returns all parts, laid end to end along the dimension named above; each array names one. Nothing has to cross between parts.
Inputs may be any that keep to these rules, and one draw needn't show every extreme that they name: Slot i holds ceil(lengths[i] / 512) cache blocks, listed first in its page table; the blocks of the slots of one instance are distinct; some slot holds exactly 4096 tokens. `page_table`: entries past a slot's block count are valid block numbers of the same pool. The two entries of a move lie on different instances; no slot appears twice in the list; half of the instances hold the cache slots of exactly 2 moves and no hidden slot, the other half exactly 2 hidden slots and no cache slot; no two moves join the same pair of instances.
All inputs are finite; a program needn't handle non-finite values.
Results may differ from the reference program's by a relative error of at most 0.0025.
Values may be sent and summed in bfloat16 or wider, within the bound.
No kernel may reach another device: no remote copies, remote signals or barrier semaphores. Data moves between devices by JAX's collectives and lax.ppermute only.
A program may use at most 64 MiB of HBM per device.

```python
import math
import jax
import jax.numpy as jnp
from jax import lax

H = 64
KVH = 8
HD = 128
BLOCK = 512
STEPS = 2
MAXB = 8
CAP = 2
ROWS_INST = 8
SLOTS = 16
ROWS = 32
POOL = 64
MOVES = 4


def layout(key):
    key = jax.random.fold_in(key, 907)
    subkeys = jax.random.split(key, 8)
    inst_count = ROWS // ROWS_INST
    half_count = inst_count // 2
    shuffle = jax.random.permutation(subkeys[0], inst_count)
    position = jnp.argsort(shuffle)
    is_busy = position < half_count
    slot_ids = jnp.arange(ROWS_INST)
    tall_row = jax.random.randint(subkeys[1], (inst_count,), 0, ROWS_INST)
    spare_pick = jax.random.randint(subkeys[2], (inst_count,), 0, ROWS_INST - 1)
    spare_row = jnp.where(spare_pick >= tall_row, spare_pick + 1, spare_pick)
    busy_counts = 1 + (MAXB - 1) * (slot_ids[None, :] == tall_row[:, None]) + (slot_ids[None, :] == spare_row[:, None])
    counts = jnp.where(is_busy[:, None], busy_counts, 1).astype(jnp.int32)
    tail_tokens = jax.random.randint(subkeys[3], (inst_count, ROWS_INST), 1, BLOCK + 1)
    full_row = is_busy[:, None] & (slot_ids[None, :] == tall_row[:, None])
    tail_tokens = jnp.where(full_row, BLOCK, tail_tokens)
    row_lengths = ((counts - 1) * BLOCK + tail_tokens).astype(jnp.int32)
    pool_orders = jax.vmap(lambda sub: jax.random.permutation(sub, SLOTS))(jax.random.split(subkeys[4], inst_count))
    first_block = jnp.cumsum(counts, axis=1) - counts
    offsets = (first_block[:, :, None] + jnp.arange(MAXB)[None, None, :]) % SLOTS
    pages = jax.vmap(lambda order_row, offset_rows: order_row[offset_rows])(pool_orders, offsets)
    busy_list = shuffle[:half_count]
    unused_list = shuffle[half_count:]
    move_ids = jnp.arange(MOVES)
    busy_index = move_ids // CAP
    turn_index = move_ids % CAP
    stride = jax.random.randint(subkeys[5], (), 1, half_count)
    source_inst = busy_list[busy_index]
    target_inst = unused_list[(busy_index + turn_index * stride) % half_count]
    out_orders = jax.vmap(lambda sub: jax.random.permutation(sub, ROWS_INST))(jax.random.split(subkeys[6], inst_count))
    in_orders = jax.vmap(lambda sub: jax.random.permutation(sub, ROWS_INST))(jax.random.split(subkeys[7], inst_count))
    source_slot = source_inst * ROWS_INST + out_orders[source_inst, turn_index]
    target_slot = target_inst * ROWS_INST + in_orders[target_inst, turn_index]
    move_list = jnp.stack([source_slot, target_slot], axis=1).astype(jnp.int32)
    return (row_lengths.reshape(ROWS), pages.reshape(ROWS, MAXB).astype(jnp.int32), move_list)


def draw_lengths(key, part):
    tables = layout(key)
    return tables[0]


def draw_page_table(key, part):
    tables = layout(key)
    return tables[1]


def draw_moves(key, part):
    tables = layout(key)
    return tables[2]


def draw_queries(key, part):
    key = jax.random.fold_in(key, 11)
    subkeys = jax.random.split(key, 1)
    result = jnp.clip(jax.random.normal(subkeys[0], (ROWS, STEPS, H, HD), jnp.float32), -4.0, 4.0)
    return result.reshape(ROWS, STEPS, H * HD).astype(jnp.bfloat16)


def draw_kv_pool(key, part):
    key = jax.random.fold_in(key, 12)
    subkeys = jax.random.split(key, 2)
    scales = jnp.exp(jax.random.uniform(subkeys[1], (POOL, 1, BLOCK, KVH, 1), jnp.float32, jnp.log(0.3), jnp.log(3.0)))
    result = jnp.clip(jax.random.normal(subkeys[0], (POOL, 2, BLOCK, KVH, HD), jnp.float32), -4.0, 4.0) * scales
    return result.reshape(POOL, 2, BLOCK, KVH * HD).astype(jnp.bfloat16)


def level_of(rng, shape, cuts, least, largest):
    factor_of = 1.0
    for axis_at, shards_of in cuts:
        draws = jax.random.uniform(jax.random.fold_in(jax.random.fold_in(rng, 6), axis_at), (shards_of,), jnp.float32, least / len(cuts), largest / len(cuts))
        factor_of = factor_of * jnp.repeat(jnp.exp(draws), shape[axis_at] // shards_of).reshape((-1,) + (1,) * (len(shape) - 1 - axis_at))
    return factor_of


def centred(own_key, extent, scale, reach, cuts=(), kind=jnp.bfloat16):
    values = scale * jax.random.normal(own_key, extent, jnp.float32)
    if cuts:
        values = values * level_of(own_key, extent, cuts, -0.22, 0.18)
    return jnp.clip(values, -reach, reach).astype(kind)


def setup_inputs(seed: int = 0, part: int = 0) -> dict:
    key_list = jax.random.split(jax.random.key(seed), 7)
    part_splits = jax.random.split(jax.random.fold_in(key_list[6], part), 7)
    return {
        "kv_pool": draw_kv_pool(jax.random.fold_in(jax.random.fold_in(key_list[6], part), 71), part),
        "page_table": draw_page_table(jax.random.fold_in(jax.random.fold_in(key_list[6], part), 71), part),
        "lengths": draw_lengths(jax.random.fold_in(jax.random.fold_in(key_list[6], part), 71), part),
        "queries": draw_queries(jax.random.fold_in(jax.random.fold_in(key_list[6], part), 71), part),
        "new_kv": centred(part_splits[4], (ROWS, STEPS, 2, KVH * HD), 1.0, 6.0, ((0, 4), (3, 4))),
        "moves": draw_moves(jax.random.fold_in(jax.random.fold_in(key_list[6], part), 71), part),
    }


def attend(query, fresh, blocks, length):
    groups = blocks.shape[-1] // HD
    per_group = query.shape[-1] // (groups * HD)
    steps_count = query.shape[0]
    token_count = blocks.shape[0] * blocks.shape[2]
    cache_keys = blocks[:, 0].reshape(token_count, groups, HD).astype(jnp.float32)
    cache_values = blocks[:, 1].reshape(token_count, groups, HD).astype(jnp.float32)
    fresh_keys = fresh[:, 0].reshape(steps_count, groups, HD).astype(jnp.float32)
    fresh_values = fresh[:, 1].reshape(steps_count, groups, HD).astype(jnp.float32)
    query_heads = query.reshape(steps_count, groups, per_group, HD).astype(jnp.float32)
    score_scale = 1.0 / math.sqrt(HD)
    cached = jnp.einsum('sgqd,tgd->sgqt', query_heads, cache_keys) * score_scale
    recent = jnp.einsum('sgqd,ugd->sgqu', query_heads, fresh_keys) * score_scale
    in_range = (jnp.arange(token_count) < length)[None, None, None, :]
    step_order = (jnp.arange(steps_count)[None, :] <= jnp.arange(steps_count)[:, None])[:, None, None, :]
    cached = jnp.where(in_range, cached, -1e+30)
    recent = jnp.where(step_order, recent, -1e+30)
    row_max = jnp.maximum(lax.optimization_barrier(jnp.max(cached, axis=3, keepdims=True)), lax.optimization_barrier(jnp.max(recent, axis=3, keepdims=True)))
    cached_exp = jnp.exp(cached - row_max)
    recent_exp = jnp.exp(recent - row_max)
    denominator = lax.optimization_barrier(jnp.sum(cached_exp, axis=3)) + lax.optimization_barrier(jnp.sum(recent_exp, axis=3))
    cached_weight = lax.optimization_barrier(cached_exp.astype(jnp.bfloat16)).astype(jnp.float32)
    recent_weight = lax.optimization_barrier(recent_exp.astype(jnp.bfloat16)).astype(jnp.float32)
    weighted = jnp.einsum('sgqt,tgd->sgqd', cached_weight, cache_values)
    weighted = weighted + jnp.einsum('sgqu,ugd->sgqd', recent_weight, fresh_values)
    result = (weighted / denominator[..., None]).astype(jnp.bfloat16)
    return result.reshape(steps_count, groups * per_group * HD)

def reference(kv_pool, page_table, lengths, queries, new_kv, moves):
    cache_source = jnp.arange(ROWS, dtype=jnp.int32).at[moves[:, 1]].set(moves[:, 0].astype(jnp.int32))
    vacated = jnp.zeros((ROWS,), jnp.int32).at[moves[:, 0]].set(1)

    def attend_slot(slot_index):
        anchor = cache_source[slot_index]
        page_list = (page_table[anchor] + anchor // ROWS_INST * SLOTS).astype(jnp.int32)
        blocks = jnp.take(kv_pool, page_list, axis=0)
        return attend(queries[slot_index], new_kv[slot_index], blocks, lengths[anchor])
    attended = lax.map(attend_slot, jnp.arange(ROWS, dtype=jnp.int32))
    return jnp.where(vacated[:, None, None] > 0, jnp.zeros_like(attended), attended)
```

```python
import functools
import math

import jax
import jax.numpy as jnp
from jax import lax
from jax.experimental import pallas as pl
from jax.experimental.pallas import tpu as pltpu
from jax.sharding import PartitionSpec as P

HD = 128
NEG = -1e30
SMEM = pltpu.SMEM
VMEM = pltpu.VMEM
ANY = pl.ANY


def find_moves(moves, rows_inst, n, me, hidden, cache):
    for d in range(n):
        if hidden is not None:
            hidden[d] = -1
        if cache is not None:
            cache[d] = -1

    def step(m, carry):
        cache_slot = moves[m, 0]
        hidden_slot = moves[m, 1]
        from_inst = cache_slot // rows_inst
        to_inst = hidden_slot // rows_inst
        shift = lax.rem(from_inst - to_inst + n, n)
        if hidden is not None:
            hidden[jnp.where(to_inst == me, shift, 0)] = lax.rem(hidden_slot, rows_inst)
        if cache is not None:
            cache[jnp.where(from_inst == me, shift, 0)] = lax.rem(cache_slot, rows_inst)
        return carry

    lax.fori_loop(0, moves.shape[0], step, 0)


def pack_kernel(n, moves, q, kv, *refs):
    outs, hidden = refs[: n - 1], refs[n - 1]
    rows_inst = q.shape[0]
    heads = q.shape[1]
    me = lax.axis_index("inst")
    find_moves(moves, rows_inst, n, me, hidden, None)
    for d in range(1, n):
        slot = jnp.maximum(hidden[d], 0)
        outs[d - 1][0:heads, :] = q[slot]
        outs[d - 1][heads:, :] = kv[slot]


def attend_kernel(n, moves, page_table, lengths, q, kv, pool, *refs):
    recv = refs[: n - 1]
    out = refs[n - 1]
    back = refs[n : 2 * n - 1]
    (cache, owner, limit, vacant, buf, qbd, fk, scores, part_max, top, part_sum, acc, sems) = refs[2 * n - 1 :]
    rows_inst, heads, hd = q.shape
    fresh_rows = kv.shape[1]
    slots, _, block, columns = pool.shape
    groups = columns // hd
    steps = fresh_rows // (2 * groups)
    per = heads // groups
    pages = page_table.shape[1]
    me = lax.axis_index("inst")
    scale = 1.0 / math.sqrt(hd)

    def fetch(p, plane):
        return pltpu.make_async_copy(pool.at[p, plane], buf.at[p, plane], sems.at[p, plane])

    for plane in range(2):
        for p in range(slots):
            fetch(p, plane).start()

    find_moves(moves, rows_inst, n, me, None, cache)
    for p in range(slots + 1):
        owner[p] = rows_inst
        limit[p] = 0
    for r in range(rows_inst):
        length = lengths[r]
        vacant[r] = 0
        for b in range(pages):
            at = jnp.where(b * block < length, page_table[r, b], slots)
            owner[at] = r
            limit[at] = length - b * block

    zero = jnp.zeros((per, hd), jnp.bfloat16)

    def set_row(r, rows, fresh):
        for g in range(groups):
            for k in range(groups):
                qbd[r, g * per : (g + 1) * per, k * hd : (k + 1) * hd] = (
                    rows[g * per : (g + 1) * per] if k == g else zero
                )
        fk[r] = fresh.astype(jnp.float32)

    for r in range(rows_inst):
        set_row(r, q[r], kv[r])
    set_row(rows_inst, q[0], kv[0])
    for d in range(1, n):

        @pl.when(cache[d] >= 0)
        def _():
            slot = cache[d]
            set_row(slot, recv[d - 1][0:heads, :], recv[d - 1][heads:, :])
            vacant[slot] = 1

    step_of = lax.broadcasted_iota(jnp.int32, (per, 1), 0) % steps
    fresh_scores = []
    for r in range(rows_inst):
        row_scores = []
        for g in range(groups):
            qg = qbd[r, g * per : (g + 1) * per, g * hd : (g + 1) * hd].astype(jnp.float32)
            line = []
            for u in range(steps):
                key = fk[r, pl.ds((u * groups + g) * 2, 1), :]
                s = jnp.sum(qg * key, axis=1, keepdims=True)
                line.append(jnp.where(step_of >= u, s, NEG))
            row_scores.append(line)
        fresh_scores.append(row_scores)
        first = jnp.concatenate(
            [functools.reduce(jnp.maximum, row_scores[g]) for g in range(groups)], axis=0
        )
        part_max[r] = jnp.broadcast_to(first, (heads, hd))
    part_max[rows_inst] = jnp.zeros((heads, hd), jnp.float32)

    lane = lax.broadcasted_iota(jnp.int32, (heads, block), 1)
    for p in range(slots):
        fetch(p, 0).wait()
        r = owner[p]
        s = lax.dot_general(
            qbd[r], buf[p, 0], (((1,), (1,)), ((), ())), preferred_element_type=jnp.float32
        )
        s = jnp.where(lane < limit[p], s, NEG)
        scores[p] = s
        m = part_max[r]
        for c in range(block // hd):
            m = jnp.maximum(m, s[:, c * hd : (c + 1) * hd])
        part_max[r] = m

    factor = scale * math.log2(math.e)
    for r in range(rows_inst):
        m = jnp.max(part_max[r], axis=1, keepdims=True)
        top[r] = jnp.broadcast_to(m, (heads, hd))
        for g in range(groups):
            mg = m[g * per : (g + 1) * per]
            total = jnp.zeros((per, 1), jnp.float32)
            value = jnp.zeros((per, hd), jnp.float32)
            for u in range(steps):
                e = jnp.exp2((fresh_scores[r][g][u] - mg) * factor)
                total = total + e
                weight = e.astype(jnp.bfloat16).astype(jnp.float32)
                value = value + weight * fk[r, pl.ds((u * groups + g) * 2 + 1, 1), :]
            acc[r, g * per : (g + 1) * per, :] = value
            first_lane = lax.broadcasted_iota(jnp.int32, (per, hd), 1) == 0
            part_sum[r, g * per : (g + 1) * per, :] = jnp.where(first_lane, total, 0.0)
    top[rows_inst] = jnp.zeros((heads, hd), jnp.float32)
    part_sum[rows_inst] = jnp.zeros((heads, hd), jnp.float32)
    acc[rows_inst] = jnp.zeros((heads, hd), jnp.float32)

    for p in range(slots):
        fetch(p, 1).wait()
        r = owner[p]
        m = top[r]
        pieces = []
        total = part_sum[r]
        for c in range(block // hd):
            e = jnp.exp2((scores[p, :, c * hd : (c + 1) * hd] - m) * factor)
            total = total + e
            pieces.append(e.astype(jnp.bfloat16))
        part_sum[r] = total
        weights = jnp.concatenate(pieces, axis=1)
        o = lax.dot_general(
            weights, buf[p, 1], (((1,), (0,)), ((), ())), preferred_element_type=jnp.float32
        )
        acc[r] = acc[r] + jnp.concatenate(
            [o[g * per : (g + 1) * per, g * hd : (g + 1) * hd] for g in range(groups)], axis=0
        )

    for r in range(rows_inst):
        total = jnp.sum(part_sum[r], axis=1, keepdims=True)
        value = acc[r] / total
        acc[r] = value
        out[r] = jnp.where(vacant[r] == 1, 0.0, value).astype(jnp.bfloat16)
    for d in range(1, n):
        back[d - 1][...] = acc[jnp.maximum(cache[d], 0)].astype(jnp.bfloat16)


def place_kernel(n, moves, local, *refs):
    back = refs[: n - 1]
    out, hidden = refs[n - 1 :]
    rows_inst = local.shape[0]
    me = lax.axis_index("inst")
    find_moves(moves, rows_inst, n, me, hidden, None)
    out[...] = local[...]
    for d in range(1, n):

        @pl.when(hidden[d] >= 0)
        def _():
            out[hidden[d]] = back[d - 1][...]


def body(kv_pool, page_table, lengths, queries, new_kv, moves):
    n = lax.axis_size("inst")
    rows_inst, steps, width = queries.shape
    columns = kv_pool.shape[3]
    slots, _, block, _ = kv_pool.shape
    groups = columns // HD
    heads_all = width // HD
    heads = steps * heads_all
    fresh_rows = steps * groups * 2
    bf16 = jnp.bfloat16
    f32 = jnp.float32
    q = queries.reshape(rows_inst, steps, heads_all, HD).transpose(0, 2, 1, 3).reshape(rows_inst, heads, HD)
    kv = (
        new_kv.reshape(rows_inst, steps, 2, groups, HD)
        .transpose(0, 1, 3, 2, 4)
        .reshape(rows_inst, fresh_rows, HD)
    )
    smem = pl.BlockSpec(memory_space=SMEM)
    vmem = pl.BlockSpec(memory_space=VMEM)
    anyspace = pl.BlockSpec(memory_space=ANY)
    forward = [[(i, (i + d) % n) for i in range(n)] for d in range(1, n)]
    backward = [[(i, (i - d) % n) for i in range(n)] for d in range(1, n)]

    packed = pl.pallas_call(
        functools.partial(pack_kernel, n),
        out_shape=[jax.ShapeDtypeStruct((heads + fresh_rows, HD), bf16)] * (n - 1),
        in_specs=[smem, vmem, vmem],
        out_specs=[vmem] * (n - 1),
        scratch_shapes=[SMEM((n,), jnp.int32)],
        name="pack",
    )(moves, q, kv)
    received = [lax.ppermute(x, "inst", perm) for x, perm in zip(packed, forward)]
    results = pl.pallas_call(
        functools.partial(attend_kernel, n),
        out_shape=[jax.ShapeDtypeStruct((rows_inst, heads, HD), bf16)]
        + [jax.ShapeDtypeStruct((heads, HD), bf16)] * (n - 1),
        in_specs=[smem, smem, smem, vmem, vmem, anyspace] + [vmem] * (n - 1),
        out_specs=[vmem] * n,
        scratch_shapes=[
            SMEM((n,), jnp.int32),
            SMEM((slots + 1,), jnp.int32),
            SMEM((slots + 1,), jnp.int32),
            SMEM((rows_inst,), jnp.int32),
            VMEM((slots, 2, block, columns), bf16),
            VMEM((rows_inst + 1, heads, columns), bf16),
            VMEM((rows_inst + 1, fresh_rows, HD), f32),
            VMEM((slots, heads, block), f32),
            VMEM((rows_inst + 1, heads, HD), f32),
            VMEM((rows_inst + 1, heads, HD), f32),
            VMEM((rows_inst + 1, heads, HD), f32),
            VMEM((rows_inst + 1, heads, HD), f32),
            pltpu.SemaphoreType.DMA((slots, 2)),
        ],
        compiler_params=pltpu.CompilerParams(vmem_limit_bytes=24 * 1024 * 1024),
        name="attend",
    )(moves, page_table, lengths, q, kv, kv_pool, *received)
    local, back = results[0], results[1:]
    returned = [lax.ppermute(x, "inst", perm) for x, perm in zip(back, backward)]
    out = pl.pallas_call(
        functools.partial(place_kernel, n),
        out_shape=jax.ShapeDtypeStruct((rows_inst, heads, HD), bf16),
        in_specs=[smem, vmem] + [vmem] * (n - 1),
        out_specs=vmem,
        scratch_shapes=[SMEM((n,), jnp.int32)],
        name="place",
    )(moves, local, *returned)
    return out.reshape(rows_inst, heads_all, steps, HD).transpose(0, 2, 1, 3).reshape(rows_inst, steps, width)


def solution(mesh):
    placed = (
        P(("groups", "inst"), None, None, "tp"),
        P(("groups", "inst"), None),
        P(("groups", "inst")),
        P(("groups", "inst"), None, "tp"),
        P(("groups", "inst"), None, None, "tp"),
        P("groups", None),
    )
    return jax.shard_map(
        body,
        mesh=mesh,
        in_specs=placed,
        out_specs=P(("groups", "inst"), None, "tp"),
        check_vma=False,
    )
```

```python
import functools
import math

import jax
import jax.numpy as jnp
from jax import lax
from jax.experimental import pallas as pl
from jax.experimental.pallas import tpu as pltpu
from jax.sharding import PartitionSpec as P

HD = 128
NEG = -1e30
SMEM = pltpu.SMEM
VMEM = pltpu.VMEM
HBM = pltpu.HBM


def find_moves(moves, rows_inst, n, me, hidden, cache):
    for d in range(n + 1):
        if hidden is not None:
            hidden[d] = -1
        if cache is not None:
            cache[d] = -1

    def step(m, carry):
        cache_slot = moves[0, m]
        hidden_slot = moves[1, m]
        from_inst = cache_slot // rows_inst
        to_inst = hidden_slot // rows_inst
        if hidden is not None:
            hidden[jnp.where(to_inst == me, from_inst, n)] = lax.rem(hidden_slot, rows_inst)
        if cache is not None:
            cache[jnp.where(from_inst == me, to_inst, n)] = lax.rem(cache_slot, rows_inst)
        return carry

    lax.fori_loop(0, moves.shape[1], step, 0)


def pack_kernel(n, moves_hbm, q_hbm, kv_hbm, out, hidden, moves, q, kv, sems):
    copies = [
        pltpu.make_async_copy(moves_hbm, moves, sems.at[0]),
        pltpu.make_async_copy(q_hbm, q, sems.at[1]),
        pltpu.make_async_copy(kv_hbm, kv, sems.at[2]),
    ]
    for c in copies:
        c.start()
    rows_inst, heads, _ = q.shape
    me = lax.axis_index("inst")
    copies[0].wait()
    find_moves(moves, rows_inst, n, me, hidden, None)
    copies[1].wait()
    copies[2].wait()
    for d in range(n):
        slot = jnp.maximum(hidden[d], 0)
        out[d, 0:heads, :] = q[slot]
        out[d, heads:, :] = kv[slot]


def attend_kernel(n, moves_hbm, page_hbm, length_hbm, q_hbm, kv_hbm, pool, recv, local, back, *refs):
    (
        moves, page_table, lengths, cache, owner, limit, vacant,
        q, kv, out, buf, qbd, fk, scores, part_max, top, part_sum, acc, small_sems, sems, out_sem,
    ) = refs
    rows_inst, heads, hd = q.shape
    fresh_rows = kv.shape[1]
    slots, _, block, columns = pool.shape
    groups = columns // hd
    steps = fresh_rows // (2 * groups)
    per = heads // groups
    pages = page_table.shape[1]
    me = lax.axis_index("inst")
    scale = 1.0 / math.sqrt(hd)

    small = [
        pltpu.make_async_copy(src, dst, small_sems.at[i])
        for i, (src, dst) in enumerate(
            [(moves_hbm, moves), (page_hbm, page_table), (length_hbm, lengths), (q_hbm, q), (kv_hbm, kv)]
        )
    ]
    for c in small:
        c.start()

    def fetch(p, plane):
        return pltpu.make_async_copy(pool.at[p, plane], buf.at[p, plane], sems.at[p, plane])

    for plane in range(2):
        for p in range(slots):
            fetch(p, plane).start()
    for c in small:
        c.wait()

    find_moves(moves, rows_inst, n, me, None, cache)
    for p in range(slots + 1):
        owner[p] = rows_inst
        limit[p] = 0
    for r in range(rows_inst):
        length = lengths[r]
        vacant[r] = 0
        for b in range(pages):
            at = jnp.where(b * block < length, page_table[r, b], slots)
            owner[at] = r
            limit[at] = length - b * block

    zero = jnp.zeros((per, hd), jnp.bfloat16)

    def set_row(r, rows, fresh):
        for g in range(groups):
            for k in range(groups):
                qbd[r, g * per : (g + 1) * per, k * hd : (k + 1) * hd] = (
                    rows[g * per : (g + 1) * per] if k == g else zero
                )
        fk[r] = fresh.astype(jnp.float32)

    for r in range(rows_inst):
        set_row(r, q[r], kv[r])
    set_row(rows_inst, q[0], kv[0])
    for d in range(n):

        @pl.when(cache[d] >= 0)
        def _():
            slot = cache[d]
            set_row(slot, recv[d, 0:heads, :], recv[d, heads:, :])
            vacant[slot] = 1

    step_of = lax.broadcasted_iota(jnp.int32, (per, 1), 0) % steps
    fresh_scores = []
    for r in range(rows_inst):
        row_scores = []
        for g in range(groups):
            qg = qbd[r, g * per : (g + 1) * per, g * hd : (g + 1) * hd].astype(jnp.float32)
            line = []
            for u in range(steps):
                key = fk[r, pl.ds((u * groups + g) * 2, 1), :]
                s = jnp.sum(qg * key, axis=1, keepdims=True)
                line.append(jnp.where(step_of >= u, s, NEG))
            row_scores.append(line)
        fresh_scores.append(row_scores)
        first = jnp.concatenate(
            [functools.reduce(jnp.maximum, row_scores[g]) for g in range(groups)], axis=0
        )
        part_max[r] = jnp.broadcast_to(first, (heads, hd))
    part_max[rows_inst] = jnp.zeros((heads, hd), jnp.float32)

    lane = lax.broadcasted_iota(jnp.int32, (heads, block), 1)
    for p in range(slots):
        fetch(p, 0).wait()
        r = owner[p]
        s = lax.dot_general(
            qbd[r], buf[p, 0], (((1,), (1,)), ((), ())), preferred_element_type=jnp.float32
        )
        s = jnp.where(lane < limit[p], s, NEG)
        scores[p] = s
        m = part_max[r]
        for c in range(block // hd):
            m = jnp.maximum(m, s[:, c * hd : (c + 1) * hd])
        part_max[r] = m

    factor = scale * math.log2(math.e)
    for r in range(rows_inst):
        m = jnp.max(part_max[r], axis=1, keepdims=True)
        top[r] = jnp.broadcast_to(m, (heads, hd))
        for g in range(groups):
            mg = m[g * per : (g + 1) * per]
            total = jnp.zeros((per, 1), jnp.float32)
            value = jnp.zeros((per, hd), jnp.float32)
            for u in range(steps):
                e = jnp.exp2((fresh_scores[r][g][u] - mg) * factor)
                total = total + e
                weight = e.astype(jnp.bfloat16).astype(jnp.float32)
                value = value + weight * fk[r, pl.ds((u * groups + g) * 2 + 1, 1), :]
            acc[r, g * per : (g + 1) * per, :] = value
            first_lane = lax.broadcasted_iota(jnp.int32, (per, hd), 1) == 0
            part_sum[r, g * per : (g + 1) * per, :] = jnp.where(first_lane, total, 0.0)
    top[rows_inst] = jnp.zeros((heads, hd), jnp.float32)
    part_sum[rows_inst] = jnp.zeros((heads, hd), jnp.float32)
    acc[rows_inst] = jnp.zeros((heads, hd), jnp.float32)

    for p in range(slots):
        fetch(p, 1).wait()
        r = owner[p]
        m = top[r]
        pieces = []
        total = part_sum[r]
        for c in range(block // hd):
            e = jnp.exp2((scores[p, :, c * hd : (c + 1) * hd] - m) * factor)
            total = total + e
            pieces.append(e.astype(jnp.bfloat16))
        part_sum[r] = total
        weights = jnp.concatenate(pieces, axis=1)
        o = lax.dot_general(
            weights, buf[p, 1], (((1,), (0,)), ((), ())), preferred_element_type=jnp.float32
        )
        acc[r] = acc[r] + jnp.concatenate(
            [o[g * per : (g + 1) * per, g * hd : (g + 1) * hd] for g in range(groups)], axis=0
        )

    for r in range(rows_inst):
        total = jnp.sum(part_sum[r], axis=1, keepdims=True)
        value = acc[r] / total
        acc[r] = value
        out[r] = jnp.where(vacant[r] == 1, 0.0, value).astype(jnp.bfloat16)
    write = pltpu.make_async_copy(out, local, out_sem)
    write.start()
    for d in range(n):
        back[d] = acc[jnp.maximum(cache[d], 0)].astype(jnp.bfloat16)
    write.wait()


def place_kernel(n, hidden, local, back, out, sems):
    def put(d):
        return pltpu.make_async_copy(back.at[d], out.at[jnp.maximum(hidden[d], 0)], sems.at[d])

    for d in range(n):

        @pl.when(hidden[d] >= 0)
        def _():
            put(d).start()

    for d in range(n):

        @pl.when(hidden[d] >= 0)
        def _():
            put(d).wait()


def body(kv_pool, page_table, lengths, queries, new_kv, moves):
    n = lax.axis_size("inst")
    rows_inst, steps, width = queries.shape
    columns = kv_pool.shape[3]
    slots, _, block, _ = kv_pool.shape
    groups = columns // HD
    heads_all = width // HD
    heads = steps * heads_all
    fresh_rows = steps * groups * 2
    pages = page_table.shape[1]
    bf16 = jnp.bfloat16
    f32 = jnp.float32
    i32 = jnp.int32
    q = queries.reshape(rows_inst, steps, heads_all, HD).transpose(0, 2, 1, 3).reshape(rows_inst, heads, HD)
    kv = (
        new_kv.reshape(rows_inst, steps, 2, groups, HD)
        .transpose(0, 1, 3, 2, 4)
        .reshape(rows_inst, fresh_rows, HD)
    )
    in_hbm = lambda x: pltpu.with_memory_space_constraint(x, HBM)
    q, kv, kv_pool, page_table, lengths = map(in_hbm, (q, kv, kv_pool, page_table, lengths))
    move_cols = in_hbm(moves.T)
    smem = pl.BlockSpec(memory_space=SMEM)
    vmem = pl.BlockSpec(memory_space=VMEM)
    hbm = pl.BlockSpec(memory_space=HBM)

    packed, hidden = pl.pallas_call(
        functools.partial(pack_kernel, n),
        out_shape=[
            jax.ShapeDtypeStruct((n, heads + fresh_rows, HD), bf16),
            SMEM((n + 1,), i32),
        ],
        in_specs=[hbm, hbm, hbm],
        out_specs=[vmem, smem],
        scratch_shapes=[
            SMEM(move_cols.shape, i32),
            VMEM(q.shape, bf16),
            VMEM(kv.shape, bf16),
            pltpu.SemaphoreType.DMA((3,)),
        ],
        name="pack",
    )(move_cols, q, kv)
    received = lax.all_to_all(packed, "inst", 0, 0)
    local, back = pl.pallas_call(
        functools.partial(attend_kernel, n),
        out_shape=[
            jax.ShapeDtypeStruct((rows_inst, heads, HD), bf16),
            jax.ShapeDtypeStruct((n, heads, HD), bf16),
        ],
        in_specs=[hbm] * 6 + [vmem],
        out_specs=[hbm, vmem],
        scratch_shapes=[
            SMEM(move_cols.shape, i32),
            SMEM(page_table.shape, i32),
            SMEM(lengths.shape, i32),
            SMEM((n + 1,), i32),
            SMEM((slots + 1,), i32),
            SMEM((slots + 1,), i32),
            SMEM((rows_inst,), i32),
            VMEM(q.shape, bf16),
            VMEM(kv.shape, bf16),
            VMEM((rows_inst, heads, HD), bf16),
            VMEM((slots, 2, block, columns), bf16),
            VMEM((rows_inst + 1, heads, columns), bf16),
            VMEM((rows_inst + 1, fresh_rows, HD), f32),
            VMEM((slots, heads, block), f32),
            VMEM((rows_inst + 1, heads, HD), f32),
            VMEM((rows_inst + 1, heads, HD), f32),
            VMEM((rows_inst + 1, heads, HD), f32),
            VMEM((rows_inst + 1, heads, HD), f32),
            pltpu.SemaphoreType.DMA((5,)),
            pltpu.SemaphoreType.DMA((slots, 2)),
            pltpu.SemaphoreType.DMA,
        ],
        compiler_params=pltpu.CompilerParams(vmem_limit_bytes=24 * 1024 * 1024),
        name="attend",
    )(move_cols, page_table, lengths, q, kv, kv_pool, received)
    returned = lax.all_to_all(back, "inst", 0, 0)
    out = pl.pallas_call(
        functools.partial(place_kernel, n),
        out_shape=jax.ShapeDtypeStruct((rows_inst, heads, HD), bf16),
        in_specs=[smem, hbm, vmem],
        out_specs=hbm,
        scratch_shapes=[pltpu.SemaphoreType.DMA((n,))],
        input_output_aliases={1: 0},
        name="place",
    )(hidden, local, returned)
    return out.reshape(rows_inst, heads_all, steps, HD).transpose(0, 2, 1, 3).reshape(rows_inst, steps, width)


def solution(mesh):
    placed = (
        P(("groups", "inst"), None, None, "tp"),
        P(("groups", "inst"), None),
        P(("groups", "inst")),
        P(("groups", "inst"), None, "tp"),
        P(("groups", "inst"), None, None, "tp"),
        P("groups", None),
    )
    return jax.shard_map(
        body,
        mesh=mesh,
        in_specs=placed,
        out_specs=P(("groups", "inst"), None, "tp"),
        check_vma=False,
    )
```

```python
import functools
import math

import jax
import jax.numpy as jnp
from jax import lax
from jax.experimental import pallas as pl
from jax.experimental.pallas import tpu as pltpu
from jax.sharding import PartitionSpec as P

HD = 128
NEG = -1e30
SMEM = pltpu.SMEM
VMEM = pltpu.VMEM
HBM = pltpu.HBM


def partner(n):
    if n & (n - 1) == 0:
        swap = lambda d: [(i, i ^ d) for i in range(n)]
        return (lambda a, b: a ^ b), swap, swap
    return (
        (lambda a, b: lax.rem(a - b + n, n)),
        lambda d: [(i, (i + d) % n) for i in range(n)],
        lambda d: [(i, (i - d) % n) for i in range(n)],
    )


def pack_kernel(n, moves_hbm, q_hbm, kv_hbm, *refs):
    outs = refs[: n - 1]
    hidden, cache, moves, q, kv, sems = refs[n - 1 :]
    copies = [
        pltpu.make_async_copy(moves_hbm, moves, sems.at[0]),
        pltpu.make_async_copy(q_hbm, q, sems.at[1]),
        pltpu.make_async_copy(kv_hbm, kv, sems.at[2]),
    ]
    for c in copies:
        c.start()
    rows_inst, heads, _ = q.shape
    me = lax.axis_index("inst")
    index_of = partner(n)[0]
    for d in range(n):
        hidden[d] = -1
        cache[d] = -1
    copies[0].wait()

    def step(m, carry):
        cache_slot = moves[0, m]
        hidden_slot = moves[1, m]
        from_inst = cache_slot // rows_inst
        to_inst = hidden_slot // rows_inst
        index = index_of(from_inst, to_inst)
        hidden[jnp.where(to_inst == me, index, 0)] = lax.rem(hidden_slot, rows_inst)
        cache[jnp.where(from_inst == me, index, 0)] = lax.rem(cache_slot, rows_inst)
        return carry

    lax.fori_loop(0, moves.shape[1], step, 0, unroll=moves.shape[1] <= 8)
    copies[1].wait()
    copies[2].wait()
    for d in range(1, n):
        slot = jnp.maximum(hidden[d], 0)
        outs[d - 1][0:heads, :] = q[slot]
        outs[d - 1][heads:, :] = kv[slot]


def attend_kernel(n, chunk, cache, page_hbm, length_hbm, q_hbm, kv_hbm, pool, *refs):
    recv, local, back = refs[: n - 1], refs[n - 1], refs[n : 2 * n - 1]
    (
        page_table, lengths, owner, limit, vacant,
        q, kv, out, buf, qbd, fk, scores, part_max, top, part_sum, acc, small_sems, sems, out_sem,
    ) = refs[2 * n - 1 :]
    rows_inst, heads, hd = q.shape
    fresh_rows = kv.shape[1]
    slots, _, block, columns = pool.shape
    groups = columns // hd
    steps = fresh_rows // (2 * groups)
    per = heads // groups
    pages = page_table.shape[1]
    scale = 1.0 / math.sqrt(hd)

    small = [
        pltpu.make_async_copy(src, dst, small_sems.at[i])
        for i, (src, dst) in enumerate(
            [(page_hbm, page_table), (length_hbm, lengths), (q_hbm, q), (kv_hbm, kv)]
        )
    ]
    for c in small:
        c.start()

    def fetch(k, plane):
        part = pl.ds(k * chunk, chunk)
        return pltpu.make_async_copy(pool.at[part, plane], buf.at[part, plane], sems.at[k, plane])

    def arrived(p, plane):
        if p % (slots // 2) == 0:
            for k in range(p // chunk, (p + slots // 2) // chunk):
                fetch(k, plane).wait()

    for plane in range(2):
        for k in range(slots // chunk):
            fetch(k, plane).start()
    for c in small:
        c.wait()

    for p in range(slots + 1):
        owner[p] = rows_inst
        limit[p] = 0
    for r in range(rows_inst):
        length = lengths[r]
        vacant[r] = 0
        for b in range(pages):
            at = jnp.where(b * block < length, page_table[r, b], slots)
            owner[at] = r
            limit[at] = length - b * block

    zero = jnp.zeros((per, hd), jnp.bfloat16)

    def set_row(r, rows, fresh):
        for g in range(groups):
            for k in range(groups):
                qbd[r, g * per : (g + 1) * per, k * hd : (k + 1) * hd] = (
                    rows[g * per : (g + 1) * per] if k == g else zero
                )
        fk[r] = fresh.astype(jnp.float32)

    for r in range(rows_inst):
        set_row(r, q[r], kv[r])
    set_row(rows_inst, q[0], kv[0])
    for d in range(1, n):

        @pl.when(cache[d] >= 0)
        def _():
            slot = cache[d]
            set_row(slot, recv[d - 1][0:heads, :], recv[d - 1][heads:, :])
            vacant[slot] = 1

    step_of = lax.broadcasted_iota(jnp.int32, (per, 1), 0) % steps
    fresh_scores = []
    for r in range(rows_inst):
        row_scores = []
        for g in range(groups):
            qg = qbd[r, g * per : (g + 1) * per, g * hd : (g + 1) * hd].astype(jnp.float32)
            line = []
            for u in range(steps):
                key = fk[r, pl.ds((u * groups + g) * 2, 1), :]
                s = jnp.sum(qg * key, axis=1, keepdims=True)
                line.append(jnp.where(step_of >= u, s, NEG))
            row_scores.append(line)
        fresh_scores.append(row_scores)
        first = jnp.concatenate(
            [functools.reduce(jnp.maximum, row_scores[g]) for g in range(groups)], axis=0
        )
        part_max[r] = jnp.broadcast_to(first, (heads, hd))
    part_max[rows_inst] = jnp.zeros((heads, hd), jnp.float32)

    lane = lax.broadcasted_iota(jnp.int32, (heads, block), 1)
    for p in range(slots):
        arrived(p, 0)
        r = owner[p]
        s = lax.dot_general(
            qbd[r], buf[p, 0], (((1,), (1,)), ((), ())), preferred_element_type=jnp.float32
        )
        s = jnp.where(lane < limit[p], s, NEG)
        scores[p] = s
        m = part_max[r]
        for c in range(block // hd):
            m = jnp.maximum(m, s[:, c * hd : (c + 1) * hd])
        part_max[r] = m

    factor = scale * math.log2(math.e)
    for r in range(rows_inst):
        m = jnp.max(part_max[r], axis=1, keepdims=True)
        top[r] = jnp.broadcast_to(m, (heads, hd))
        for g in range(groups):
            mg = m[g * per : (g + 1) * per]
            total = jnp.zeros((per, 1), jnp.float32)
            value = jnp.zeros((per, hd), jnp.float32)
            for u in range(steps):
                e = jnp.exp2((fresh_scores[r][g][u] - mg) * factor)
                total = total + e
                weight = e.astype(jnp.bfloat16).astype(jnp.float32)
                value = value + weight * fk[r, pl.ds((u * groups + g) * 2 + 1, 1), :]
            acc[r, g * per : (g + 1) * per, :] = value
            first_lane = lax.broadcasted_iota(jnp.int32, (per, hd), 1) == 0
            part_sum[r, g * per : (g + 1) * per, :] = jnp.where(first_lane, total, 0.0)
    top[rows_inst] = jnp.zeros((heads, hd), jnp.float32)
    part_sum[rows_inst] = jnp.zeros((heads, hd), jnp.float32)
    acc[rows_inst] = jnp.zeros((heads, hd), jnp.float32)

    for p in range(slots):
        arrived(p, 1)
        r = owner[p]
        m = top[r]
        pieces = []
        total = part_sum[r]
        for c in range(block // hd):
            e = jnp.exp2((scores[p, :, c * hd : (c + 1) * hd] - m) * factor)
            total = total + e
            pieces.append(e.astype(jnp.bfloat16))
        part_sum[r] = total
        weights = jnp.concatenate(pieces, axis=1)
        o = lax.dot_general(
            weights, buf[p, 1], (((1,), (0,)), ((), ())), preferred_element_type=jnp.float32
        )
        acc[r] = acc[r] + jnp.concatenate(
            [o[g * per : (g + 1) * per, g * hd : (g + 1) * hd] for g in range(groups)], axis=0
        )

    for r in range(rows_inst):
        total = jnp.sum(part_sum[r], axis=1, keepdims=True)
        value = acc[r] / total
        acc[r] = value
        out[r] = jnp.where(vacant[r] == 1, 0.0, value).astype(jnp.bfloat16)
    write = pltpu.make_async_copy(out, local, out_sem)
    write.start()
    for d in range(1, n):
        back[d - 1][...] = acc[jnp.maximum(cache[d], 0)].astype(jnp.bfloat16)
    write.wait()


def place_kernel(n, hidden, local, *refs):
    back, out, sems = refs[: n - 1], refs[n - 1], refs[n]

    def put(d):
        return pltpu.make_async_copy(back[d - 1], out.at[jnp.maximum(hidden[d], 0)], sems.at[d])

    for d in range(1, n):

        @pl.when(hidden[d] >= 0)
        def _():
            put(d).start()

    for d in range(1, n):

        @pl.when(hidden[d] >= 0)
        def _():
            put(d).wait()


def body(kv_pool, page_table, lengths, queries, new_kv, moves):
    n = lax.axis_size("inst")
    rows_inst, steps, width = queries.shape
    columns = kv_pool.shape[3]
    slots, _, block, _ = kv_pool.shape
    groups = columns // HD
    heads_all = width // HD
    heads = steps * heads_all
    fresh_rows = steps * groups * 2
    pages = page_table.shape[1]
    bf16 = jnp.bfloat16
    f32 = jnp.float32
    i32 = jnp.int32
    q = queries.reshape(rows_inst, steps, heads_all, HD).transpose(0, 2, 1, 3).reshape(rows_inst, heads, HD)
    kv = (
        new_kv.reshape(rows_inst, steps, 2, groups, HD)
        .transpose(0, 1, 3, 2, 4)
        .reshape(rows_inst, fresh_rows, HD)
    )
    in_hbm = lambda x: pltpu.with_memory_space_constraint(x, HBM)
    q, kv, kv_pool, page_table, lengths = map(in_hbm, (q, kv, kv_pool, page_table, lengths))
    move_cols = in_hbm(moves.T)
    smem = pl.BlockSpec(memory_space=SMEM)
    vmem = pl.BlockSpec(memory_space=VMEM)
    hbm = pl.BlockSpec(memory_space=HBM)

    _, forward, backward = partner(n)
    chunk = math.gcd(slots, 4)

    *packed, hidden, cache = pl.pallas_call(
        functools.partial(pack_kernel, n),
        out_shape=[jax.ShapeDtypeStruct((heads + fresh_rows, HD), bf16)] * (n - 1)
        + [SMEM((n,), i32), SMEM((n,), i32)],
        in_specs=[hbm, hbm, hbm],
        out_specs=[vmem] * (n - 1) + [smem, smem],
        scratch_shapes=[
            SMEM(move_cols.shape, i32),
            VMEM(q.shape, bf16),
            VMEM(kv.shape, bf16),
            pltpu.SemaphoreType.DMA((3,)),
        ],
        name="pack",
    )(move_cols, q, kv)
    received = [lax.ppermute(x, "inst", forward(d + 1)) for d, x in enumerate(packed)]
    local, *back = pl.pallas_call(
        functools.partial(attend_kernel, n, chunk),
        out_shape=[jax.ShapeDtypeStruct((rows_inst, heads, HD), bf16)]
        + [jax.ShapeDtypeStruct((heads, HD), bf16)] * (n - 1),
        in_specs=[smem] + [hbm] * 5 + [vmem] * (n - 1),
        out_specs=[hbm] + [vmem] * (n - 1),
        scratch_shapes=[
            SMEM(page_table.shape, i32),
            SMEM(lengths.shape, i32),
            SMEM((slots + 1,), i32),
            SMEM((slots + 1,), i32),
            SMEM((rows_inst,), i32),
            VMEM(q.shape, bf16),
            VMEM(kv.shape, bf16),
            VMEM((rows_inst, heads, HD), bf16),
            VMEM((slots, 2, block, columns), bf16),
            VMEM((rows_inst + 1, heads, columns), bf16),
            VMEM((rows_inst + 1, fresh_rows, HD), f32),
            VMEM((slots, heads, block), f32),
            VMEM((rows_inst + 1, heads, HD), f32),
            VMEM((rows_inst + 1, heads, HD), f32),
            VMEM((rows_inst + 1, heads, HD), f32),
            VMEM((rows_inst + 1, heads, HD), f32),
            pltpu.SemaphoreType.DMA((4,)),
            pltpu.SemaphoreType.DMA((slots // chunk, 2)),
            pltpu.SemaphoreType.DMA,
        ],
        compiler_params=pltpu.CompilerParams(vmem_limit_bytes=24 * 1024 * 1024),
        name="attend",
    )(cache, page_table, lengths, q, kv, kv_pool, *received)
    returned = [lax.ppermute(x, "inst", backward(d + 1)) for d, x in enumerate(back)]
    out = pl.pallas_call(
        functools.partial(place_kernel, n),
        out_shape=jax.ShapeDtypeStruct((rows_inst, heads, HD), bf16),
        in_specs=[smem, hbm] + [vmem] * (n - 1),
        out_specs=hbm,
        scratch_shapes=[pltpu.SemaphoreType.DMA((n,))],
        input_output_aliases={1: 0},
        name="place",
    )(hidden, local, *returned)
    return out.reshape(rows_inst, heads_all, steps, HD).transpose(0, 2, 1, 3).reshape(rows_inst, steps, width)


def solution(mesh):
    placed = (
        P(("groups", "inst"), None, None, "tp"),
        P(("groups", "inst"), None),
        P(("groups", "inst")),
        P(("groups", "inst"), None, "tp"),
        P(("groups", "inst"), None, None, "tp"),
        P("groups", None),
    )
    return jax.shard_map(
        body,
        mesh=mesh,
        in_specs=placed,
        out_specs=P(("groups", "inst"), None, "tp"),
        check_vma=False,
    )
```

```python
import functools
import itertools
import math

import jax
import jax.numpy as jnp
from jax import lax
from jax.experimental import pallas as pl
from jax.experimental.pallas import tpu as pltpu
from jax.sharding import PartitionSpec as P

HD = 128
CAP = 2
NEG = -1e30
MAX_HALVES = 6
SMEM = pltpu.SMEM
VMEM = pltpu.VMEM
HBM = pltpu.HBM


class Links:
    def __init__(self, n):
        self.n = n
        half = n // 2
        self.halves = []
        if n % 2 == 0 and math.comb(n, half) <= MAX_HALVES:
            self.halves = list(itertools.combinations(range(n), half))
        self.split = bool(self.halves)
        self.count = half if self.split else n - 1

    def index(self, busy, a, b):
        n = self.n
        if self.split:
            half = n // 2
            rank_a = sum(jnp.where(k < a, busy[k], 0) for k in range(n))
            rank_b = sum(jnp.where(k < b, 1 - busy[k], 0) for k in range(n))
            return lax.rem(rank_a - rank_b + half, half)
        if n & (n - 1) == 0:
            return (a ^ b) - 1
        return lax.rem(a - b + n, n) - 1

    def branch(self, busy):
        mask = sum(busy[k] << k for k in range(self.n))
        return sum(
            jnp.where(mask == sum(1 << i for i in half), k, 0) for k, half in enumerate(self.halves)
        )

    def forward(self, which, j):
        n = self.n
        if self.split:
            busy = self.halves[which]
            spare = [i for i in range(n) if i not in busy]
            return [(s, busy[(k + j) % len(busy)]) for k, s in enumerate(spare)]
        if n & (n - 1) == 0:
            return [(i, i ^ (j + 1)) for i in range(n)]
        return [(i, (i + j + 1) % n) for i in range(n)]

    def backward(self, which, j):
        return [(b, a) for a, b in self.forward(which, j)]


def find_moves(links, moves, rows_inst, me, hidden=None, rank=None, slot=None):
    n = links.n
    count = links.count
    for j in range(count + 1):
        if hidden is not None:
            hidden[j] = -1
        if rank is not None:
            rank[j] = CAP
    if slot is not None:
        for c in range(CAP + 1):
            slot[c] = -1
    total = moves.shape[1]
    busy = None
    if links.split:
        froms = [moves[0, m] // rows_inst for m in range(total)]
        busy = [
            functools.reduce(jnp.bitwise_or, [(f == k).astype(jnp.int32) for f in froms]) for k in range(n)
        ]

    def step(m, seen):
        cache_slot = moves[0, m]
        hidden_slot = moves[1, m]
        from_inst = cache_slot // rows_inst
        to_inst = hidden_slot // rows_inst
        index = links.index(busy, from_inst, to_inst)
        if hidden is not None:
            hidden[jnp.where(to_inst == me, index, count)] = lax.rem(hidden_slot, rows_inst)
        mine = from_inst == me
        if rank is not None:
            rank[jnp.where(mine, index, count)] = seen
        if slot is not None:
            slot[jnp.where(mine, seen, CAP)] = lax.rem(cache_slot, rows_inst)
        return jnp.where(mine, seen + 1, seen)

    if links.split:
        seen = jnp.int32(0)
        for m in range(total):
            seen = step(m, seen)
    else:
        lax.fori_loop(0, total, step, jnp.int32(0))
    return busy


def pack_kernel(links, moves_hbm, q_hbm, kv_hbm, *refs):
    outs = refs[: links.count]
    branch, hidden, moves, q, kv, sems = refs[links.count :]
    copies = [
        pltpu.make_async_copy(moves_hbm, moves, sems.at[0]),
        pltpu.make_async_copy(q_hbm, q, sems.at[1]),
        pltpu.make_async_copy(kv_hbm, kv, sems.at[2]),
    ]
    for c in copies:
        c.start()
    rows_inst, heads, _ = q.shape
    me = lax.axis_index("inst")
    copies[0].wait()
    busy = find_moves(links, moves, rows_inst, me, hidden=hidden)
    branch[0] = links.branch(busy) if links.split else 0
    copies[1].wait()
    copies[2].wait()
    for j, out in enumerate(outs):
        row = jnp.maximum(hidden[j], 0)
        out[0:heads, :] = q[row]
        out[heads:, :] = kv[row]


def set_row(at, rows, fresh, qbd, fk, groups):
    per = rows.shape[0] // groups
    hd = rows.shape[1]
    zero = jnp.zeros((per, hd), jnp.bfloat16)
    for g in range(groups):
        for k in range(groups):
            qbd[at, g * per : (g + 1) * per, k * hd : (k + 1) * hd] = (
                rows[g * per : (g + 1) * per] if k == g else zero
            )
    fk[at] = fresh.astype(jnp.float32)


def attend_list(rows, chunk, steps, lists, count, wait, buf, qbd, fk, scores, part_max, top, part_sum, acc):
    page, owner, limit = lists
    _, heads, columns = qbd.shape
    hd = acc.shape[2]
    groups = columns // hd
    per = heads // groups
    block = buf.shape[2]
    factor = math.log2(math.e) / math.sqrt(hd)
    loops = lax.div(count + (chunk - 1), jnp.int32(chunk))

    step_of = lax.broadcasted_iota(jnp.int32, (per, 1), 0) % steps
    fresh_scores = []
    for r in range(rows):
        row_scores = []
        for g in range(groups):
            qg = qbd[r, g * per : (g + 1) * per, g * hd : (g + 1) * hd].astype(jnp.float32)
            line = []
            for u in range(steps):
                key = fk[r, pl.ds((u * groups + g) * 2, 1), :]
                s = jnp.sum(qg * key, axis=1, keepdims=True)
                line.append(jnp.where(step_of >= u, s, NEG))
            row_scores.append(line)
        fresh_scores.append(row_scores)
        first = jnp.concatenate(
            [functools.reduce(jnp.maximum, row_scores[g]) for g in range(groups)], axis=0
        )
        part_max[r] = jnp.broadcast_to(first, (heads, hd))
    part_max[rows] = jnp.zeros((heads, hd), jnp.float32)

    lane = lax.broadcasted_iota(jnp.int32, (heads, block), 1)
    wait(0)

    def first_pass(i, carry):
        for j in range(chunk):
            k = i * chunk + j
            r = owner[k]
            s = lax.dot_general(
                qbd[r], buf[page[k], 0], (((1,), (1,)), ((), ())), preferred_element_type=jnp.float32
            )
            s = jnp.where(lane < limit[k], s, NEG)
            scores[k] = s
            m = s[:, 0:hd]
            for c in range(1, block // hd):
                m = jnp.maximum(m, s[:, c * hd : (c + 1) * hd])
            part_max[r] = jnp.maximum(part_max[r], m)
        return carry

    lax.fori_loop(0, loops, first_pass, 0)

    first_lane = lax.broadcasted_iota(jnp.int32, (per, hd), 1) == 0
    for r in range(rows):
        m = jnp.max(part_max[r], axis=1, keepdims=True)
        top[r] = jnp.broadcast_to(m, (heads, hd))
        for g in range(groups):
            mg = m[g * per : (g + 1) * per]
            total = jnp.zeros((per, 1), jnp.float32)
            value = jnp.zeros((per, hd), jnp.float32)
            for u in range(steps):
                e = jnp.exp2((fresh_scores[r][g][u] - mg) * factor)
                total = total + e
                weight = e.astype(jnp.bfloat16).astype(jnp.float32)
                value = value + weight * fk[r, pl.ds((u * groups + g) * 2 + 1, 1), :]
            acc[r, g * per : (g + 1) * per, :] = value
            part_sum[r, g * per : (g + 1) * per, :] = jnp.where(first_lane, total, 0.0)
    top[rows] = jnp.zeros((heads, hd), jnp.float32)
    part_sum[rows] = jnp.zeros((heads, hd), jnp.float32)
    acc[rows] = jnp.zeros((heads, hd), jnp.float32)
    wait(1)

    def second_pass(i, carry):
        for j in range(chunk):
            k = i * chunk + j
            r = owner[k]
            m = top[r]
            pieces = []
            total = jnp.zeros((heads, hd), jnp.float32)
            for c in range(block // hd):
                e = jnp.exp2((scores[k, :, c * hd : (c + 1) * hd] - m) * factor)
                total = total + e
                pieces.append(e.astype(jnp.bfloat16))
            o = lax.dot_general(
                jnp.concatenate(pieces, axis=1),
                buf[page[k], 1],
                (((1,), (0,)), ((), ())),
                preferred_element_type=jnp.float32,
            )
            part_sum[r] = part_sum[r] + total
            acc[r] = acc[r] + jnp.concatenate(
                [o[g * per : (g + 1) * per, g * hd : (g + 1) * hd] for g in range(groups)], axis=0
            )
        return carry

    lax.fori_loop(0, loops, second_pass, 0)
    for r in range(rows):
        acc[r] = acc[r] / jnp.sum(part_sum[r], axis=1, keepdims=True)


def stay_kernel(links, chunk, fetches, moves_hbm, page_hbm, length_hbm, q_hbm, kv_hbm, pool, *refs):
    (
        local, buf, hidden, rank, far_page, far_owner, far_limit, far_count,
        moves, page_table, lengths, slot, page, owner, limit, q, kv, out, qbd, fk,
        scores, part_max, top, part_sum, acc, small_sems, sems, out_sem,
    ) = refs
    rows_inst, heads, hd = q.shape
    fresh_rows = kv.shape[1]
    slots, _, block, columns = pool.shape
    groups = columns // hd
    steps = fresh_rows // (2 * groups)
    pages = page_table.shape[1]
    me = lax.axis_index("inst")

    small = [
        pltpu.make_async_copy(src, dst, small_sems.at[i])
        for i, (src, dst) in enumerate(
            [(moves_hbm, moves), (page_hbm, page_table), (length_hbm, lengths), (q_hbm, q), (kv_hbm, kv)]
        )
    ]
    for c in small:
        c.start()

    part = slots // fetches

    def fetch(k, plane):
        at = pl.ds(k * part, part)
        return pltpu.make_async_copy(pool.at[at, plane], buf.at[at, plane], sems.at[k, plane])

    for plane in range(2):
        for k in range(fetches):
            fetch(k, plane).start()

    def wait(plane):
        for k in range(fetches):
            fetch(k, plane).wait()

    for c in small:
        c.wait()
    find_moves(links, moves, rows_inst, me, hidden=hidden, rank=rank, slot=slot)

    def row(r, counts):
        near, far = counts
        length = lengths[r]
        which = jnp.int32(CAP)
        for c in range(CAP):
            which = jnp.where(slot[c] == r, c, which)
        moved = which < CAP

        def one(b, counts):
            near, far = counts
            number = page_table[r, b]
            left = length - b * block
            at = jnp.where(moved, slots + chunk, near)
            page[at] = number
            owner[at] = r
            limit[at] = left
            at = jnp.where(moved, far, slots + chunk)
            far_page[at] = number
            far_owner[at] = which
            far_limit[at] = left
            return jnp.where(moved, near, near + 1), jnp.where(moved, far + 1, far)

        return lax.fori_loop(0, lax.div(length + (block - 1), jnp.int32(block)), one, (near, far))

    near, far = lax.fori_loop(0, rows_inst, row, (jnp.int32(0), jnp.int32(0)))
    far_count[0] = far
    for j in range(chunk):
        page[near + j] = 0
        owner[near + j] = rows_inst
        limit[near + j] = 0
        far_page[far + j] = 0
        far_owner[far + j] = CAP
        far_limit[far + j] = 0

    for r in range(rows_inst):
        set_row(r, q[r], kv[r], qbd, fk, groups)
    set_row(rows_inst, q[0], kv[0], qbd, fk, groups)
    attend_list(
        rows_inst, chunk, steps, (page, owner, limit), near, wait,
        buf, qbd, fk, scores, part_max, top, part_sum, acc,
    )
    for r in range(rows_inst):
        vacant = functools.reduce(jnp.logical_or, [slot[c] == r for c in range(CAP)])
        out[r] = jnp.where(vacant, 0.0, acc[r]).astype(jnp.bfloat16)
    write = pltpu.make_async_copy(out, local, out_sem)
    write.start()
    write.wait()


def moved_kernel(links, chunk, rank, far_page, far_owner, far_limit, far_count, buf, *refs):
    recv, back = refs[: links.count], refs[links.count : 2 * links.count]
    qbd, fk, scores, part_max, top, part_sum, acc = refs[2 * links.count :]
    _, heads, columns = qbd.shape
    hd = acc.shape[2]
    groups = columns // hd
    steps = fk.shape[1] // (2 * groups)
    count = far_count[0]

    @pl.when(count > 0)
    def _():
        if links.count > CAP:
            qbd[...] = jnp.zeros(qbd.shape, qbd.dtype)
            fk[...] = jnp.zeros(fk.shape, fk.dtype)
        else:
            qbd[CAP] = jnp.zeros(qbd.shape[1:], qbd.dtype)
        for j in range(links.count):

            def put(j=j):
                set_row(rank[j], recv[j][0:heads, :], recv[j][heads:, :], qbd, fk, groups)

            pl.when(rank[j] < CAP)(put)
        attend_list(
            CAP, chunk, steps, (far_page, far_owner, far_limit), count, lambda plane: None,
            buf, qbd, fk, scores, part_max, top, part_sum, acc,
        )
        for j in range(links.count):
            back[j][...] = acc[rank[j]].astype(jnp.bfloat16)


def place_kernel(links, hidden, local, *refs):
    back, out, sems = refs[: links.count], refs[links.count], refs[links.count + 1]

    def put(j):
        return pltpu.make_async_copy(back[j], out.at[jnp.maximum(hidden[j], 0)], sems.at[j])

    for j in range(links.count):

        @pl.when(hidden[j] >= 0)
        def _():
            put(j).start()

    for j in range(links.count):

        @pl.when(hidden[j] >= 0)
        def _():
            put(j).wait()


def body(kv_pool, page_table, lengths, queries, new_kv, moves):
    links = Links(lax.axis_size("inst"))
    rows_inst, steps, width = queries.shape
    slots, _, block, columns = kv_pool.shape
    groups = columns // HD
    heads_all = width // HD
    heads = steps * heads_all
    fresh_rows = steps * groups * 2
    bf16 = jnp.bfloat16
    f32 = jnp.float32
    i32 = jnp.int32
    q = queries.reshape(rows_inst, steps, heads_all, HD).transpose(0, 2, 1, 3).reshape(rows_inst, heads, HD)
    kv = (
        new_kv.reshape(rows_inst, steps, 2, groups, HD)
        .transpose(0, 1, 3, 2, 4)
        .reshape(rows_inst, fresh_rows, HD)
    )
    smem = pl.BlockSpec(memory_space=SMEM)
    vmem = pl.BlockSpec(memory_space=VMEM)
    hbm = pl.BlockSpec(memory_space=HBM)
    in_hbm = lambda x: pltpu.with_memory_space_constraint(x, HBM)
    move_cols = moves.T
    count = links.count
    chunk = 4
    fetches = math.gcd(slots, 4)
    mib = 1024 * 1024

    *packed, branch = pl.pallas_call(
        functools.partial(pack_kernel, links),
        out_shape=[jax.ShapeDtypeStruct((heads + fresh_rows, HD), bf16)] * count
        + [jax.ShapeDtypeStruct((1,), i32)],
        in_specs=[hbm, hbm, hbm],
        out_specs=[vmem] * count + [smem],
        scratch_shapes=[
            SMEM((count + 1,), i32),
            SMEM(move_cols.shape, i32),
            VMEM(q.shape, bf16),
            VMEM(kv.shape, bf16),
            pltpu.SemaphoreType.DMA((3,)),
        ],
        compiler_params=pltpu.CompilerParams(vmem_limit_bytes=4 * mib),
        name="pack",
    )(in_hbm(move_cols), in_hbm(q), in_hbm(kv))

    def state(rows):
        return [
            VMEM((rows + 1, heads, columns), bf16),
            VMEM((rows + 1, fresh_rows, HD), f32),
            VMEM((slots + chunk, heads, block), f32),
            VMEM((rows + 1, heads, HD), f32),
            VMEM((rows + 1, heads, HD), f32),
            VMEM((rows + 1, heads, HD), f32),
            VMEM((rows + 1, heads, HD), f32),
        ]

    blocks = SMEM((slots + chunk + 1,), i32)

    def rest(which, kv_pool, page_table, lengths, q, kv, move_cols, *packed):
        received = [lax.ppermute(x, "inst", links.forward(which, j)) for j, x in enumerate(packed)]
        local, buf, hidden, rank, far_page, far_owner, far_limit, far_count = pl.pallas_call(
            functools.partial(stay_kernel, links, chunk, fetches),
            out_shape=[
                jax.ShapeDtypeStruct((rows_inst, heads, HD), bf16),
                VMEM(kv_pool.shape, bf16),
                SMEM((count + 1,), i32),
                SMEM((count + 1,), i32),
                blocks,
                blocks,
                blocks,
                SMEM((1,), i32),
            ],
            in_specs=[hbm] * 6,
            out_specs=[hbm, vmem] + [smem] * 6,
            scratch_shapes=[
                SMEM(move_cols.shape, i32),
                SMEM(page_table.shape, i32),
                SMEM(lengths.shape, i32),
                SMEM((CAP + 1,), i32),
                blocks,
                blocks,
                blocks,
                VMEM(q.shape, bf16),
                VMEM(kv.shape, bf16),
                VMEM((rows_inst, heads, HD), bf16),
            ]
            + state(rows_inst)
            + [
                pltpu.SemaphoreType.DMA((5,)),
                pltpu.SemaphoreType.DMA((fetches, 2)),
                pltpu.SemaphoreType.DMA,
            ],
            compiler_params=pltpu.CompilerParams(vmem_limit_bytes=16 * mib),
            cost_estimate=pl.CostEstimate(flops=2**27, bytes_accessed=2**23, transcendentals=2**18),
            name="stay",
        )(*map(in_hbm, (move_cols, page_table, lengths, q, kv, kv_pool)))
        back = pl.pallas_call(
            functools.partial(moved_kernel, links, chunk),
            out_shape=[jax.ShapeDtypeStruct((heads, HD), bf16)] * count,
            in_specs=[smem] * 5 + [vmem] + [vmem] * count,
            out_specs=[vmem] * count,
            scratch_shapes=state(CAP),
            compiler_params=pltpu.CompilerParams(vmem_limit_bytes=16 * mib),
            name="moved",
        )(rank, far_page, far_owner, far_limit, far_count, buf, *received)
        returned = [lax.ppermute(x, "inst", links.backward(which, j)) for j, x in enumerate(back)]
        anyspace = pl.BlockSpec(memory_space=pl.ANY)
        out = pl.pallas_call(
            functools.partial(place_kernel, links),
            out_shape=jax.ShapeDtypeStruct((rows_inst, heads, HD), bf16),
            in_specs=[smem, hbm] + [anyspace] * count,
            out_specs=hbm,
            scratch_shapes=[pltpu.SemaphoreType.DMA((count,))],
            input_output_aliases={1: 0},
            compiler_params=pltpu.CompilerParams(vmem_limit_bytes=4 * mib),
            name="place",
        )(hidden, local, *returned)
        out = out.reshape(rows_inst, heads_all, steps, HD).transpose(0, 2, 1, 3)
        return out.reshape(rows_inst, steps, width)

    operands = (kv_pool, page_table, lengths, q, kv, move_cols, *packed)
    if links.split:
        return lax.switch(
            branch[0], [functools.partial(rest, k) for k in range(len(links.halves))], *operands
        )
    return rest(0, *operands)


def solution(mesh):
    placed = (
        P(("groups", "inst"), None, None, "tp"),
        P(("groups", "inst"), None),
        P(("groups", "inst")),
        P(("groups", "inst"), None, "tp"),
        P(("groups", "inst"), None, None, "tp"),
        P("groups", None),
    )
    return jax.shard_map(
        body,
        mesh=mesh,
        in_specs=placed,
        out_specs=P(("groups", "inst"), None, "tp"),
        check_vma=False,
    )
```

```python
import functools
import itertools
import math

import jax
import jax.numpy as jnp
from jax import lax
from jax.experimental import pallas as pl
from jax.experimental.pallas import tpu as pltpu
from jax.sharding import PartitionSpec as P

HD = 128
CAP = 2
NEG = -1e30
MAX_HALVES = 6
SMEM = pltpu.SMEM
VMEM = pltpu.VMEM
HBM = pltpu.HBM


class Links:
    def __init__(self, n):
        self.n = n
        half = n // 2
        self.halves = []
        if n % 2 == 0 and math.comb(n, half) <= MAX_HALVES:
            self.halves = list(itertools.combinations(range(n), half))
        self.split = bool(self.halves)
        self.count = half if self.split else n - 1

    def index(self, busy, a, b):
        n = self.n
        if self.split:
            half = n // 2
            rank_a = sum(jnp.where(k < a, busy[k], 0) for k in range(n))
            rank_b = sum(jnp.where(k < b, 1 - busy[k], 0) for k in range(n))
            return lax.rem(rank_a - rank_b + half, half)
        if n & (n - 1) == 0:
            return (a ^ b) - 1
        return lax.rem(a - b + n, n) - 1

    def branch(self, busy):
        mask = sum(busy[k] << k for k in range(self.n))
        return sum(
            jnp.where(mask == sum(1 << i for i in half), k, 0) for k, half in enumerate(self.halves)
        )

    def forward(self, which, j):
        n = self.n
        if self.split:
            busy = self.halves[which]
            spare = [i for i in range(n) if i not in busy]
            return [(s, busy[(k + j) % len(busy)]) for k, s in enumerate(spare)]
        if n & (n - 1) == 0:
            return [(i, i ^ (j + 1)) for i in range(n)]
        return [(i, (i + j + 1) % n) for i in range(n)]

    def backward(self, which, j):
        return [(b, a) for a, b in self.forward(which, j)]

    def both(self, pairs):
        return sorted(set(pairs) | {(b, a) for a, b in pairs}) if self.split else pairs


def find_moves(links, moves, rows_inst, me, hidden=None, rank=None, slot=None):
    n = links.n
    count = links.count
    for j in range(count + 1):
        if hidden is not None:
            hidden[j] = -1
        if rank is not None:
            rank[j] = CAP
    if slot is not None:
        for c in range(CAP + 1):
            slot[c] = -1
    total = moves.shape[1]
    busy = None
    if links.split:
        froms = [moves[0, m] // rows_inst for m in range(total)]
        busy = [
            functools.reduce(jnp.bitwise_or, [(f == k).astype(jnp.int32) for f in froms]) for k in range(n)
        ]

    def step(m, seen):
        cache_slot = moves[0, m]
        hidden_slot = moves[1, m]
        from_inst = cache_slot // rows_inst
        to_inst = hidden_slot // rows_inst
        index = links.index(busy, from_inst, to_inst)
        if hidden is not None:
            hidden[jnp.where(to_inst == me, index, count)] = lax.rem(hidden_slot, rows_inst)
        mine = from_inst == me
        if rank is not None:
            rank[jnp.where(mine, index, count)] = seen
        if slot is not None:
            slot[jnp.where(mine, seen, CAP)] = lax.rem(cache_slot, rows_inst)
        return jnp.where(mine, seen + 1, seen)

    if links.split:
        seen = jnp.int32(0)
        for m in range(total):
            seen = step(m, seen)
    else:
        lax.fori_loop(0, total, step, jnp.int32(0))
    return busy


def pack_kernel(links, moves_hbm, q_hbm, kv_hbm, *refs):
    outs = refs[: links.count]
    branch, hidden, moves, q, kv, sems = refs[links.count :]
    copies = [
        pltpu.make_async_copy(moves_hbm, moves, sems.at[0]),
        pltpu.make_async_copy(q_hbm, q, sems.at[1]),
        pltpu.make_async_copy(kv_hbm, kv, sems.at[2]),
    ]
    for c in copies:
        c.start()
    rows_inst, heads, _ = q.shape
    me = lax.axis_index("inst")
    copies[0].wait()
    busy = find_moves(links, moves, rows_inst, me, hidden=hidden)
    branch[0] = links.branch(busy) if links.split else 0
    copies[1].wait()
    copies[2].wait()
    for j, out in enumerate(outs):
        row = jnp.maximum(hidden[j], 0)
        out[0:heads, :] = q[row]
        out[heads:, :] = kv[row]


def set_row(at, rows, fresh, qbd, fk, groups):
    per = rows.shape[0] // groups
    hd = rows.shape[1]
    zero = jnp.zeros((per, hd), jnp.bfloat16)
    for g in range(groups):
        for k in range(groups):
            qbd[at, g * per : (g + 1) * per, k * hd : (k + 1) * hd] = (
                rows[g * per : (g + 1) * per] if k == g else zero
            )
    fk[at] = fresh.astype(jnp.float32)


def attend_list(rows, chunk, steps, lists, count, wait, buf, qbd, fk, scores, part_max, top, part_sum, acc):
    page, owner, limit = lists
    _, heads, columns = qbd.shape
    hd = acc.shape[2]
    groups = columns // hd
    per = heads // groups
    block = buf.shape[2]
    factor = math.log2(math.e) / math.sqrt(hd)
    loops = lax.div(count + (chunk - 1), jnp.int32(chunk))

    step_of = lax.broadcasted_iota(jnp.int32, (per, 1), 0) % steps
    fresh_scores = []
    for r in range(rows):
        row_scores = []
        for g in range(groups):
            qg = qbd[r, g * per : (g + 1) * per, g * hd : (g + 1) * hd].astype(jnp.float32)
            line = []
            for u in range(steps):
                key = fk[r, pl.ds((u * groups + g) * 2, 1), :]
                s = jnp.sum(qg * key, axis=1, keepdims=True)
                line.append(jnp.where(step_of >= u, s, NEG))
            row_scores.append(line)
        fresh_scores.append(row_scores)
        first = jnp.concatenate(
            [functools.reduce(jnp.maximum, row_scores[g]) for g in range(groups)], axis=0
        )
        part_max[r] = jnp.broadcast_to(first, (heads, hd))
    part_max[rows] = jnp.zeros((heads, hd), jnp.float32)

    lane = lax.broadcasted_iota(jnp.int32, (heads, block), 1)
    wait(0)

    def first_pass(i, carry):
        for j in range(chunk):
            k = i * chunk + j
            r = owner[k]
            s = lax.dot_general(
                qbd[r], buf[page[k], 0], (((1,), (1,)), ((), ())), preferred_element_type=jnp.float32
            )
            s = jnp.where(lane < limit[k], s, NEG)
            scores[k] = s
            m = s[:, 0:hd]
            for c in range(1, block // hd):
                m = jnp.maximum(m, s[:, c * hd : (c + 1) * hd])
            part_max[r] = jnp.maximum(part_max[r], m)
        return carry

    lax.fori_loop(0, loops, first_pass, 0)

    first_lane = lax.broadcasted_iota(jnp.int32, (per, hd), 1) == 0
    for r in range(rows):
        m = jnp.max(part_max[r], axis=1, keepdims=True)
        top[r] = jnp.broadcast_to(m, (heads, hd))
        for g in range(groups):
            mg = m[g * per : (g + 1) * per]
            total = jnp.zeros((per, 1), jnp.float32)
            value = jnp.zeros((per, hd), jnp.float32)
            for u in range(steps):
                e = jnp.exp2((fresh_scores[r][g][u] - mg) * factor)
                total = total + e
                weight = e.astype(jnp.bfloat16).astype(jnp.float32)
                value = value + weight * fk[r, pl.ds((u * groups + g) * 2 + 1, 1), :]
            acc[r, g * per : (g + 1) * per, :] = value
            part_sum[r, g * per : (g + 1) * per, :] = jnp.where(first_lane, total, 0.0)
    top[rows] = jnp.zeros((heads, hd), jnp.float32)
    part_sum[rows] = jnp.zeros((heads, hd), jnp.float32)
    acc[rows] = jnp.zeros((heads, hd), jnp.float32)
    wait(1)

    def second_pass(i, carry):
        for j in range(chunk):
            k = i * chunk + j
            r = owner[k]
            m = top[r]
            pieces = []
            total = jnp.zeros((heads, hd), jnp.float32)
            for c in range(block // hd):
                e = jnp.exp2((scores[k, :, c * hd : (c + 1) * hd] - m) * factor)
                total = total + e
                pieces.append(e.astype(jnp.bfloat16))
            o = lax.dot_general(
                jnp.concatenate(pieces, axis=1),
                buf[page[k], 1],
                (((1,), (0,)), ((), ())),
                preferred_element_type=jnp.float32,
            )
            part_sum[r] = part_sum[r] + total
            acc[r] = acc[r] + jnp.concatenate(
                [o[g * per : (g + 1) * per, g * hd : (g + 1) * hd] for g in range(groups)], axis=0
            )
        return carry

    lax.fori_loop(0, loops, second_pass, 0)
    for r in range(rows):
        acc[r] = acc[r] / jnp.sum(part_sum[r], axis=1, keepdims=True)


def attend_near(rows_inst, chunk, steps, lists, count, slot, wait, buf, qbd, fk, local, out, out_sem, *work):
    attend_list(rows_inst, chunk, steps, lists, count, wait, buf, qbd, fk, *work)
    acc = work[-1]
    for r in range(rows_inst):
        vacant = functools.reduce(jnp.logical_or, [slot[c] == r for c in range(CAP)])
        out[r] = jnp.where(vacant, 0.0, acc[r]).astype(jnp.bfloat16)
    write = pltpu.make_async_copy(out, local, out_sem)
    write.start()
    write.wait()


def stay_kernel(links, chunk, fetches, moves_hbm, page_hbm, length_hbm, q_hbm, kv_hbm, pool, *refs):
    (
        local, buf, qbd, fk, hidden, rank, slot,
        page, owner, limit, counts, far_page, far_owner, far_limit,
        moves, page_table, lengths, q, kv, out,
        scores, part_max, top, part_sum, acc, small_sems, sems, out_sem,
    ) = refs
    rows_inst, heads, hd = q.shape
    fresh_rows = kv.shape[1]
    slots, _, block, columns = pool.shape
    groups = columns // hd
    steps = fresh_rows // (2 * groups)
    me = lax.axis_index("inst")

    small = [
        pltpu.make_async_copy(src, dst, small_sems.at[i])
        for i, (src, dst) in enumerate(
            [(moves_hbm, moves), (page_hbm, page_table), (length_hbm, lengths), (q_hbm, q), (kv_hbm, kv)]
        )
    ]
    for c in small:
        c.start()

    part = slots // fetches

    def fetch(k, plane):
        at = pl.ds(k * part, part)
        return pltpu.make_async_copy(pool.at[at, plane], buf.at[at, plane], sems.at[k, plane])

    for plane in range(2):
        for k in range(fetches):
            fetch(k, plane).start()

    def wait(plane):
        for k in range(fetches):
            fetch(k, plane).wait()

    for c in small:
        c.wait()
    find_moves(links, moves, rows_inst, me, hidden=hidden, rank=rank, slot=slot)

    def row(r, counts):
        near, far = counts
        length = lengths[r]
        which = jnp.int32(CAP)
        for c in range(CAP):
            which = jnp.where(slot[c] == r, c, which)
        moved = which < CAP

        def one(b, counts):
            near, far = counts
            number = page_table[r, b]
            left = length - b * block
            at = jnp.where(moved, slots + chunk, near)
            page[at] = number
            owner[at] = r
            limit[at] = left
            at = jnp.where(moved, far, slots + chunk)
            far_page[at] = number
            far_owner[at] = which
            far_limit[at] = left
            return jnp.where(moved, near, near + 1), jnp.where(moved, far + 1, far)

        return lax.fori_loop(0, lax.div(length + (block - 1), jnp.int32(block)), one, (near, far))

    near, far = lax.fori_loop(0, rows_inst, row, (jnp.int32(0), jnp.int32(0)))
    counts[0] = near
    counts[1] = far
    for j in range(chunk):
        page[near + j] = 0
        owner[near + j] = rows_inst
        limit[near + j] = 0
        far_page[far + j] = 0
        far_owner[far + j] = CAP
        far_limit[far + j] = 0

    for r in range(rows_inst):
        set_row(r, q[r], kv[r], qbd, fk, groups)
    set_row(rows_inst, q[0], kv[0], qbd, fk, groups)

    @pl.when(far == 0)
    def _():
        attend_near(
            rows_inst, chunk, steps, (page, owner, limit), near, slot, wait,
            buf, qbd, fk, local, out, out_sem, scores, part_max, top, part_sum, acc,
        )

    @pl.when(far > 0)
    def _():
        wait(0)
        wait(1)


def late_kernel(chunk, slot, page, owner, limit, counts, buf, qbd, fk, local_in, order, local, *refs):
    out, out_sem, *work = refs
    rows_inst = out.shape[0]
    steps = fk.shape[1] // (2 * (qbd.shape[2] // fk.shape[2]))

    @pl.when(counts[1] > 0)
    def _():
        attend_near(
            rows_inst, chunk, steps, (page, owner, limit), counts[0], slot, lambda plane: None,
            buf, qbd, fk, local, out, out_sem, *work,
        )


def moved_kernel(links, chunk, rank, far_page, far_owner, far_limit, counts, buf, *refs):
    recv, back = refs[: links.count], refs[links.count : 2 * links.count]
    qbd, fk, scores, part_max, top, part_sum, acc = refs[2 * links.count :]
    _, heads, columns = qbd.shape
    hd = acc.shape[2]
    groups = columns // hd
    steps = fk.shape[1] // (2 * groups)
    count = counts[1]

    @pl.when(count > 0)
    def _():
        if links.count > CAP:
            qbd[...] = jnp.zeros(qbd.shape, qbd.dtype)
            fk[...] = jnp.zeros(fk.shape, fk.dtype)
        else:
            qbd[CAP] = jnp.zeros(qbd.shape[1:], qbd.dtype)
        for j in range(links.count):

            def put(j=j):
                set_row(rank[j], recv[j][0:heads, :], recv[j][heads:, :], qbd, fk, groups)

            pl.when(rank[j] < CAP)(put)
        attend_list(
            CAP, chunk, steps, (far_page, far_owner, far_limit), count, lambda plane: None,
            buf, qbd, fk, scores, part_max, top, part_sum, acc,
        )
        for j in range(links.count):
            back[j][...] = acc[rank[j]].astype(jnp.bfloat16)


def place_kernel(links, hidden, local, *refs):
    back, out, sems = refs[: links.count], refs[links.count], refs[links.count + 1]

    def put(j):
        return pltpu.make_async_copy(back[j], out.at[jnp.maximum(hidden[j], 0)], sems.at[j])

    for j in range(links.count):

        @pl.when(hidden[j] >= 0)
        def _():
            put(j).start()

    for j in range(links.count):

        @pl.when(hidden[j] >= 0)
        def _():
            put(j).wait()


def body(kv_pool, page_table, lengths, queries, new_kv, moves):
    links = Links(lax.axis_size("inst"))
    rows_inst, steps, width = queries.shape
    slots, _, block, columns = kv_pool.shape
    groups = columns // HD
    heads_all = width // HD
    heads = steps * heads_all
    fresh_rows = steps * groups * 2
    bf16 = jnp.bfloat16
    f32 = jnp.float32
    i32 = jnp.int32
    q = queries.reshape(rows_inst, steps, heads_all, HD).transpose(0, 2, 1, 3).reshape(rows_inst, heads, HD)
    kv = (
        new_kv.reshape(rows_inst, steps, 2, groups, HD)
        .transpose(0, 1, 3, 2, 4)
        .reshape(rows_inst, fresh_rows, HD)
    )
    smem = pl.BlockSpec(memory_space=SMEM)
    vmem = pl.BlockSpec(memory_space=VMEM)
    hbm = pl.BlockSpec(memory_space=HBM)
    in_hbm = lambda x: pltpu.with_memory_space_constraint(x, HBM)
    move_cols = moves.T
    count = links.count
    chunk = 4
    fetches = math.gcd(slots, 4)
    mib = 1024 * 1024

    *packed, branch = pl.pallas_call(
        functools.partial(pack_kernel, links),
        out_shape=[jax.ShapeDtypeStruct((heads + fresh_rows, HD), bf16)] * count
        + [SMEM((1,), i32)],
        in_specs=[hbm, hbm, hbm],
        out_specs=[vmem] * count + [smem],
        scratch_shapes=[
            SMEM((count + 1,), i32),
            SMEM(move_cols.shape, i32),
            VMEM(q.shape, bf16),
            VMEM(kv.shape, bf16),
            pltpu.SemaphoreType.DMA((3,)),
        ],
        compiler_params=pltpu.CompilerParams(vmem_limit_bytes=4 * mib),
        name="pack",
    )(in_hbm(move_cols), in_hbm(q), in_hbm(kv))

    def rows_state(rows):
        return [VMEM((rows + 1, heads, columns), bf16), VMEM((rows + 1, fresh_rows, HD), f32)]

    def work_state(rows):
        return [VMEM((slots + chunk, heads, block), f32)] + [VMEM((rows + 1, heads, HD), f32)] * 4

    anyspace = pl.BlockSpec(memory_space=pl.ANY)
    blocks = SMEM((slots + chunk + 1,), i32)
    whole = jax.ShapeDtypeStruct((rows_inst, heads, HD), bf16)
    staged = VMEM((rows_inst, heads, HD), bf16)

    def rest(which, kv_pool, page_table, lengths, q, kv, move_cols, *packed):
        received = [
            lax.ppermute(x, "inst", links.both(links.forward(which, j))) for j, x in enumerate(packed)
        ]
        (
            local, buf, qbd, fk, hidden, rank, slot,
            page, owner, limit, counts, far_page, far_owner, far_limit,
        ) = pl.pallas_call(
            functools.partial(stay_kernel, links, chunk, fetches),
            out_shape=[whole, VMEM(kv_pool.shape, bf16)]
            + rows_state(rows_inst)
            + [SMEM((count + 1,), i32), SMEM((count + 1,), i32), SMEM((CAP + 1,), i32)]
            + [blocks, blocks, blocks, SMEM((2,), i32), blocks, blocks, blocks],
            in_specs=[hbm] * 6,
            out_specs=[hbm] + [vmem] * 3 + [smem] * 10,
            scratch_shapes=[
                SMEM(move_cols.shape, i32),
                SMEM(page_table.shape, i32),
                SMEM(lengths.shape, i32),
                VMEM(q.shape, bf16),
                VMEM(kv.shape, bf16),
                staged,
            ]
            + work_state(rows_inst)
            + [
                pltpu.SemaphoreType.DMA((5,)),
                pltpu.SemaphoreType.DMA((fetches, 2)),
                pltpu.SemaphoreType.DMA,
            ],
            compiler_params=pltpu.CompilerParams(vmem_limit_bytes=16 * mib),
            cost_estimate=pl.CostEstimate(flops=2**27, bytes_accessed=2**23, transcendentals=2**18),
            name="stay",
        )(*map(in_hbm, (move_cols, page_table, lengths, q, kv, kv_pool)))
        back = pl.pallas_call(
            functools.partial(moved_kernel, links, chunk),
            out_shape=[jax.ShapeDtypeStruct((heads, HD), bf16)] * count,
            in_specs=[smem] * 5 + [vmem] + [vmem] * count,
            out_specs=[vmem] * count,
            scratch_shapes=rows_state(CAP) + work_state(CAP),
            compiler_params=pltpu.CompilerParams(vmem_limit_bytes=16 * mib),
            name="moved",
        )(rank, far_page, far_owner, far_limit, counts, buf, *received)
        ways = [links.backward(which, j) for j in range(count)]
        ways[-1] = links.both(ways[-1])
        returned = [lax.ppermute(x, "inst", way) for x, way in zip(back, ways)]
        local = pl.pallas_call(
            functools.partial(late_kernel, chunk),
            out_shape=whole,
            in_specs=[smem] * 5 + [vmem] * 3 + [hbm, anyspace],
            out_specs=hbm,
            scratch_shapes=[staged, pltpu.SemaphoreType.DMA] + work_state(rows_inst),
            input_output_aliases={8: 0},
            compiler_params=pltpu.CompilerParams(vmem_limit_bytes=16 * mib),
            cost_estimate=pl.CostEstimate(flops=2**27, bytes_accessed=2**23, transcendentals=2**18),
            name="late",
        )(slot, page, owner, limit, counts, buf, qbd, fk, local, back[0])
        out = pl.pallas_call(
            functools.partial(place_kernel, links),
            out_shape=jax.ShapeDtypeStruct((rows_inst, heads, HD), bf16),
            in_specs=[smem, hbm] + [anyspace] * count,
            out_specs=hbm,
            scratch_shapes=[pltpu.SemaphoreType.DMA((count,))],
            input_output_aliases={1: 0},
            compiler_params=pltpu.CompilerParams(vmem_limit_bytes=4 * mib),
            name="place",
        )(hidden, local, *returned)
        out = out.reshape(rows_inst, heads_all, steps, HD).transpose(0, 2, 1, 3)
        return out.reshape(rows_inst, steps, width)

    operands = (kv_pool, page_table, lengths, q, kv, move_cols, *packed)
    if links.split:
        return lax.switch(
            branch[0], [functools.partial(rest, k) for k in range(len(links.halves))], *operands
        )
    return rest(0, *operands)


def solution(mesh):
    placed = (
        P(("groups", "inst"), None, None, "tp"),
        P(("groups", "inst"), None),
        P(("groups", "inst")),
        P(("groups", "inst"), None, "tp"),
        P(("groups", "inst"), None, None, "tp"),
        P("groups", None),
    )
    return jax.shard_map(
        body,
        mesh=mesh,
        in_specs=placed,
        out_specs=P(("groups", "inst"), None, "tp"),
        check_vma=False,
    )
```

```python
import functools
import itertools
import math

import jax
import jax.numpy as jnp
from jax import lax
from jax.experimental import pallas as pl
from jax.experimental.pallas import tpu as pltpu
from jax.sharding import PartitionSpec as P

HD = 128
CAP = 2
NEG = -1e30
MAX_HALVES = 6
SMEM = pltpu.SMEM
VMEM = pltpu.VMEM
HBM = pltpu.HBM


class Links:
    def __init__(self, n):
        self.n = n
        half = n // 2
        self.halves = []
        if n % 2 == 0 and math.comb(n, half) <= MAX_HALVES:
            self.halves = list(itertools.combinations(range(n), half))
        self.split = bool(self.halves)
        self.count = half if self.split else n - 1

    def index(self, busy, a, b):
        n = self.n
        if self.split:
            half = n // 2
            rank_a = sum(jnp.where(k < a, busy[k], 0) for k in range(n))
            rank_b = sum(jnp.where(k < b, 1 - busy[k], 0) for k in range(n))
            return lax.rem(rank_a - rank_b + half, half)
        if n & (n - 1) == 0:
            return (a ^ b) - 1
        return lax.rem(a - b + n, n) - 1

    def branch(self, busy):
        mask = sum(busy[k] << k for k in range(self.n))
        return sum(
            jnp.where(mask == sum(1 << i for i in half), k, 0) for k, half in enumerate(self.halves)
        )

    def forward(self, which, j):
        n = self.n
        if self.split:
            busy = self.halves[which]
            spare = [i for i in range(n) if i not in busy]
            return [(s, busy[(k + j) % len(busy)]) for k, s in enumerate(spare)]
        if n & (n - 1) == 0:
            return [(i, i ^ (j + 1)) for i in range(n)]
        return [(i, (i + j + 1) % n) for i in range(n)]

    def backward(self, which, j):
        return [(b, a) for a, b in self.forward(which, j)]

    def both(self, pairs):
        return sorted(set(pairs) | {(b, a) for a, b in pairs}) if self.split else pairs


def find_moves(links, moves, rows_inst, me, hidden=None, rank=None, slot=None):
    n = links.n
    count = links.count
    for j in range(count + 1):
        if hidden is not None:
            hidden[j] = -1
        if rank is not None:
            rank[j] = CAP
    if slot is not None:
        for c in range(CAP + 1):
            slot[c] = -1
    total = moves.shape[1]
    busy = None
    if links.split:
        froms = [moves[0, m] // rows_inst for m in range(total)]
        busy = [
            functools.reduce(jnp.bitwise_or, [(f == k).astype(jnp.int32) for f in froms]) for k in range(n)
        ]

    def step(m, seen):
        cache_slot = moves[0, m]
        hidden_slot = moves[1, m]
        from_inst = cache_slot // rows_inst
        to_inst = hidden_slot // rows_inst
        index = links.index(busy, from_inst, to_inst)
        if hidden is not None:
            hidden[jnp.where(to_inst == me, index, count)] = lax.rem(hidden_slot, rows_inst)
        mine = from_inst == me
        if rank is not None:
            rank[jnp.where(mine, index, count)] = seen
        if slot is not None:
            slot[jnp.where(mine, seen, CAP)] = lax.rem(cache_slot, rows_inst)
        return jnp.where(mine, seen + 1, seen)

    if links.split:
        seen = jnp.int32(0)
        for m in range(total):
            seen = step(m, seen)
    else:
        lax.fori_loop(0, total, step, jnp.int32(0))
    return busy


def pack_kernel(links, moves_hbm, q_hbm, kv_hbm, *refs):
    outs = refs[: links.count]
    branch, hidden, moves, q, kv, sems = refs[links.count :]
    copies = [
        pltpu.make_async_copy(moves_hbm, moves, sems.at[0]),
        pltpu.make_async_copy(q_hbm, q, sems.at[1]),
        pltpu.make_async_copy(kv_hbm, kv, sems.at[2]),
    ]
    for c in copies:
        c.start()
    rows_inst, heads, _ = q.shape
    me = lax.axis_index("inst")
    copies[0].wait()
    busy = find_moves(links, moves, rows_inst, me, hidden=hidden)
    branch[0] = links.branch(busy) if links.split else 0
    copies[1].wait()
    copies[2].wait()
    for j, out in enumerate(outs):
        row = jnp.maximum(hidden[j], 0)
        out[0:heads, :] = q[row]
        out[heads:, :] = kv[row]


def set_row(at, rows, fresh, qbd, fk, fv, groups):
    heads, hd = rows.shape
    per = heads // groups
    zero = jnp.zeros((per, hd), jnp.bfloat16)
    for g in range(groups):
        for k in range(groups):
            qbd[at, g * per : (g + 1) * per, k * hd : (k + 1) * hd] = (
                rows[g * per : (g + 1) * per] if k == g else zero
            )
    if fk is None:
        return
    fresh = fresh.astype(jnp.float32)
    token = lax.broadcasted_iota(jnp.int32, (16, hd), 0)
    for plane, ref in enumerate((fk, fv)):
        for g in range(groups):
            block = jnp.zeros((16, hd), jnp.float32)
            for u in range(fresh.shape[0] // (2 * groups)):
                line = (u * groups + g) * 2 + plane
                block = jnp.where(token == u, fresh[line : line + 1], block)
            ref[at, 0:16, g * hd : (g + 1) * hd] = block.astype(jnp.bfloat16)


def attend_list(rows, chunk, steps, lists, count, wait, buf, qbd, fk, fv, scores, new, part_max, top, part_sum, acc):
    page, owner, limit = lists
    _, heads, columns = qbd.shape
    hd = acc.shape[2]
    groups = columns // hd
    per = heads // groups
    block = buf.shape[2]
    factor = math.log2(math.e) / math.sqrt(hd)
    loops = lax.div(count + (chunk - 1), jnp.int32(chunk))

    def diagonal(o):
        return jnp.concatenate(
            [o[g * per : (g + 1) * per, g * hd : (g + 1) * hd] for g in range(groups)], axis=0
        )

    keys_of = (((1,), (1,)), ((), ()))
    values_of = (((1,), (0,)), ((), ()))
    token = lax.broadcasted_iota(jnp.int32, (heads, hd), 1)
    seen = token <= lax.broadcasted_iota(jnp.int32, (heads, hd), 0) % steps
    for r in range(rows):
        s = lax.dot_general(qbd[r], fk[r], keys_of, preferred_element_type=jnp.float32)
        s = jnp.where(seen, s, NEG)
        new[r] = s
        part_max[r] = s
    part_max[rows] = jnp.zeros((heads, hd), jnp.float32)

    lane = lax.broadcasted_iota(jnp.int32, (heads, block), 1)
    wait(0)

    def first_pass(i, carry):
        for j in range(chunk):
            k = i * chunk + j
            r = owner[k]
            s = lax.dot_general(
                qbd[r], buf[page[k], 0], keys_of, preferred_element_type=jnp.float32
            )
            s = jnp.where(lane < limit[k], s, NEG)
            scores[k] = s
            m = s[:, 0:hd]
            for c in range(1, block // hd):
                m = jnp.maximum(m, s[:, c * hd : (c + 1) * hd])
            part_max[r] = jnp.maximum(part_max[r], m)
        return carry

    lax.fori_loop(0, loops, first_pass, 0)

    for r in range(rows):
        m = jnp.broadcast_to(jnp.max(part_max[r], axis=1, keepdims=True), (heads, hd))
        top[r] = m
        e = jnp.exp2((new[r] - m) * factor)
        part_sum[r] = e
        acc[r] = diagonal(
            lax.dot_general(e.astype(jnp.bfloat16), fv[r], values_of, preferred_element_type=jnp.float32)
        )
    top[rows] = jnp.zeros((heads, hd), jnp.float32)
    part_sum[rows] = jnp.zeros((heads, hd), jnp.float32)
    acc[rows] = jnp.zeros((heads, hd), jnp.float32)
    wait(1)

    def second_pass(i, carry):
        for j in range(chunk):
            k = i * chunk + j
            r = owner[k]
            m = top[r]
            pieces = []
            total = jnp.zeros((heads, hd), jnp.float32)
            for c in range(block // hd):
                e = jnp.exp2((scores[k, :, c * hd : (c + 1) * hd] - m) * factor)
                total = total + e
                pieces.append(e.astype(jnp.bfloat16))
            o = lax.dot_general(
                jnp.concatenate(pieces, axis=1),
                buf[page[k], 1],
                values_of,
                preferred_element_type=jnp.float32,
            )
            part_sum[r] = part_sum[r] + total
            acc[r] = acc[r] + diagonal(o)
        return carry

    lax.fori_loop(0, loops, second_pass, 0)
    for r in range(rows):
        acc[r] = acc[r] / jnp.sum(part_sum[r], axis=1, keepdims=True)


def attend_near(rows_inst, chunk, steps, lists, count, slot, wait, buf, qbd, fk, fv, local, *work):
    attend_list(rows_inst, chunk, steps, lists, count, wait, buf, qbd, fk, fv, *work)
    acc = work[-1]
    for r in range(rows_inst):
        vacant = functools.reduce(jnp.logical_or, [slot[c] == r for c in range(CAP)])
        local[r] = jnp.where(vacant, 0.0, acc[r]).astype(jnp.bfloat16)


def stay_kernel(links, chunk, far_chunk, fetches, moves_hbm, page_hbm, length_hbm, q_hbm, kv_hbm, pool, *refs):
    (
        local, buf, qbd, fk, fv, hidden, rank, slot,
        page, owner, limit, counts, far_page, far_owner, far_limit,
        moves, page_table, lengths, q, kv, *work, small_sems, sems,
    ) = refs
    rows_inst, heads, hd = q.shape
    fresh_rows = kv.shape[1]
    slots, _, block, columns = pool.shape
    groups = columns // hd
    steps = fresh_rows // (2 * groups)
    me = lax.axis_index("inst")

    small = [
        pltpu.make_async_copy(src, dst, small_sems.at[i])
        for i, (src, dst) in enumerate(
            [(moves_hbm, moves), (page_hbm, page_table), (length_hbm, lengths), (q_hbm, q), (kv_hbm, kv)]
        )
    ]
    for c in small:
        c.start()

    part = slots // fetches

    def fetch(k, plane):
        at = pl.ds(k * part, part)
        return pltpu.make_async_copy(pool.at[at, plane], buf.at[at, plane], sems.at[k, plane])

    for plane in range(2):
        for k in range(fetches):
            fetch(k, plane).start()

    def wait(plane):
        for k in range(fetches):
            fetch(k, plane).wait()

    fk[...] = jnp.zeros(fk.shape, fk.dtype)
    fv[...] = jnp.zeros(fv.shape, fv.dtype)
    for c in small:
        c.wait()
    find_moves(links, moves, rows_inst, me, hidden=hidden, rank=rank, slot=slot)

    def row(r, counts):
        near, far = counts
        length = lengths[r]
        which = jnp.int32(CAP)
        for c in range(CAP):
            which = jnp.where(slot[c] == r, c, which)
        moved = which < CAP

        def one(b, counts):
            near, far = counts
            number = page_table[r, b]
            left = length - b * block
            at = jnp.where(moved, slots + far_chunk, near)
            page[at] = number
            owner[at] = r
            limit[at] = left
            at = jnp.where(moved, far, slots + far_chunk)
            far_page[at] = number
            far_owner[at] = which
            far_limit[at] = left
            return jnp.where(moved, near, near + 1), jnp.where(moved, far + 1, far)

        return lax.fori_loop(0, lax.div(length + (block - 1), jnp.int32(block)), one, (near, far))

    near, far = lax.fori_loop(0, rows_inst, row, (jnp.int32(0), jnp.int32(0)))
    counts[0] = near
    counts[1] = far
    for j in range(chunk):
        page[near + j] = 0
        owner[near + j] = rows_inst
        limit[near + j] = 0
    for j in range(far_chunk):
        far_page[far + j] = 0
        far_owner[far + j] = CAP
        far_limit[far + j] = 0

    for r in range(rows_inst):
        set_row(r, q[r], kv[r], qbd, fk, fv, groups)
    set_row(rows_inst, q[0], None, qbd, None, None, groups)

    @pl.when(far == 0)
    def _():
        attend_near(
            rows_inst, chunk, steps, (page, owner, limit), near, slot, wait,
            buf, qbd, fk, fv, local, *work,
        )

    @pl.when(far > 0)
    def _():
        wait(0)
        wait(1)


def late_kernel(chunk, steps, slot, page, owner, limit, counts, buf, qbd, fk, fv, local_in, order, local, *work):
    @pl.when(counts[1] > 0)
    def _():
        attend_near(
            local.shape[0], chunk, steps, (page, owner, limit), counts[0], slot, lambda plane: None,
            buf, qbd, fk, fv, local, *work,
        )


def moved_kernel(links, chunk, steps, rank, far_page, far_owner, far_limit, counts, buf, *refs):
    recv, back = refs[: links.count], refs[links.count : 2 * links.count]
    qbd, fk, fv, *work = refs[2 * links.count :]
    acc = work[-1]
    heads = qbd.shape[1]
    groups = qbd.shape[2] // acc.shape[2]
    count = counts[1]

    @pl.when(count > 0)
    def _():
        fk[...] = jnp.zeros(fk.shape, fk.dtype)
        fv[...] = jnp.zeros(fv.shape, fv.dtype)
        qbd[...] = jnp.zeros(qbd.shape, qbd.dtype)
        for j in range(links.count):

            def put(j=j):
                set_row(rank[j], recv[j][0:heads, :], recv[j][heads:, :], qbd, fk, fv, groups)

            pl.when(rank[j] < CAP)(put)
        attend_list(
            CAP, chunk, steps, (far_page, far_owner, far_limit), count, lambda plane: None,
            buf, qbd, fk, fv, *work,
        )
        for j in range(links.count):
            back[j][...] = acc[rank[j]].astype(jnp.bfloat16)


def place_kernel(links, hidden, local, *refs):
    back, (out, staged, sem) = refs[: links.count], refs[links.count :]
    staged[...] = local[...]
    for j in range(links.count):

        @pl.when(hidden[j] >= 0)
        def _():
            staged[hidden[j]] = back[j][...]

    write = pltpu.make_async_copy(staged, out, sem)
    write.start()
    write.wait()


def body(kv_pool, page_table, lengths, queries, new_kv, moves):
    links = Links(lax.axis_size("inst"))
    rows_inst, steps, width = queries.shape
    slots, _, block, columns = kv_pool.shape
    groups = columns // HD
    heads_all = width // HD
    heads = steps * heads_all
    fresh_rows = steps * groups * 2
    bf16 = jnp.bfloat16
    f32 = jnp.float32
    i32 = jnp.int32
    q = queries.reshape(rows_inst, steps, heads_all, HD).transpose(0, 2, 1, 3).reshape(rows_inst, heads, HD)
    kv = (
        new_kv.reshape(rows_inst, steps, 2, groups, HD)
        .transpose(0, 1, 3, 2, 4)
        .reshape(rows_inst, fresh_rows, HD)
    )
    smem = pl.BlockSpec(memory_space=SMEM)
    vmem = pl.BlockSpec(memory_space=VMEM)
    hbm = pl.BlockSpec(memory_space=HBM)
    in_hbm = lambda x: pltpu.with_memory_space_constraint(x, HBM)
    move_cols = moves.T
    count = links.count
    chunk = 4
    far_chunk = 5
    fetches = math.gcd(slots, 4)
    mib = 1024 * 1024

    *packed, branch = pl.pallas_call(
        functools.partial(pack_kernel, links),
        out_shape=[jax.ShapeDtypeStruct((heads + fresh_rows, HD), bf16)] * count
        + [SMEM((1,), i32)],
        in_specs=[hbm, hbm, hbm],
        out_specs=[vmem] * count + [smem],
        scratch_shapes=[
            SMEM((count + 1,), i32),
            SMEM(move_cols.shape, i32),
            VMEM(q.shape, bf16),
            VMEM(kv.shape, bf16),
            pltpu.SemaphoreType.DMA((3,)),
        ],
        compiler_params=pltpu.CompilerParams(vmem_limit_bytes=4 * mib),
        name="pack",
    )(in_hbm(move_cols), in_hbm(q), in_hbm(kv))

    def rows_state(rows):
        return [
            VMEM((rows + 1, heads, columns), bf16),
            VMEM((rows, HD, columns), bf16),
            VMEM((rows, HD, columns), bf16),
        ]

    def work_state(rows):
        return [
            VMEM((slots + far_chunk, heads, block), f32),
            VMEM((rows, heads, HD), f32),
        ] + [VMEM((rows + 1, heads, HD), f32)] * 4

    anyspace = pl.BlockSpec(memory_space=pl.ANY)
    blocks = SMEM((slots + far_chunk + 1,), i32)
    staged = VMEM((rows_inst, heads, HD), bf16)

    def rest(which, kv_pool, page_table, lengths, q, kv, move_cols, *packed):
        received = [
            lax.ppermute(x, "inst", links.both(links.forward(which, j))) for j, x in enumerate(packed)
        ]
        (
            local, buf, qbd, fk, fv, hidden, rank, slot,
            page, owner, limit, counts, far_page, far_owner, far_limit,
        ) = pl.pallas_call(
            functools.partial(stay_kernel, links, chunk, far_chunk, fetches),
            out_shape=[staged, VMEM(kv_pool.shape, bf16)]
            + rows_state(rows_inst)
            + [SMEM((count + 1,), i32), SMEM((count + 1,), i32), SMEM((CAP + 1,), i32)]
            + [blocks, blocks, blocks, SMEM((2,), i32), blocks, blocks, blocks],
            in_specs=[hbm] * 6,
            out_specs=[vmem] * 5 + [smem] * 10,
            scratch_shapes=[
                SMEM(move_cols.shape, i32),
                SMEM(page_table.shape, i32),
                SMEM(lengths.shape, i32),
                VMEM(q.shape, bf16),
                VMEM(kv.shape, bf16),
            ]
            + work_state(rows_inst)
            + [pltpu.SemaphoreType.DMA((5,)), pltpu.SemaphoreType.DMA((fetches, 2))],
            compiler_params=pltpu.CompilerParams(vmem_limit_bytes=16 * mib),
            cost_estimate=pl.CostEstimate(flops=2**27, bytes_accessed=2**23, transcendentals=2**18),
            name="stay",
        )(*map(in_hbm, (move_cols, page_table, lengths, q, kv, kv_pool)))
        back = pl.pallas_call(
            functools.partial(moved_kernel, links, far_chunk, steps),
            out_shape=[jax.ShapeDtypeStruct((heads, HD), bf16)] * count,
            in_specs=[smem] * 5 + [vmem] + [vmem] * count,
            out_specs=[vmem] * count,
            scratch_shapes=rows_state(CAP) + work_state(CAP),
            compiler_params=pltpu.CompilerParams(vmem_limit_bytes=16 * mib),
            name="moved",
        )(rank, far_page, far_owner, far_limit, counts, buf, *received)
        ways = [links.backward(which, j) for j in range(count)]
        ways[-1] = links.both(ways[-1])
        returned = [lax.ppermute(x, "inst", way) for x, way in zip(back, ways)]
        local = pl.pallas_call(
            functools.partial(late_kernel, chunk, steps),
            out_shape=staged,
            in_specs=[smem] * 5 + [vmem] * 5 + [anyspace],
            out_specs=vmem,
            scratch_shapes=work_state(rows_inst),
            input_output_aliases={9: 0},
            compiler_params=pltpu.CompilerParams(vmem_limit_bytes=16 * mib),
            cost_estimate=pl.CostEstimate(flops=2**27, bytes_accessed=2**23, transcendentals=2**18),
            name="late",
        )(slot, page, owner, limit, counts, buf, qbd, fk, fv, local, back[0])
        out = pl.pallas_call(
            functools.partial(place_kernel, links),
            out_shape=HBM((rows_inst, heads, HD), bf16),
            in_specs=[smem, vmem] + [vmem] * count,
            out_specs=hbm,
            scratch_shapes=[staged, pltpu.SemaphoreType.DMA],
            compiler_params=pltpu.CompilerParams(vmem_limit_bytes=4 * mib),
            name="place",
        )(hidden, local, *returned)
        out = out.reshape(rows_inst, heads_all, steps, HD).transpose(0, 2, 1, 3)
        return out.reshape(rows_inst, steps, width)

    operands = (kv_pool, page_table, lengths, q, kv, move_cols, *packed)
    if links.split:
        return lax.switch(
            branch[0], [functools.partial(rest, k) for k in range(len(links.halves))], *operands
        )
    return rest(0, *operands)


def solution(mesh):
    placed = (
        P(("groups", "inst"), None, None, "tp"),
        P(("groups", "inst"), None),
        P(("groups", "inst")),
        P(("groups", "inst"), None, "tp"),
        P(("groups", "inst"), None, None, "tp"),
        P("groups", None),
    )
    return jax.shard_map(
        body,
        mesh=mesh,
        in_specs=placed,
        out_specs=P(("groups", "inst"), None, "tp"),
        check_vma=False,
    )
```

```python
import functools
import itertools
import math

import jax
import jax.numpy as jnp
from jax import lax
from jax.experimental import pallas as pl
from jax.experimental.pallas import tpu as pltpu
from jax.sharding import PartitionSpec as P

HD = 128
CAP = 2
NEG = -1e30
MAX_HALVES = 6
SMEM = pltpu.SMEM
VMEM = pltpu.VMEM
HBM = pltpu.HBM


class Links:
    def __init__(self, n):
        self.n = n
        half = n // 2
        self.halves = []
        if n % 2 == 0 and math.comb(n, half) <= MAX_HALVES:
            self.halves = list(itertools.combinations(range(n), half))
        self.split = bool(self.halves)
        self.count = half if self.split else n - 1

    def index(self, busy, a, b):
        n = self.n
        if self.split:
            half = n // 2
            rank_a = sum(jnp.where(k < a, busy[k], 0) for k in range(n))
            rank_b = sum(jnp.where(k < b, 1 - busy[k], 0) for k in range(n))
            return lax.rem(rank_a - rank_b + half, half)
        if n & (n - 1) == 0:
            return (a ^ b) - 1
        return lax.rem(a - b + n, n) - 1

    def branch(self, busy):
        mask = sum(busy[k] << k for k in range(self.n))
        return sum(
            jnp.where(mask == sum(1 << i for i in half), k, 0) for k, half in enumerate(self.halves)
        )

    def forward(self, which, j):
        n = self.n
        if self.split:
            busy = self.halves[which]
            spare = [i for i in range(n) if i not in busy]
            return [(s, busy[(k + j) % len(busy)]) for k, s in enumerate(spare)]
        if n & (n - 1) == 0:
            return [(i, i ^ (j + 1)) for i in range(n)]
        return [(i, (i + j + 1) % n) for i in range(n)]

    def backward(self, which, j):
        return [(b, a) for a, b in self.forward(which, j)]

    def both(self, pairs):
        return sorted(set(pairs) | {(b, a) for a, b in pairs}) if self.split else pairs


def find_moves(links, moves, rows_inst, me, hidden=None, rank=None, slot=None):
    n = links.n
    count = links.count
    for j in range(count + 1):
        if hidden is not None:
            hidden[j] = -1
        if rank is not None:
            rank[j] = CAP
    if slot is not None:
        for c in range(CAP + 1):
            slot[c] = -1
    total = moves.shape[1]
    busy = None
    if links.split:
        froms = [moves[0, m] // rows_inst for m in range(total)]
        busy = [
            functools.reduce(jnp.bitwise_or, [(f == k).astype(jnp.int32) for f in froms]) for k in range(n)
        ]

    def step(m, seen):
        cache_slot = moves[0, m]
        hidden_slot = moves[1, m]
        from_inst = cache_slot // rows_inst
        to_inst = hidden_slot // rows_inst
        index = links.index(busy, from_inst, to_inst)
        if hidden is not None:
            hidden[jnp.where(to_inst == me, index, count)] = lax.rem(hidden_slot, rows_inst)
        mine = from_inst == me
        if rank is not None:
            rank[jnp.where(mine, index, count)] = seen
        if slot is not None:
            slot[jnp.where(mine, seen, CAP)] = lax.rem(cache_slot, rows_inst)
        return jnp.where(mine, seen + 1, seen)

    if links.split:
        seen = jnp.int32(0)
        for m in range(total):
            seen = step(m, seen)
    else:
        lax.fori_loop(0, total, step, jnp.int32(0))
    return busy


def pack_kernel(links, moves_hbm, q_hbm, kv_hbm, *refs):
    outs = refs[: links.count]
    branch, hidden, moves, q, kv, sems = refs[links.count :]
    copies = [
        pltpu.make_async_copy(moves_hbm, moves, sems.at[0]),
        pltpu.make_async_copy(q_hbm, q, sems.at[1]),
        pltpu.make_async_copy(kv_hbm, kv, sems.at[2]),
    ]
    for c in copies:
        c.start()
    rows_inst, heads, _ = q.shape
    me = lax.axis_index("inst")
    copies[0].wait()
    busy = find_moves(links, moves, rows_inst, me, hidden=hidden)
    branch[0] = links.branch(busy) if links.split else 0
    copies[1].wait()
    copies[2].wait()
    for j, out in enumerate(outs):
        row = jnp.maximum(hidden[j], 0)
        out[0:heads, :] = q[row]
        out[heads:, :] = kv[row]


def set_row(at, rows, fresh, qbd, fk, fv, groups):
    heads, hd = rows.shape
    per = heads // groups
    zero = jnp.zeros((per, hd), jnp.bfloat16)
    for g in range(groups):
        for k in range(groups):
            qbd[at, g * per : (g + 1) * per, k * hd : (k + 1) * hd] = (
                rows[g * per : (g + 1) * per] if k == g else zero
            )
    if fk is None:
        return
    fresh = fresh.astype(jnp.float32)
    token = lax.broadcasted_iota(jnp.int32, (16, hd), 0)
    for plane, ref in enumerate((fk, fv)):
        for g in range(groups):
            block = jnp.zeros((16, hd), jnp.float32)
            for u in range(fresh.shape[0] // (2 * groups)):
                line = (u * groups + g) * 2 + plane
                block = jnp.where(token == u, fresh[line : line + 1], block)
            ref[at, 0:16, g * hd : (g + 1) * hd] = block.astype(jnp.bfloat16)


def attend_list(rows, chunk, steps, lists, count, buf, qbd, fk, fv, scores, new, part_max, top, part_sum, acc):
    page, owner, limit = lists
    _, heads, columns = qbd.shape
    hd = acc.shape[2]
    groups = columns // hd
    per = heads // groups
    block = buf.shape[2]
    factor = math.log2(math.e) / math.sqrt(hd)
    loops = lax.div(count + (chunk - 1), jnp.int32(chunk))
    keys_of = (((1,), (1,)), ((), ()))
    values_of = (((1,), (0,)), ((), ()))
    lane = lax.broadcasted_iota(jnp.int32, (heads, block), 1)
    token = lax.broadcasted_iota(jnp.int32, (heads, hd), 1)
    seen = token <= lax.broadcasted_iota(jnp.int32, (heads, hd), 0) % steps

    def diagonal(o):
        return jnp.concatenate(
            [o[g * per : (g + 1) * per, g * hd : (g + 1) * hd] for g in range(groups)], axis=0
        )

    def first(k):
        r = owner[k]
        s = lax.dot_general(qbd[r], buf[page[k], 0], keys_of, preferred_element_type=jnp.float32)
        s = jnp.where(lane < limit[k], s, NEG)
        scores[k] = s
        m = s[:, 0:hd]
        for c in range(1, block // hd):
            m = jnp.maximum(m, s[:, c * hd : (c + 1) * hd])
        part_max[r] = jnp.maximum(part_max[r], m)

    def second(k):
        r = owner[k]
        m = top[r]
        pieces = []
        total = jnp.zeros((heads, hd), jnp.float32)
        for c in range(block // hd):
            e = jnp.exp2((scores[k, :, c * hd : (c + 1) * hd] - m) * factor)
            total = total + e
            pieces.append(e.astype(jnp.bfloat16))
        o = lax.dot_general(
            jnp.concatenate(pieces, axis=1), buf[page[k], 1], values_of, preferred_element_type=jnp.float32
        )
        part_sum[r] = part_sum[r] + total
        acc[r] = acc[r] + diagonal(o)

    def others(do):
        def step(i, carry):
            for j in range(chunk):
                do(i * chunk + j)
            return carry

        lax.fori_loop(1, loops, step, 0)

    for r in range(rows):
        s = lax.dot_general(qbd[r], fk[r], keys_of, preferred_element_type=jnp.float32)
        s = jnp.where(seen, s, NEG)
        new[r] = s
        part_max[r] = s
    part_max[rows] = jnp.zeros((heads, hd), jnp.float32)
    for j in range(chunk):
        first(j)
    others(first)

    top[rows] = jnp.zeros((heads, hd), jnp.float32)
    part_sum[rows] = jnp.zeros((heads, hd), jnp.float32)
    acc[rows] = jnp.zeros((heads, hd), jnp.float32)
    for r in range(rows):
        m = jnp.broadcast_to(jnp.max(part_max[r], axis=1, keepdims=True), (heads, hd))
        top[r] = m
        e = jnp.exp2((new[r] - m) * factor)
        part_sum[r] = e
        acc[r] = diagonal(
            lax.dot_general(e.astype(jnp.bfloat16), fv[r], values_of, preferred_element_type=jnp.float32)
        )
    for j in range(chunk):
        second(j)
    others(second)
    for r in range(rows):
        acc[r] = acc[r] / jnp.sum(part_sum[r], axis=1, keepdims=True)


def list_kernel(links, chunk, far_chunk, fetches, moves_hbm, page_hbm, length_hbm, q_hbm, kv_hbm, pool, *refs):
    (
        buf, qbd, fk, fv, hidden, rank, slot,
        page, owner, limit, counts, far_page, far_owner, far_limit,
        moves, page_table, lengths, q, kv, small_sems, sems,
    ) = refs
    rows_inst, heads, hd = q.shape
    slots, _, block, columns = pool.shape
    groups = columns // hd
    me = lax.axis_index("inst")

    small = [
        pltpu.make_async_copy(src, dst, small_sems.at[i])
        for i, (src, dst) in enumerate(
            [(moves_hbm, moves), (page_hbm, page_table), (length_hbm, lengths), (q_hbm, q), (kv_hbm, kv)]
        )
    ]
    for c in small:
        c.start()

    part = slots // fetches

    def fetch(k, plane):
        at = pl.ds(k * part, part)
        return pltpu.make_async_copy(pool.at[at, plane], buf.at[at, plane], sems.at[k, plane])

    for plane in range(2):
        for k in range(fetches):
            fetch(k, plane).start()

    fk[...] = jnp.zeros(fk.shape, fk.dtype)
    fv[...] = jnp.zeros(fv.shape, fv.dtype)
    for c in small:
        c.wait()
    find_moves(links, moves, rows_inst, me, hidden=hidden, rank=rank, slot=slot)

    def row(r, counts):
        near, far = counts
        length = lengths[r]
        which = jnp.int32(CAP)
        for c in range(CAP):
            which = jnp.where(slot[c] == r, c, which)
        moved = which < CAP

        def one(b, counts):
            near, far = counts
            number = page_table[r, b]
            left = length - b * block
            at = jnp.where(moved, slots + far_chunk, near)
            page[at] = number
            owner[at] = r
            limit[at] = left
            at = jnp.where(moved, far, slots + far_chunk)
            far_page[at] = number
            far_owner[at] = which
            far_limit[at] = left
            return jnp.where(moved, near, near + 1), jnp.where(moved, far + 1, far)

        return lax.fori_loop(0, lax.div(length + (block - 1), jnp.int32(block)), one, (near, far))

    near, far = lax.fori_loop(0, rows_inst, row, (jnp.int32(0), jnp.int32(0)))
    counts[0] = near
    counts[1] = far
    for j in range(chunk):
        page[near + j] = 0
        owner[near + j] = rows_inst
        limit[near + j] = 0
    for j in range(far_chunk):
        far_page[far + j] = 0
        far_owner[far + j] = CAP
        far_limit[far + j] = 0

    for r in range(rows_inst):
        set_row(r, q[r], kv[r], qbd, fk, fv, groups)
    set_row(rows_inst, q[0], None, qbd, None, None, groups)

    for plane in range(2):
        for k in range(fetches):
            fetch(k, plane).wait()


def stay_kernel(chunk, steps, slot, page, owner, limit, counts, buf, qbd, fk, fv, order, local, *work):
    rows_inst = local.shape[0]
    attend_list(rows_inst, chunk, steps, (page, owner, limit), counts[0], buf, qbd, fk, fv, *work)
    acc = work[-1]
    for r in range(rows_inst):
        vacant = functools.reduce(jnp.logical_or, [slot[c] == r for c in range(CAP)])
        local[r] = jnp.where(vacant, 0.0, acc[r]).astype(jnp.bfloat16)


def moved_kernel(links, chunk, steps, rank, far_page, far_owner, far_limit, counts, buf, *refs):
    recv, back = refs[: links.count], refs[links.count : 2 * links.count]
    qbd, fk, fv, *work = refs[2 * links.count :]
    acc = work[-1]
    heads = qbd.shape[1]
    groups = qbd.shape[2] // acc.shape[2]
    count = counts[1]

    @pl.when(count > 0)
    def _():
        fk[:, 16:, :] = jnp.zeros((CAP, fk.shape[1] - 16, fk.shape[2]), fk.dtype)
        fv[:, 16:, :] = jnp.zeros((CAP, fv.shape[1] - 16, fv.shape[2]), fv.dtype)
        for j in range(links.count):

            def put(j=j):
                set_row(rank[j], recv[j][0:heads, :], recv[j][heads:, :], qbd, fk, fv, groups)

            if links.count == CAP:
                put()
            else:
                pl.when(rank[j] < CAP)(put)
        attend_list(
            CAP, chunk, steps, (far_page, far_owner, far_limit), count,
            buf, qbd, fk, fv, *work,
        )
        for j in range(links.count):
            back[j][...] = acc[rank[j]].astype(jnp.bfloat16)


def place_kernel(links, hidden, local, *refs):
    back, (out, staged, sem) = refs[: links.count], refs[links.count :]
    staged[...] = local[...]
    for j in range(links.count):

        @pl.when(hidden[j] >= 0)
        def _():
            staged[hidden[j]] = back[j][...]

    write = pltpu.make_async_copy(staged, out, sem)
    write.start()
    write.wait()


def body(kv_pool, page_table, lengths, queries, new_kv, moves):
    links = Links(lax.axis_size("inst"))
    rows_inst, steps, width = queries.shape
    slots, _, block, columns = kv_pool.shape
    groups = columns // HD
    heads_all = width // HD
    heads = steps * heads_all
    fresh_rows = steps * groups * 2
    bf16 = jnp.bfloat16
    f32 = jnp.float32
    i32 = jnp.int32
    q = queries.reshape(rows_inst, steps, heads_all, HD).transpose(0, 2, 1, 3).reshape(rows_inst, heads, HD)
    kv = (
        new_kv.reshape(rows_inst, steps, 2, groups, HD)
        .transpose(0, 1, 3, 2, 4)
        .reshape(rows_inst, fresh_rows, HD)
    )
    smem = pl.BlockSpec(memory_space=SMEM)
    vmem = pl.BlockSpec(memory_space=VMEM)
    hbm = pl.BlockSpec(memory_space=HBM)
    in_hbm = lambda x: pltpu.with_memory_space_constraint(x, HBM)
    move_cols = moves.T
    count = links.count
    chunk = 4
    far_chunk = 5
    fetches = math.gcd(slots, 4)
    mib = 1024 * 1024

    *packed, branch = pl.pallas_call(
        functools.partial(pack_kernel, links),
        out_shape=[jax.ShapeDtypeStruct((heads + fresh_rows, HD), bf16)] * count
        + [SMEM((1,), i32)],
        in_specs=[hbm, hbm, hbm],
        out_specs=[vmem] * count + [smem],
        scratch_shapes=[
            SMEM((count + 1,), i32),
            SMEM(move_cols.shape, i32),
            VMEM(q.shape, bf16),
            VMEM(kv.shape, bf16),
            pltpu.SemaphoreType.DMA((3,)),
        ],
        compiler_params=pltpu.CompilerParams(vmem_limit_bytes=4 * mib),
        name="pack",
    )(in_hbm(move_cols), in_hbm(q), in_hbm(kv))

    def rows_state(rows):
        return [
            VMEM((rows + 1, heads, columns), bf16),
            VMEM((rows, HD, columns), bf16),
            VMEM((rows, HD, columns), bf16),
        ]

    def work_state(rows):
        return [
            VMEM((slots + far_chunk, heads, block), f32),
            VMEM((rows, heads, HD), f32),
        ] + [VMEM((rows + 1, heads, HD), f32)] * 4

    anyspace = pl.BlockSpec(memory_space=pl.ANY)
    blocks = SMEM((slots + far_chunk + 1,), i32)
    staged = VMEM((rows_inst, heads, HD), bf16)

    def exchange(arrays, ways):
        done = {j: lax.ppermute(arrays[j], "inst", ways[j]) for j in reversed(range(count))}
        return [done[j] for j in range(count)]

    def rest(which, kv_pool, page_table, lengths, q, kv, move_cols, *packed):
        ways = [links.forward(which, j) for j in range(count)]
        received = exchange(packed, [links.both(way) for way in ways])
        (
            buf, qbd, fk, fv, hidden, rank, slot,
            page, owner, limit, counts, far_page, far_owner, far_limit,
        ) = pl.pallas_call(
            functools.partial(list_kernel, links, chunk, far_chunk, fetches),
            out_shape=[VMEM(kv_pool.shape, bf16)]
            + rows_state(rows_inst)
            + [SMEM((count + 1,), i32), SMEM((count + 1,), i32), SMEM((CAP + 1,), i32)]
            + [blocks, blocks, blocks, SMEM((2,), i32), blocks, blocks, blocks],
            in_specs=[hbm] * 6,
            out_specs=[vmem] * 4 + [smem] * 10,
            scratch_shapes=[
                SMEM(move_cols.shape, i32),
                SMEM(page_table.shape, i32),
                SMEM(lengths.shape, i32),
                VMEM(q.shape, bf16),
                VMEM(kv.shape, bf16),
                pltpu.SemaphoreType.DMA((5,)),
                pltpu.SemaphoreType.DMA((fetches, 2)),
            ],
            compiler_params=pltpu.CompilerParams(vmem_limit_bytes=16 * mib),
            cost_estimate=pl.CostEstimate(flops=2**27, bytes_accessed=2**23, transcendentals=2**18),
            name="list",
        )(*map(in_hbm, (move_cols, page_table, lengths, q, kv, kv_pool)))
        back = pl.pallas_call(
            functools.partial(moved_kernel, links, far_chunk, steps),
            out_shape=[jax.ShapeDtypeStruct((heads, HD), bf16)] * count,
            in_specs=[smem] * 5 + [vmem] + [vmem] * count,
            out_specs=[vmem] * count,
            scratch_shapes=rows_state(CAP) + work_state(CAP),
            compiler_params=pltpu.CompilerParams(vmem_limit_bytes=16 * mib),
            name="moved",
        )(rank, far_page, far_owner, far_limit, counts, buf, *received)
        returned = exchange(back, [links.backward(which, j) for j in range(count)])
        local = pl.pallas_call(
            functools.partial(stay_kernel, chunk, steps),
            out_shape=staged,
            in_specs=[smem] * 5 + [vmem] * 4 + [anyspace],
            out_specs=vmem,
            scratch_shapes=work_state(rows_inst),
            compiler_params=pltpu.CompilerParams(vmem_limit_bytes=16 * mib),
            cost_estimate=pl.CostEstimate(flops=2**27, bytes_accessed=2**23, transcendentals=2**18),
            name="stay",
        )(slot, page, owner, limit, counts, buf, qbd, fk, fv, back[0])
        out = pl.pallas_call(
            functools.partial(place_kernel, links),
            out_shape=HBM((rows_inst, heads, HD), bf16),
            in_specs=[smem, vmem] + [vmem] * count,
            out_specs=hbm,
            scratch_shapes=[staged, pltpu.SemaphoreType.DMA],
            compiler_params=pltpu.CompilerParams(vmem_limit_bytes=4 * mib),
            name="place",
        )(hidden, local, *returned)
        out = out.reshape(rows_inst, heads_all, steps, HD).transpose(0, 2, 1, 3)
        return out.reshape(rows_inst, steps, width)

    operands = (kv_pool, page_table, lengths, q, kv, move_cols, *packed)
    if links.split:
        return lax.switch(
            branch[0], [functools.partial(rest, k) for k in range(len(links.halves))], *operands
        )
    return rest(0, *operands)


def solution(mesh):
    placed = (
        P(("groups", "inst"), None, None, "tp"),
        P(("groups", "inst"), None),
        P(("groups", "inst")),
        P(("groups", "inst"), None, "tp"),
        P(("groups", "inst"), None, None, "tp"),
        P("groups", None),
    )
    return jax.shard_map(
        body,
        mesh=mesh,
        in_specs=placed,
        out_specs=P(("groups", "inst"), None, "tp"),
        check_vma=False,
    )
```

```python
import functools
import itertools
import math

import jax
import jax.numpy as jnp
from jax import lax
from jax.experimental import pallas as pl
from jax.experimental.pallas import tpu as pltpu
from jax.sharding import PartitionSpec as P

HD = 128
CAP = 2
NEG = -1e30
MAX_HALVES = 6
SMEM = pltpu.SMEM
VMEM = pltpu.VMEM
HBM = pltpu.HBM


class Links:
    def __init__(self, n):
        self.n = n
        half = n // 2
        self.halves = []
        if n % 2 == 0 and math.comb(n, half) <= MAX_HALVES:
            self.halves = list(itertools.combinations(range(n), half))
        self.split = bool(self.halves)
        self.count = half if self.split else n - 1

    def index(self, busy, a, b):
        n = self.n
        if self.split:
            half = n // 2
            rank_a = sum(jnp.where(k < a, busy[k], 0) for k in range(n))
            rank_b = sum(jnp.where(k < b, 1 - busy[k], 0) for k in range(n))
            return half - 1 - lax.rem(rank_a - rank_b + half, half)
        if n & (n - 1) == 0:
            return (a ^ b) - 1
        return lax.rem(a - b + n, n) - 1

    def branch(self, busy):
        mask = sum(busy[k] << k for k in range(self.n))
        return sum(
            jnp.where(mask == sum(1 << i for i in half), k, 0) for k, half in enumerate(self.halves)
        )

    def forward(self, which, j):
        n = self.n
        if self.split:
            busy = self.halves[which]
            spare = [i for i in range(n) if i not in busy]
            shift = self.count - 1 - j
            return [(s, busy[(k + shift) % len(busy)]) for k, s in enumerate(spare)]
        if n & (n - 1) == 0:
            return [(i, i ^ (j + 1)) for i in range(n)]
        return [(i, (i + j + 1) % n) for i in range(n)]

    def backward(self, which, j):
        return [(b, a) for a, b in self.forward(which, j)]

    def both(self, pairs):
        return sorted(set(pairs) | {(b, a) for a, b in pairs}) if self.split else pairs


def find_moves(links, moves, rows_inst, me, hidden=None, rank=None, slot=None):
    n = links.n
    count = links.count
    for j in range(count + 1):
        if hidden is not None:
            hidden[j] = -1
        if rank is not None:
            rank[j] = CAP
    if slot is not None:
        for c in range(CAP + 1):
            slot[c] = -1
    total = moves.shape[1]
    busy = None
    if links.split:
        froms = [moves[0, m] // rows_inst for m in range(total)]
        busy = [
            functools.reduce(jnp.bitwise_or, [(f == k).astype(jnp.int32) for f in froms]) for k in range(n)
        ]

    def step(m, seen):
        cache_slot = moves[0, m]
        hidden_slot = moves[1, m]
        from_inst = cache_slot // rows_inst
        to_inst = hidden_slot // rows_inst
        index = links.index(busy, from_inst, to_inst)
        if hidden is not None:
            hidden[jnp.where(to_inst == me, index, count)] = lax.rem(hidden_slot, rows_inst)
        mine = from_inst == me
        if rank is not None:
            rank[jnp.where(mine, index, count)] = seen
        if slot is not None:
            slot[jnp.where(mine, seen, CAP)] = lax.rem(cache_slot, rows_inst)
        return jnp.where(mine, seen + 1, seen)

    if links.split:
        seen = jnp.int32(0)
        for m in range(total):
            seen = step(m, seen)
    else:
        lax.fori_loop(0, total, step, jnp.int32(0))
    return busy


def fetch(pool, buf, sems, part, k, plane):
    at = pl.ds(k * part, part)
    return pltpu.make_async_copy(pool.at[at, plane], buf.at[at, plane], sems.at[k, plane])


def pack_kernel(links, part, moves_hbm, q_hbm, kv_hbm, pool, *refs):
    outs = refs[: links.count]
    branch, buf, hidden, moves, q, kv, sems, pool_sems = refs[links.count :]
    copies = [
        pltpu.make_async_copy(moves_hbm, moves, sems.at[0]),
        pltpu.make_async_copy(q_hbm, q, sems.at[1]),
        pltpu.make_async_copy(kv_hbm, kv, sems.at[2]),
    ]
    for c in copies:
        c.start()
    for plane in range(2):
        fetch(pool, buf, pool_sems, part, 0, plane).start()
    rows_inst, heads, _ = q.shape
    me = lax.axis_index("inst")
    copies[0].wait()
    busy = find_moves(links, moves, rows_inst, me, hidden=hidden)
    branch[0] = links.branch(busy) if links.split else 0
    copies[1].wait()
    copies[2].wait()
    for j, out in enumerate(outs):
        row = jnp.maximum(hidden[j], 0)
        out[0:heads, :] = q[row]
        out[heads:, :] = kv[row]
    for plane in range(2):
        fetch(pool, buf, pool_sems, part, 0, plane).wait()


def set_row(at, rows, fresh, qbd, fk, fv, groups):
    heads, hd = rows.shape
    per = heads // groups
    zero = jnp.zeros((per, hd), jnp.bfloat16)
    for g in range(groups):
        for k in range(groups):
            qbd[at, g * per : (g + 1) * per, k * hd : (k + 1) * hd] = (
                rows[g * per : (g + 1) * per] if k == g else zero
            )
    if fk is None:
        return
    fresh = fresh.astype(jnp.float32)
    token = lax.broadcasted_iota(jnp.int32, (16, hd), 0)
    for plane, ref in enumerate((fk, fv)):
        for g in range(groups):
            block = jnp.zeros((16, hd), jnp.float32)
            for u in range(fresh.shape[0] // (2 * groups)):
                line = (u * groups + g) * 2 + plane
                block = jnp.where(token == u, fresh[line : line + 1], block)
            ref[at, 0:16, g * hd : (g + 1) * hd] = block.astype(jnp.bfloat16)


def attend_list(rows, ahead, chunk, steps, lists, count, buf, qbd, fk, fv, scores, new, part_max, top, part_sum, acc):
    page, owner, limit = lists
    _, heads, columns = qbd.shape
    hd = acc.shape[2]
    groups = columns // hd
    per = heads // groups
    block = buf.shape[2]
    factor = math.log2(math.e) / math.sqrt(hd)
    loops = lax.div(count - ahead + (chunk - 1), jnp.int32(chunk))
    keys_of = (((1,), (1,)), ((), ()))
    values_of = (((1,), (0,)), ((), ()))
    lane = lax.broadcasted_iota(jnp.int32, (heads, block), 1)
    token = lax.broadcasted_iota(jnp.int32, (heads, hd), 1)
    seen = token <= lax.broadcasted_iota(jnp.int32, (heads, hd), 0) % steps

    def diagonal(o):
        return jnp.concatenate(
            [o[g * per : (g + 1) * per, g * hd : (g + 1) * hd] for g in range(groups)], axis=0
        )

    def first(k):
        r = owner[k]
        s = lax.dot_general(qbd[r], buf[page[k], 0], keys_of, preferred_element_type=jnp.float32)
        s = jnp.where(lane < limit[k], s, NEG)
        scores[k] = s
        m = s[:, 0:hd]
        for c in range(1, block // hd):
            m = jnp.maximum(m, s[:, c * hd : (c + 1) * hd])
        part_max[r] = jnp.maximum(part_max[r], m)

    def second(k):
        r = owner[k]
        m = top[r]
        pieces = []
        total = jnp.zeros((heads, hd), jnp.float32)
        for c in range(block // hd):
            e = jnp.exp2((scores[k, :, c * hd : (c + 1) * hd] - m) * factor)
            total = total + e
            pieces.append(e.astype(jnp.bfloat16))
        o = lax.dot_general(
            jnp.concatenate(pieces, axis=1), buf[page[k], 1], values_of, preferred_element_type=jnp.float32
        )
        part_sum[r] = part_sum[r] + total
        acc[r] = acc[r] + diagonal(o)

    def others(do):
        def step(i, carry):
            for j in range(chunk):
                do(ahead + i * chunk + j)
            return carry

        lax.fori_loop(0, loops, step, 0)

    for r in range(rows):
        s = lax.dot_general(qbd[r], fk[r], keys_of, preferred_element_type=jnp.float32)
        s = jnp.where(seen, s, NEG)
        new[r] = s
        part_max[r] = s
    part_max[rows] = jnp.zeros((heads, hd), jnp.float32)
    for j in range(ahead):
        first(j)
    others(first)

    top[rows] = jnp.zeros((heads, hd), jnp.float32)
    part_sum[rows] = jnp.zeros((heads, hd), jnp.float32)
    acc[rows] = jnp.zeros((heads, hd), jnp.float32)
    for r in range(rows):
        m = jnp.broadcast_to(jnp.max(part_max[r], axis=1, keepdims=True), (heads, hd))
        top[r] = m
        e = jnp.exp2((new[r] - m) * factor)
        part_sum[r] = e
        acc[r] = diagonal(
            lax.dot_general(e.astype(jnp.bfloat16), fv[r], values_of, preferred_element_type=jnp.float32)
        )
    for j in range(ahead):
        second(j)
    others(second)
    for r in range(rows):
        acc[r] = acc[r] / jnp.sum(part_sum[r], axis=1, keepdims=True)


def list_kernel(links, chunk, far_chunk, part, moves_hbm, page_hbm, length_hbm, q_hbm, kv_hbm, pool, begun, *refs):
    (
        buf, qbd, fk, fv, hidden, rank, slot,
        page, owner, limit, counts, far_page, far_owner, far_limit,
        moves, page_table, lengths, q, kv, small_sems, sems,
    ) = refs
    rows_inst, heads, hd = q.shape
    slots, _, block, columns = pool.shape
    groups = columns // hd
    me = lax.axis_index("inst")

    small = [
        pltpu.make_async_copy(src, dst, small_sems.at[i])
        for i, (src, dst) in enumerate(
            [(moves_hbm, moves), (page_hbm, page_table), (length_hbm, lengths), (q_hbm, q), (kv_hbm, kv)]
        )
    ]
    for c in small:
        c.start()

    rest = [(k, plane) for plane in range(2) for k in range(1, slots // part)]
    for k, plane in rest:
        fetch(pool, buf, sems, part, k, plane).start()

    fk[...] = jnp.zeros(fk.shape, fk.dtype)
    fv[...] = jnp.zeros(fv.shape, fv.dtype)
    for c in small:
        c.wait()
    find_moves(links, moves, rows_inst, me, hidden=hidden, rank=rank, slot=slot)

    def row(r, counts):
        near, far = counts
        length = lengths[r]
        which = jnp.int32(CAP)
        for c in range(CAP):
            which = jnp.where(slot[c] == r, c, which)
        moved = which < CAP

        def one(b, counts):
            near, far = counts
            number = page_table[r, b]
            left = length - b * block
            at = jnp.where(moved, slots + far_chunk, near)
            page[at] = number
            owner[at] = r
            limit[at] = left
            at = jnp.where(moved, far, slots + far_chunk)
            far_page[at] = number
            far_owner[at] = which
            far_limit[at] = left
            return jnp.where(moved, near, near + 1), jnp.where(moved, far + 1, far)

        return lax.fori_loop(0, lax.div(length + (block - 1), jnp.int32(block)), one, (near, far))

    near, far = lax.fori_loop(0, rows_inst, row, (jnp.int32(0), jnp.int32(0)))
    counts[0] = near
    counts[1] = far
    for j in range(chunk):
        page[near + j] = 0
        owner[near + j] = rows_inst
        limit[near + j] = 0
    for j in range(far_chunk):
        far_page[far + j] = 0
        far_owner[far + j] = CAP
        far_limit[far + j] = 0

    for r in range(rows_inst):
        set_row(r, q[r], kv[r], qbd, fk, fv, groups)
    set_row(rows_inst, q[0], None, qbd, None, None, groups)

    for k, plane in rest:
        fetch(pool, buf, sems, part, k, plane).wait()


def stay_kernel(chunk, steps, slot, page, owner, limit, counts, buf, qbd, fk, fv, order, local, *work):
    rows_inst = local.shape[0]
    attend_list(rows_inst, chunk, chunk, steps, (page, owner, limit), counts[0], buf, qbd, fk, fv, *work)
    acc = work[-1]
    for r in range(rows_inst):
        vacant = functools.reduce(jnp.logical_or, [slot[c] == r for c in range(CAP)])
        local[r] = jnp.where(vacant, 0.0, acc[r]).astype(jnp.bfloat16)


def moved_kernel(links, ahead, chunk, steps, rank, far_page, far_owner, far_limit, counts, buf, *refs):
    recv, back = refs[: links.count], refs[links.count : 2 * links.count]
    qbd, fk, fv, *work = refs[2 * links.count :]
    acc = work[-1]
    heads = qbd.shape[1]
    groups = qbd.shape[2] // acc.shape[2]
    count = counts[1]

    @pl.when(count > 0)
    def _():
        fk[:, 16:, :] = jnp.zeros((CAP, fk.shape[1] - 16, fk.shape[2]), fk.dtype)
        fv[:, 16:, :] = jnp.zeros((CAP, fv.shape[1] - 16, fv.shape[2]), fv.dtype)
        for j in range(links.count):

            def put(j=j):
                set_row(rank[j], recv[j][0:heads, :], recv[j][heads:, :], qbd, fk, fv, groups)

            if links.count == CAP:
                put()
            else:
                pl.when(rank[j] < CAP)(put)
        attend_list(
            CAP, ahead, chunk, steps, (far_page, far_owner, far_limit), count,
            buf, qbd, fk, fv, *work,
        )
        for j in range(links.count):
            back[j][...] = acc[rank[j]].astype(jnp.bfloat16)


def place_kernel(links, hidden, local, *refs):
    back, (out, staged, sem) = refs[: links.count], refs[links.count :]
    staged[...] = local[...]
    for j in range(links.count):

        @pl.when(hidden[j] >= 0)
        def _():
            staged[hidden[j]] = back[j][...]

    write = pltpu.make_async_copy(staged, out, sem)
    write.start()
    write.wait()


def body(kv_pool, page_table, lengths, queries, new_kv, moves):
    links = Links(lax.axis_size("inst"))
    rows_inst, steps, width = queries.shape
    slots, _, block, columns = kv_pool.shape
    groups = columns // HD
    heads_all = width // HD
    heads = steps * heads_all
    fresh_rows = steps * groups * 2
    bf16 = jnp.bfloat16
    f32 = jnp.float32
    i32 = jnp.int32
    q = queries.reshape(rows_inst, steps, heads_all, HD).transpose(0, 2, 1, 3).reshape(rows_inst, heads, HD)
    kv = (
        new_kv.reshape(rows_inst, steps, 2, groups, HD)
        .transpose(0, 1, 3, 2, 4)
        .reshape(rows_inst, fresh_rows, HD)
    )
    smem = pl.BlockSpec(memory_space=SMEM)
    vmem = pl.BlockSpec(memory_space=VMEM)
    hbm = pl.BlockSpec(memory_space=HBM)
    in_hbm = lambda x: pltpu.with_memory_space_constraint(x, HBM)
    move_cols = moves.T
    count = links.count
    chunk = 4
    far_chunk = 6
    part = math.gcd(slots, 4)
    mib = 1024 * 1024

    *packed, branch, begun = pl.pallas_call(
        functools.partial(pack_kernel, links, part),
        out_shape=[jax.ShapeDtypeStruct((heads + fresh_rows, HD), bf16)] * count
        + [SMEM((1,), i32), VMEM(kv_pool.shape, bf16)],
        in_specs=[hbm] * 4,
        out_specs=[vmem] * count + [smem, vmem],
        scratch_shapes=[
            SMEM((count + 1,), i32),
            SMEM(move_cols.shape, i32),
            VMEM(q.shape, bf16),
            VMEM(kv.shape, bf16),
            pltpu.SemaphoreType.DMA((3,)),
            pltpu.SemaphoreType.DMA((1, 2)),
        ],
        compiler_params=pltpu.CompilerParams(vmem_limit_bytes=4 * mib),
        name="pack",
    )(*map(in_hbm, (move_cols, q, kv, kv_pool)))

    def rows_state(rows):
        return [
            VMEM((rows + 1, heads, columns), bf16),
            VMEM((rows, HD, columns), bf16),
            VMEM((rows, HD, columns), bf16),
        ]

    def work_state(rows):
        return [
            VMEM((slots + far_chunk, heads, block), f32),
            VMEM((rows, heads, HD), f32),
        ] + [VMEM((rows + 1, heads, HD), f32)] * 4

    anyspace = pl.BlockSpec(memory_space=pl.ANY)
    blocks = SMEM((slots + far_chunk + 1,), i32)
    staged = VMEM((rows_inst, heads, HD), bf16)

    def exchange(arrays, ways):
        return [lax.ppermute(x, "inst", way) for x, way in zip(arrays, ways)]

    def rest(which, kv_pool, page_table, lengths, q, kv, move_cols, begun, *packed):
        ways = [links.forward(which, j) for j in range(count)]
        received = exchange(packed, [links.both(way) for way in ways])
        (
            buf, qbd, fk, fv, hidden, rank, slot,
            page, owner, limit, counts, far_page, far_owner, far_limit,
        ) = pl.pallas_call(
            functools.partial(list_kernel, links, chunk, far_chunk, part),
            out_shape=[VMEM(kv_pool.shape, bf16)]
            + rows_state(rows_inst)
            + [SMEM((count + 1,), i32), SMEM((count + 1,), i32), SMEM((CAP + 1,), i32)]
            + [blocks, blocks, blocks, SMEM((2,), i32), blocks, blocks, blocks],
            in_specs=[hbm] * 6 + [vmem],
            out_specs=[vmem] * 4 + [smem] * 10,
            input_output_aliases={6: 0},
            scratch_shapes=[
                SMEM(move_cols.shape, i32),
                SMEM(page_table.shape, i32),
                SMEM(lengths.shape, i32),
                VMEM(q.shape, bf16),
                VMEM(kv.shape, bf16),
                pltpu.SemaphoreType.DMA((5,)),
                pltpu.SemaphoreType.DMA((slots // part, 2)),
            ],
            compiler_params=pltpu.CompilerParams(vmem_limit_bytes=16 * mib),
            cost_estimate=pl.CostEstimate(flops=2**27, bytes_accessed=2**23, transcendentals=2**18),
            name="list",
        )(*map(in_hbm, (move_cols, page_table, lengths, q, kv, kv_pool)), begun)
        back = pl.pallas_call(
            functools.partial(moved_kernel, links, chunk, far_chunk, steps),
            out_shape=[jax.ShapeDtypeStruct((heads, HD), bf16)] * count,
            in_specs=[smem] * 5 + [vmem] + [vmem] * count,
            out_specs=[vmem] * count,
            scratch_shapes=rows_state(CAP) + work_state(CAP),
            compiler_params=pltpu.CompilerParams(vmem_limit_bytes=16 * mib),
            name="moved",
        )(rank, far_page, far_owner, far_limit, counts, buf, *received)
        returned = exchange(back, [links.backward(which, j) for j in range(count)])
        local = pl.pallas_call(
            functools.partial(stay_kernel, chunk, steps),
            out_shape=staged,
            in_specs=[smem] * 5 + [vmem] * 4 + [anyspace],
            out_specs=vmem,
            scratch_shapes=work_state(rows_inst),
            compiler_params=pltpu.CompilerParams(vmem_limit_bytes=16 * mib),
            cost_estimate=pl.CostEstimate(flops=2**27, bytes_accessed=2**23, transcendentals=2**18),
            name="stay",
        )(slot, page, owner, limit, counts, buf, qbd, fk, fv, back[0])
        out = pl.pallas_call(
            functools.partial(place_kernel, links),
            out_shape=HBM((rows_inst, heads, HD), bf16),
            in_specs=[smem, vmem] + [vmem] * count,
            out_specs=hbm,
            scratch_shapes=[staged, pltpu.SemaphoreType.DMA],
            compiler_params=pltpu.CompilerParams(vmem_limit_bytes=4 * mib),
            name="place",
        )(hidden, local, *returned)
        out = out.reshape(rows_inst, heads_all, steps, HD).transpose(0, 2, 1, 3)
        return out.reshape(rows_inst, steps, width)

    operands = (kv_pool, page_table, lengths, q, kv, move_cols, begun, *packed)
    if links.split:
        return lax.switch(
            branch[0], [functools.partial(rest, k) for k in range(len(links.halves))], *operands
        )
    return rest(0, *operands)


def solution(mesh):
    placed = (
        P(("groups", "inst"), None, None, "tp"),
        P(("groups", "inst"), None),
        P(("groups", "inst")),
        P(("groups", "inst"), None, "tp"),
        P(("groups", "inst"), None, None, "tp"),
        P("groups", None),
    )
    return jax.shard_map(
        body,
        mesh=mesh,
        in_specs=placed,
        out_specs=P(("groups", "inst"), None, "tp"),
        check_vma=False,
    )
```

```python
import functools
import itertools
import math

import jax
import jax.numpy as jnp
from jax import lax
from jax.experimental import pallas as pl
from jax.experimental.pallas import tpu as pltpu
from jax.sharding import PartitionSpec as P

HD = 128
CAP = 2
NEG = -1e30
MAX_HALVES = 6
SMEM = pltpu.SMEM
VMEM = pltpu.VMEM
HBM = pltpu.HBM


class Links:
    def __init__(self, n):
        self.n = n
        half = n // 2
        self.halves = []
        if n % 2 == 0 and math.comb(n, half) <= MAX_HALVES:
            self.halves = list(itertools.combinations(range(n), half))
        self.split = bool(self.halves)
        self.count = half if self.split else n - 1

    def index(self, busy, a, b):
        n = self.n
        if self.split:
            half = n // 2
            rank_a = sum(jnp.where(k < a, busy[k], 0) for k in range(n))
            rank_b = sum(jnp.where(k < b, 1 - busy[k], 0) for k in range(n))
            return lax.rem(rank_a - rank_b + half, half)
        if n & (n - 1) == 0:
            return (a ^ b) - 1
        return lax.rem(a - b + n, n) - 1

    def branch(self, busy):
        mask = sum(busy[k] << k for k in range(self.n))
        return sum(
            jnp.where(mask == sum(1 << i for i in half), k, 0) for k, half in enumerate(self.halves)
        )

    def forward(self, which, j):
        n = self.n
        if self.split:
            busy = self.halves[which]
            spare = [i for i in range(n) if i not in busy]
            return [(s, busy[(k + j) % len(busy)]) for k, s in enumerate(spare)]
        if n & (n - 1) == 0:
            return [(i, i ^ (j + 1)) for i in range(n)]
        return [(i, (i + j + 1) % n) for i in range(n)]

    def backward(self, which, j):
        return [(b, a) for a, b in self.forward(which, j)]

    def both(self, pairs):
        return sorted(set(pairs) | {(b, a) for a, b in pairs}) if self.split else pairs


def find_moves(links, moves, rows_inst, me, hidden=None, rank=None, slot=None):
    n = links.n
    count = links.count
    for j in range(count + 1):
        if hidden is not None:
            hidden[j] = -1
        if rank is not None:
            rank[j] = CAP
    if slot is not None:
        for c in range(CAP + 1):
            slot[c] = -1
    total = moves.shape[1]
    busy = None
    if links.split:
        froms = [moves[0, m] // rows_inst for m in range(total)]
        busy = [
            functools.reduce(jnp.bitwise_or, [(f == k).astype(jnp.int32) for f in froms]) for k in range(n)
        ]

    def step(m, seen):
        cache_slot = moves[0, m]
        hidden_slot = moves[1, m]
        from_inst = cache_slot // rows_inst
        to_inst = hidden_slot // rows_inst
        index = links.index(busy, from_inst, to_inst)
        if hidden is not None:
            hidden[jnp.where(to_inst == me, index, count)] = lax.rem(hidden_slot, rows_inst)
        mine = from_inst == me
        if rank is not None:
            rank[jnp.where(mine, index, count)] = seen
        if slot is not None:
            slot[jnp.where(mine, seen, CAP)] = lax.rem(cache_slot, rows_inst)
        return jnp.where(mine, seen + 1, seen)

    if links.split:
        seen = jnp.int32(0)
        for m in range(total):
            seen = step(m, seen)
    else:
        lax.fori_loop(0, total, step, jnp.int32(0))
    return busy


def pack_kernel(links, moves_hbm, q_hbm, kv_hbm, *refs):
    outs = refs[: links.count]
    branch, hidden, moves, q, kv, sems = refs[links.count :]
    copies = [
        pltpu.make_async_copy(moves_hbm, moves, sems.at[0]),
        pltpu.make_async_copy(q_hbm, q, sems.at[1]),
        pltpu.make_async_copy(kv_hbm, kv, sems.at[2]),
    ]
    for c in copies:
        c.start()
    rows_inst, heads, _ = q.shape
    me = lax.axis_index("inst")
    copies[0].wait()
    busy = find_moves(links, moves, rows_inst, me, hidden=hidden)
    branch[0] = links.branch(busy) if links.split else 0
    copies[1].wait()
    copies[2].wait()
    for j, out in enumerate(outs):
        row = jnp.maximum(hidden[j], 0)
        out[0:heads, :] = q[row]
        out[heads:, :] = kv[row]


def set_row(at, rows, fresh, qbd, fk, fv, groups):
    heads, hd = rows.shape
    per = heads // groups
    zero = jnp.zeros((per, hd), jnp.bfloat16)
    for g in range(groups):
        for k in range(groups):
            qbd[at, g * per : (g + 1) * per, k * hd : (k + 1) * hd] = (
                rows[g * per : (g + 1) * per] if k == g else zero
            )
    if fk is None:
        return
    fresh = fresh.astype(jnp.float32)
    token = lax.broadcasted_iota(jnp.int32, (16, hd), 0)
    for plane, ref in enumerate((fk, fv)):
        for g in range(groups):
            block = jnp.zeros((16, hd), jnp.float32)
            for u in range(fresh.shape[0] // (2 * groups)):
                line = (u * groups + g) * 2 + plane
                block = jnp.where(token == u, fresh[line : line + 1], block)
            ref[at, 0:16, g * hd : (g + 1) * hd] = block.astype(jnp.bfloat16)


def attend_list(rows, ahead, chunk, steps, lists, count, buf, qbd, fk, fv, scores, new, part_max, top, part_sum, acc):
    page, owner, limit = lists
    _, heads, columns = qbd.shape
    hd = acc.shape[2]
    groups = columns // hd
    per = heads // groups
    block = buf.shape[2]
    factor = math.log2(math.e) / math.sqrt(hd)
    loops = lax.div(count - ahead + (chunk - 1), jnp.int32(chunk))
    keys_of = (((1,), (1,)), ((), ()))
    values_of = (((1,), (0,)), ((), ()))
    lane = lax.broadcasted_iota(jnp.int32, (heads, block), 1)
    token = lax.broadcasted_iota(jnp.int32, (heads, hd), 1)
    seen = token <= lax.broadcasted_iota(jnp.int32, (heads, hd), 0) % steps

    def diagonal(o):
        return jnp.concatenate(
            [o[g * per : (g + 1) * per, g * hd : (g + 1) * hd] for g in range(groups)], axis=0
        )

    def first(k):
        r = owner[k]
        s = lax.dot_general(qbd[r], buf[page[k], 0], keys_of, preferred_element_type=jnp.float32)
        s = jnp.where(lane < limit[k], s, NEG)
        scores[k] = s
        m = s[:, 0:hd]
        for c in range(1, block // hd):
            m = jnp.maximum(m, s[:, c * hd : (c + 1) * hd])
        part_max[r] = jnp.maximum(part_max[r], m)

    def second(k):
        r = owner[k]
        m = top[r]
        pieces = []
        total = jnp.zeros((heads, hd), jnp.float32)
        for c in range(block // hd):
            e = jnp.exp2((scores[k, :, c * hd : (c + 1) * hd] - m) * factor)
            total = total + e
            pieces.append(e.astype(jnp.bfloat16))
        o = lax.dot_general(
            jnp.concatenate(pieces, axis=1), buf[page[k], 1], values_of, preferred_element_type=jnp.float32
        )
        part_sum[r] = part_sum[r] + total
        acc[r] = acc[r] + diagonal(o)

    def others(do):
        def step(i, carry):
            for j in range(chunk):
                do(ahead + i * chunk + j)
            return carry

        lax.fori_loop(0, loops, step, 0)

    for r in range(rows):
        s = lax.dot_general(qbd[r], fk[r], keys_of, preferred_element_type=jnp.float32)
        s = jnp.where(seen, s, NEG)
        new[r] = s
        part_max[r] = s
    part_max[rows] = jnp.zeros((heads, hd), jnp.float32)
    for j in range(ahead):
        first(j)
    others(first)

    top[rows] = jnp.zeros((heads, hd), jnp.float32)
    part_sum[rows] = jnp.zeros((heads, hd), jnp.float32)
    acc[rows] = jnp.zeros((heads, hd), jnp.float32)
    for r in range(rows):
        m = jnp.broadcast_to(jnp.max(part_max[r], axis=1, keepdims=True), (heads, hd))
        top[r] = m
        e = jnp.exp2((new[r] - m) * factor)
        part_sum[r] = e
        acc[r] = diagonal(
            lax.dot_general(e.astype(jnp.bfloat16), fv[r], values_of, preferred_element_type=jnp.float32)
        )
    for j in range(ahead):
        second(j)
    others(second)
    for r in range(rows):
        acc[r] = acc[r] / jnp.sum(part_sum[r], axis=1, keepdims=True)


def list_kernel(links, chunk, far_chunk, fetches, moves_hbm, page_hbm, length_hbm, q_hbm, kv_hbm, pool, *refs):
    (
        buf, qbd, fk, fv, hidden, rank, slot,
        page, owner, limit, counts, far_page, far_owner, far_limit,
        moves, page_table, lengths, q, kv, small_sems, sems,
    ) = refs
    rows_inst, heads, hd = q.shape
    slots, _, block, columns = pool.shape
    groups = columns // hd
    me = lax.axis_index("inst")

    small = [
        pltpu.make_async_copy(src, dst, small_sems.at[i])
        for i, (src, dst) in enumerate(
            [(moves_hbm, moves), (page_hbm, page_table), (length_hbm, lengths), (q_hbm, q), (kv_hbm, kv)]
        )
    ]
    for c in small:
        c.start()

    part = slots // fetches

    def fetch(k, plane):
        at = pl.ds(k * part, part)
        return pltpu.make_async_copy(pool.at[at, plane], buf.at[at, plane], sems.at[k, plane])

    for plane in range(2):
        for k in range(fetches):
            fetch(k, plane).start()

    fk[...] = jnp.zeros(fk.shape, fk.dtype)
    fv[...] = jnp.zeros(fv.shape, fv.dtype)
    for c in small:
        c.wait()
    find_moves(links, moves, rows_inst, me, hidden=hidden, rank=rank, slot=slot)

    def row(r, counts):
        near, far = counts
        length = lengths[r]
        which = jnp.int32(CAP)
        for c in range(CAP):
            which = jnp.where(slot[c] == r, c, which)
        moved = which < CAP

        def one(b, counts):
            near, far = counts
            number = page_table[r, b]
            left = length - b * block
            at = jnp.where(moved, slots + far_chunk, near)
            page[at] = number
            owner[at] = r
            limit[at] = left
            at = jnp.where(moved, far, slots + far_chunk)
            far_page[at] = number
            far_owner[at] = which
            far_limit[at] = left
            return jnp.where(moved, near, near + 1), jnp.where(moved, far + 1, far)

        return lax.fori_loop(0, lax.div(length + (block - 1), jnp.int32(block)), one, (near, far))

    near, far = lax.fori_loop(0, rows_inst, row, (jnp.int32(0), jnp.int32(0)))
    counts[0] = near
    counts[1] = far
    for j in range(chunk):
        page[near + j] = 0
        owner[near + j] = rows_inst
        limit[near + j] = 0
    for j in range(far_chunk):
        far_page[far + j] = 0
        far_owner[far + j] = CAP
        far_limit[far + j] = 0

    for r in range(rows_inst):
        set_row(r, q[r], kv[r], qbd, fk, fv, groups)
    set_row(rows_inst, q[0], None, qbd, None, None, groups)

    for plane in range(2):
        for k in range(fetches):
            fetch(k, plane).wait()


def stay_kernel(chunk, steps, slot, page, owner, limit, counts, buf, qbd, fk, fv, order, local, *work):
    rows_inst = local.shape[0]
    attend_list(rows_inst, chunk, chunk, steps, (page, owner, limit), counts[0], buf, qbd, fk, fv, *work)
    acc = work[-1]
    for r in range(rows_inst):
        vacant = functools.reduce(jnp.logical_or, [slot[c] == r for c in range(CAP)])
        local[r] = jnp.where(vacant, 0.0, acc[r]).astype(jnp.bfloat16)


def moved_kernel(links, ahead, chunk, steps, rank, far_page, far_owner, far_limit, counts, buf, *refs):
    recv, back = refs[: links.count], refs[links.count : 2 * links.count]
    qbd, fk, fv, *work = refs[2 * links.count :]
    acc = work[-1]
    heads = qbd.shape[1]
    groups = qbd.shape[2] // acc.shape[2]
    count = counts[1]

    @pl.when(count > 0)
    def _():
        fk[:, 16:, :] = jnp.zeros((CAP, fk.shape[1] - 16, fk.shape[2]), fk.dtype)
        fv[:, 16:, :] = jnp.zeros((CAP, fv.shape[1] - 16, fv.shape[2]), fv.dtype)
        for j in range(links.count):

            def put(j=j):
                set_row(rank[j], recv[j][0:heads, :], recv[j][heads:, :], qbd, fk, fv, groups)

            if links.count == CAP:
                put()
            else:
                pl.when(rank[j] < CAP)(put)
        attend_list(
            CAP, ahead, chunk, steps, (far_page, far_owner, far_limit), count,
            buf, qbd, fk, fv, *work,
        )
        for out, j in zip(back, reversed(range(links.count))):
            out[...] = acc[rank[j]].astype(jnp.bfloat16)


def place_kernel(links, hidden, local, *refs):
    back, (out, staged, sem) = refs[: links.count], refs[links.count :]
    staged[...] = local[...]
    for j in range(links.count):

        @pl.when(hidden[j] >= 0)
        def _():
            staged[hidden[j]] = back[j][...]

    write = pltpu.make_async_copy(staged, out, sem)
    write.start()
    write.wait()


def body(kv_pool, page_table, lengths, queries, new_kv, moves):
    links = Links(lax.axis_size("inst"))
    rows_inst, steps, width = queries.shape
    slots, _, block, columns = kv_pool.shape
    groups = columns // HD
    heads_all = width // HD
    heads = steps * heads_all
    fresh_rows = steps * groups * 2
    bf16 = jnp.bfloat16
    f32 = jnp.float32
    i32 = jnp.int32
    q = queries.reshape(rows_inst, steps, heads_all, HD).transpose(0, 2, 1, 3).reshape(rows_inst, heads, HD)
    kv = (
        new_kv.reshape(rows_inst, steps, 2, groups, HD)
        .transpose(0, 1, 3, 2, 4)
        .reshape(rows_inst, fresh_rows, HD)
    )
    smem = pl.BlockSpec(memory_space=SMEM)
    vmem = pl.BlockSpec(memory_space=VMEM)
    hbm = pl.BlockSpec(memory_space=HBM)
    in_hbm = lambda x: pltpu.with_memory_space_constraint(x, HBM)
    move_cols = moves.T
    count = links.count
    chunk = 4
    far_chunk = 6
    fetches = math.gcd(slots, 4)
    mib = 1024 * 1024

    *packed, branch = pl.pallas_call(
        functools.partial(pack_kernel, links),
        out_shape=[jax.ShapeDtypeStruct((heads + fresh_rows, HD), bf16)] * count
        + [SMEM((1,), i32)],
        in_specs=[hbm, hbm, hbm],
        out_specs=[vmem] * count + [smem],
        scratch_shapes=[
            SMEM((count + 1,), i32),
            SMEM(move_cols.shape, i32),
            VMEM(q.shape, bf16),
            VMEM(kv.shape, bf16),
            pltpu.SemaphoreType.DMA((3,)),
        ],
        compiler_params=pltpu.CompilerParams(vmem_limit_bytes=4 * mib),
        name="pack",
    )(in_hbm(move_cols), in_hbm(q), in_hbm(kv))

    def rows_state(rows):
        return [
            VMEM((rows + 1, heads, columns), bf16),
            VMEM((rows, HD, columns), bf16),
            VMEM((rows, HD, columns), bf16),
        ]

    def work_state(rows):
        return [
            VMEM((slots + far_chunk, heads, block), f32),
            VMEM((rows, heads, HD), f32),
        ] + [VMEM((rows + 1, heads, HD), f32)] * 4

    anyspace = pl.BlockSpec(memory_space=pl.ANY)
    blocks = SMEM((slots + far_chunk + 1,), i32)
    staged = VMEM((rows_inst, heads, HD), bf16)

    def rest(which, kv_pool, page_table, lengths, q, kv, move_cols, *packed):
        ways = [links.forward(which, j) for j in range(count)]
        received = [lax.ppermute(x, "inst", links.both(way)) for x, way in zip(packed, ways)]
        (
            buf, qbd, fk, fv, hidden, rank, slot,
            page, owner, limit, counts, far_page, far_owner, far_limit,
        ) = pl.pallas_call(
            functools.partial(list_kernel, links, chunk, far_chunk, fetches),
            out_shape=[VMEM(kv_pool.shape, bf16)]
            + rows_state(rows_inst)
            + [SMEM((count + 1,), i32), SMEM((count + 1,), i32), SMEM((CAP + 1,), i32)]
            + [blocks, blocks, blocks, SMEM((2,), i32), blocks, blocks, blocks],
            in_specs=[hbm] * 6,
            out_specs=[vmem] * 4 + [smem] * 10,
            scratch_shapes=[
                SMEM(move_cols.shape, i32),
                SMEM(page_table.shape, i32),
                SMEM(lengths.shape, i32),
                VMEM(q.shape, bf16),
                VMEM(kv.shape, bf16),
                pltpu.SemaphoreType.DMA((5,)),
                pltpu.SemaphoreType.DMA((fetches, 2)),
            ],
            compiler_params=pltpu.CompilerParams(vmem_limit_bytes=16 * mib),
            cost_estimate=pl.CostEstimate(flops=2**27, bytes_accessed=2**23, transcendentals=2**18),
            name="list",
        )(*map(in_hbm, (move_cols, page_table, lengths, q, kv, kv_pool)))
        back = pl.pallas_call(
            functools.partial(moved_kernel, links, chunk, far_chunk, steps),
            out_shape=[jax.ShapeDtypeStruct((heads, HD), bf16)] * count,
            in_specs=[smem] * 5 + [vmem] + [vmem] * count,
            out_specs=[vmem] * count,
            scratch_shapes=rows_state(CAP) + work_state(CAP),
            compiler_params=pltpu.CompilerParams(vmem_limit_bytes=16 * mib),
            name="moved",
        )(rank, far_page, far_owner, far_limit, counts, buf, *received)
        ways = [links.backward(which, j) for j in range(count)]
        ways[0] = links.both(ways[0])
        returned = [lax.ppermute(x, "inst", way) for x, way in zip(back, reversed(ways))]
        returned.reverse()
        local = pl.pallas_call(
            functools.partial(stay_kernel, chunk, steps),
            out_shape=staged,
            in_specs=[smem] * 5 + [vmem] * 4 + [anyspace],
            out_specs=vmem,
            scratch_shapes=work_state(rows_inst),
            compiler_params=pltpu.CompilerParams(vmem_limit_bytes=16 * mib),
            cost_estimate=pl.CostEstimate(flops=2**27, bytes_accessed=2**23, transcendentals=2**18),
            name="stay",
        )(slot, page, owner, limit, counts, buf, qbd, fk, fv, back[0])
        out = pl.pallas_call(
            functools.partial(place_kernel, links),
            out_shape=HBM((rows_inst, heads, HD), bf16),
            in_specs=[smem, vmem] + [vmem] * count,
            out_specs=hbm,
            scratch_shapes=[staged, pltpu.SemaphoreType.DMA],
            compiler_params=pltpu.CompilerParams(vmem_limit_bytes=4 * mib),
            name="place",
        )(hidden, local, *returned)
        out = out.reshape(rows_inst, heads_all, steps, HD).transpose(0, 2, 1, 3)
        return out.reshape(rows_inst, steps, width)

    operands = (kv_pool, page_table, lengths, q, kv, move_cols, *packed)
    if links.split:
        return lax.switch(
            branch[0], [functools.partial(rest, k) for k in range(len(links.halves))], *operands
        )
    return rest(0, *operands)


def solution(mesh):
    placed = (
        P(("groups", "inst"), None, None, "tp"),
        P(("groups", "inst"), None),
        P(("groups", "inst")),
        P(("groups", "inst"), None, "tp"),
        P(("groups", "inst"), None, None, "tp"),
        P("groups", None),
    )
    return jax.shard_map(
        body,
        mesh=mesh,
        in_specs=placed,
        out_specs=P(("groups", "inst"), None, "tp"),
        check_vma=False,
    )
```

```python
import functools
import itertools
import math

import jax
import jax.numpy as jnp
from jax import lax
from jax.experimental import pallas as pl
from jax.experimental.pallas import tpu as pltpu
from jax.sharding import PartitionSpec as P

HD = 128
CAP = 2
NEG = -1e30
MAX_HALVES = 6
SMEM = pltpu.SMEM
VMEM = pltpu.VMEM
HBM = pltpu.HBM


class Links:
    def __init__(self, n):
        self.n = n
        half = n // 2
        self.halves = []
        if n % 2 == 0 and math.comb(n, half) <= MAX_HALVES:
            self.halves = list(itertools.combinations(range(n), half))
        self.split = bool(self.halves)
        self.count = half if self.split else n - 1

    def index(self, busy, a, b):
        n = self.n
        if self.split:
            half = n // 2
            rank_a = sum(jnp.where(k < a, busy[k], 0) for k in range(n))
            rank_b = sum(jnp.where(k < b, 1 - busy[k], 0) for k in range(n))
            return lax.rem(rank_a - rank_b + half, half)
        if n & (n - 1) == 0:
            return (a ^ b) - 1
        return lax.rem(a - b + n, n) - 1

    def branch(self, busy):
        mask = sum(busy[k] << k for k in range(self.n))
        return sum(
            jnp.where(mask == sum(1 << i for i in half), k, 0) for k, half in enumerate(self.halves)
        )

    def forward(self, which, j):
        n = self.n
        if self.split:
            busy = self.halves[which]
            spare = [i for i in range(n) if i not in busy]
            return [(s, busy[(k + j) % len(busy)]) for k, s in enumerate(spare)]
        if n & (n - 1) == 0:
            return [(i, i ^ (j + 1)) for i in range(n)]
        return [(i, (i + j + 1) % n) for i in range(n)]

    def backward(self, which, j):
        return [(b, a) for a, b in self.forward(which, j)]

    def both(self, pairs):
        return sorted(set(pairs) | {(b, a) for a, b in pairs}) if self.split else pairs


def find_moves(links, moves, rows_inst, me, hidden=None, rank=None, slot=None):
    n = links.n
    count = links.count
    for j in range(count + 1):
        if hidden is not None:
            hidden[j] = -1
        if rank is not None:
            rank[j] = CAP
    if slot is not None:
        for c in range(CAP + 1):
            slot[c] = -1
    total = moves.shape[1]
    busy = None
    if links.split:
        froms = [moves[0, m] // rows_inst for m in range(total)]
        busy = [
            functools.reduce(jnp.bitwise_or, [(f == k).astype(jnp.int32) for f in froms]) for k in range(n)
        ]

    def step(m, seen):
        cache_slot = moves[0, m]
        hidden_slot = moves[1, m]
        from_inst = cache_slot // rows_inst
        to_inst = hidden_slot // rows_inst
        index = links.index(busy, from_inst, to_inst)
        if hidden is not None:
            hidden[jnp.where(to_inst == me, index, count)] = lax.rem(hidden_slot, rows_inst)
        mine = from_inst == me
        if rank is not None:
            rank[jnp.where(mine, index, count)] = seen
        if slot is not None:
            slot[jnp.where(mine, seen, CAP)] = lax.rem(cache_slot, rows_inst)
        return jnp.where(mine, seen + 1, seen)

    if links.split:
        seen = jnp.int32(0)
        for m in range(total):
            seen = step(m, seen)
    else:
        lax.fori_loop(0, total, step, jnp.int32(0))
    return busy


def pack_kernel(links, moves_hbm, q_hbm, kv_hbm, *refs):
    outs = refs[: links.count]
    branch, hidden, moves, q, kv, sems = refs[links.count :]
    copies = [
        pltpu.make_async_copy(moves_hbm, moves, sems.at[0]),
        pltpu.make_async_copy(q_hbm, q, sems.at[1]),
        pltpu.make_async_copy(kv_hbm, kv, sems.at[2]),
    ]
    for c in copies:
        c.start()
    rows_inst, heads, _ = q.shape
    me = lax.axis_index("inst")
    copies[0].wait()
    busy = find_moves(links, moves, rows_inst, me, hidden=hidden)
    branch[0] = links.branch(busy) if links.split else 0
    copies[1].wait()
    copies[2].wait()
    for j, out in enumerate(outs):
        row = jnp.maximum(hidden[j], 0)
        out[0:heads, :] = q[row]
        out[heads:, :] = kv[row]


def set_row(at, rows, fresh, qbd, fk, fv, groups):
    heads, hd = rows.shape
    per = heads // groups
    zero = jnp.zeros((per, hd), jnp.bfloat16)
    for g in range(groups):
        for k in range(groups):
            qbd[at, g * per : (g + 1) * per, k * hd : (k + 1) * hd] = (
                rows[g * per : (g + 1) * per] if k == g else zero
            )
    if fk is None:
        return
    fresh = fresh.astype(jnp.float32)
    token = lax.broadcasted_iota(jnp.int32, (16, hd), 0)
    for plane, ref in enumerate((fk, fv)):
        for g in range(groups):
            block = jnp.zeros((16, hd), jnp.float32)
            for u in range(fresh.shape[0] // (2 * groups)):
                line = (u * groups + g) * 2 + plane
                block = jnp.where(token == u, fresh[line : line + 1], block)
            ref[at, 0:16, g * hd : (g + 1) * hd] = block.astype(jnp.bfloat16)


def attend_list(rows, ahead, chunk, steps, lists, count, buf, qbd, fk, fv, scores, new, part_max, top, part_sum, acc):
    page, owner, limit = lists
    _, heads, columns = qbd.shape
    hd = acc.shape[2]
    groups = columns // hd
    per = heads // groups
    block = buf.shape[2]
    factor = math.log2(math.e) / math.sqrt(hd)
    loops = lax.div(count - ahead + (chunk - 1), jnp.int32(chunk))
    keys_of = (((1,), (1,)), ((), ()))
    values_of = (((1,), (0,)), ((), ()))
    lane = lax.broadcasted_iota(jnp.int32, (heads, block), 1)
    token = lax.broadcasted_iota(jnp.int32, (heads, hd), 1)
    seen = token <= lax.broadcasted_iota(jnp.int32, (heads, hd), 0) % steps

    def diagonal(o):
        return jnp.concatenate(
            [o[g * per : (g + 1) * per, g * hd : (g + 1) * hd] for g in range(groups)], axis=0
        )

    def first(k):
        r = owner[k]
        s = lax.dot_general(qbd[r], buf[page[k], 0], keys_of, preferred_element_type=jnp.float32)
        s = jnp.where(lane < limit[k], s, NEG)
        scores[k] = s
        m = s[:, 0:hd]
        for c in range(1, block // hd):
            m = jnp.maximum(m, s[:, c * hd : (c + 1) * hd])
        part_max[r] = jnp.maximum(part_max[r], m)

    def second(k):
        r = owner[k]
        m = top[r]
        pieces = []
        total = jnp.zeros((heads, hd), jnp.float32)
        for c in range(block // hd):
            e = jnp.exp2((scores[k, :, c * hd : (c + 1) * hd] - m) * factor)
            total = total + e
            pieces.append(e.astype(jnp.bfloat16))
        o = lax.dot_general(
            jnp.concatenate(pieces, axis=1), buf[page[k], 1], values_of, preferred_element_type=jnp.float32
        )
        part_sum[r] = part_sum[r] + total
        acc[r] = acc[r] + diagonal(o)

    def others(do):
        def step(i, carry):
            for j in range(chunk):
                do(ahead + i * chunk + j)
            return carry

        lax.fori_loop(0, loops, step, 0)

    for r in range(rows):
        s = lax.dot_general(qbd[r], fk[r], keys_of, preferred_element_type=jnp.float32)
        s = jnp.where(seen, s, NEG)
        new[r] = s
        part_max[r] = s
    part_max[rows] = jnp.zeros((heads, hd), jnp.float32)
    for j in range(ahead):
        first(j)
    others(first)

    top[rows] = jnp.zeros((heads, hd), jnp.float32)
    part_sum[rows] = jnp.zeros((heads, hd), jnp.float32)
    acc[rows] = jnp.zeros((heads, hd), jnp.float32)
    for r in range(rows):
        m = jnp.broadcast_to(jnp.max(part_max[r], axis=1, keepdims=True), (heads, hd))
        top[r] = m
        e = jnp.exp2((new[r] - m) * factor)
        part_sum[r] = e
        acc[r] = diagonal(
            lax.dot_general(e.astype(jnp.bfloat16), fv[r], values_of, preferred_element_type=jnp.float32)
        )
    for j in range(ahead):
        second(j)
    others(second)
    for r in range(rows):
        acc[r] = acc[r] / jnp.sum(part_sum[r], axis=1, keepdims=True)


def list_kernel(links, chunk, far_chunk, fetches, moves_hbm, page_hbm, length_hbm, q_hbm, kv_hbm, pool, *refs):
    (
        buf, qbd, fk, fv, hidden, rank, slot,
        page, owner, limit, counts, far_page, far_owner, far_limit,
        moves, page_table, lengths, q, kv, small_sems, sems,
    ) = refs
    rows_inst, heads, hd = q.shape
    slots, _, block, columns = pool.shape
    groups = columns // hd
    me = lax.axis_index("inst")

    small = [
        pltpu.make_async_copy(src, dst, small_sems.at[i])
        for i, (src, dst) in enumerate(
            [(moves_hbm, moves), (page_hbm, page_table), (length_hbm, lengths), (q_hbm, q), (kv_hbm, kv)]
        )
    ]
    for c in small:
        c.start()

    part = slots // fetches

    def fetch(k, plane):
        at = pl.ds(k * part, part)
        return pltpu.make_async_copy(pool.at[at, plane], buf.at[at, plane], sems.at[k, plane])

    for plane in range(2):
        for k in range(fetches):
            fetch(k, plane).start()

    fk[...] = jnp.zeros(fk.shape, fk.dtype)
    fv[...] = jnp.zeros(fv.shape, fv.dtype)
    for c in small:
        c.wait()
    find_moves(links, moves, rows_inst, me, hidden=hidden, rank=rank, slot=slot)

    def row(r, counts):
        near, far = counts
        length = lengths[r]
        which = jnp.int32(CAP)
        for c in range(CAP):
            which = jnp.where(slot[c] == r, c, which)
        moved = which < CAP

        def one(b, counts):
            near, far = counts
            number = page_table[r, b]
            left = length - b * block
            at = jnp.where(moved, slots + far_chunk, near)
            page[at] = number
            owner[at] = r
            limit[at] = left
            at = jnp.where(moved, far, slots + far_chunk)
            far_page[at] = number
            far_owner[at] = which
            far_limit[at] = left
            return jnp.where(moved, near, near + 1), jnp.where(moved, far + 1, far)

        return lax.fori_loop(0, lax.div(length + (block - 1), jnp.int32(block)), one, (near, far))

    near, far = lax.fori_loop(0, rows_inst, row, (jnp.int32(0), jnp.int32(0)))
    counts[0] = near
    counts[1] = far
    for j in range(chunk):
        page[near + j] = 0
        owner[near + j] = rows_inst
        limit[near + j] = 0
    for j in range(far_chunk):
        far_page[far + j] = 0
        far_owner[far + j] = CAP
        far_limit[far + j] = 0

    for r in range(rows_inst):
        set_row(r, q[r], kv[r], qbd, fk, fv, groups)
    set_row(rows_inst, q[0], None, qbd, None, None, groups)

    for plane in range(2):
        for k in range(fetches):
            fetch(k, plane).wait()


def stay_kernel(chunk, steps, slot, page, owner, limit, counts, buf, qbd, fk, fv, order, local, *work):
    rows_inst = local.shape[0]
    attend_list(rows_inst, chunk, chunk, steps, (page, owner, limit), counts[0], buf, qbd, fk, fv, *work)
    acc = work[-1]
    for r in range(rows_inst):
        vacant = functools.reduce(jnp.logical_or, [slot[c] == r for c in range(CAP)])
        local[r] = jnp.where(vacant, 0.0, acc[r]).astype(jnp.bfloat16)


def moved_kernel(links, ahead, chunk, steps, rank, far_page, far_owner, far_limit, counts, buf, *refs):
    recv, back = refs[: links.count], refs[links.count : 2 * links.count]
    qbd, fk, fv, *work = refs[2 * links.count :]
    acc = work[-1]
    heads = qbd.shape[1]
    groups = qbd.shape[2] // acc.shape[2]
    count = counts[1]

    @pl.when(count > 0)
    def _():
        fk[:, 16:, :] = jnp.zeros((CAP, fk.shape[1] - 16, fk.shape[2]), fk.dtype)
        fv[:, 16:, :] = jnp.zeros((CAP, fv.shape[1] - 16, fv.shape[2]), fv.dtype)
        for j in range(links.count):

            def put(j=j):
                set_row(rank[j], recv[j][0:heads, :], recv[j][heads:, :], qbd, fk, fv, groups)

            if links.count == CAP:
                put()
            else:
                pl.when(rank[j] < CAP)(put)
        attend_list(
            CAP, ahead, chunk, steps, (far_page, far_owner, far_limit), count,
            buf, qbd, fk, fv, *work,
        )
        for out, j in zip(back, reversed(range(links.count))):
            out[...] = acc[rank[j]].astype(jnp.bfloat16)


def place_kernel(links, hidden, local, *refs):
    back, (out, staged, sem) = refs[: links.count], refs[links.count :]
    staged[...] = local[...]
    for ref, j in zip(back, reversed(range(links.count))):

        def put(ref=ref, j=j):
            staged[hidden[j]] = ref[...]

        pl.when(hidden[j] >= 0)(put)

    write = pltpu.make_async_copy(staged, out, sem)
    write.start()
    write.wait()


def body(kv_pool, page_table, lengths, queries, new_kv, moves):
    links = Links(lax.axis_size("inst"))
    rows_inst, steps, width = queries.shape
    slots, _, block, columns = kv_pool.shape
    groups = columns // HD
    heads_all = width // HD
    heads = steps * heads_all
    fresh_rows = steps * groups * 2
    bf16 = jnp.bfloat16
    f32 = jnp.float32
    i32 = jnp.int32
    q = queries.reshape(rows_inst, steps, heads_all, HD).transpose(0, 2, 1, 3).reshape(rows_inst, heads, HD)
    kv = (
        new_kv.reshape(rows_inst, steps, 2, groups, HD)
        .transpose(0, 1, 3, 2, 4)
        .reshape(rows_inst, fresh_rows, HD)
    )
    smem = pl.BlockSpec(memory_space=SMEM)
    vmem = pl.BlockSpec(memory_space=VMEM)
    hbm = pl.BlockSpec(memory_space=HBM)
    in_hbm = lambda x: pltpu.with_memory_space_constraint(x, HBM)
    move_cols = moves.T
    count = links.count
    chunk = 4
    far_chunk = 6
    fetches = math.gcd(slots, 4)
    mib = 1024 * 1024

    *packed, branch = pl.pallas_call(
        functools.partial(pack_kernel, links),
        out_shape=[jax.ShapeDtypeStruct((heads + fresh_rows, HD), bf16)] * count
        + [SMEM((1,), i32)],
        in_specs=[hbm, hbm, hbm],
        out_specs=[vmem] * count + [smem],
        scratch_shapes=[
            SMEM((count + 1,), i32),
            SMEM(move_cols.shape, i32),
            VMEM(q.shape, bf16),
            VMEM(kv.shape, bf16),
            pltpu.SemaphoreType.DMA((3,)),
        ],
        compiler_params=pltpu.CompilerParams(vmem_limit_bytes=4 * mib),
        name="pack",
    )(in_hbm(move_cols), in_hbm(q), in_hbm(kv))

    def rows_state(rows):
        return [
            VMEM((rows + 1, heads, columns), bf16),
            VMEM((rows, HD, columns), bf16),
            VMEM((rows, HD, columns), bf16),
        ]

    def work_state(rows):
        return [
            VMEM((slots + far_chunk, heads, block), f32),
            VMEM((rows, heads, HD), f32),
        ] + [VMEM((rows + 1, heads, HD), f32)] * 4

    anyspace = pl.BlockSpec(memory_space=pl.ANY)
    blocks = SMEM((slots + far_chunk + 1,), i32)
    staged = VMEM((rows_inst, heads, HD), bf16)

    def rest(which, kv_pool, page_table, lengths, q, kv, move_cols, *packed):
        ways = [links.forward(which, j) for j in range(count)]
        received = [lax.ppermute(x, "inst", links.both(way)) for x, way in zip(packed, ways)]
        (
            buf, qbd, fk, fv, hidden, rank, slot,
            page, owner, limit, counts, far_page, far_owner, far_limit,
        ) = pl.pallas_call(
            functools.partial(list_kernel, links, chunk, far_chunk, fetches),
            out_shape=[VMEM(kv_pool.shape, bf16)]
            + rows_state(rows_inst)
            + [SMEM((count + 1,), i32), SMEM((count + 1,), i32), SMEM((CAP + 1,), i32)]
            + [blocks, blocks, blocks, SMEM((2,), i32), blocks, blocks, blocks],
            in_specs=[hbm] * 6,
            out_specs=[vmem] * 4 + [smem] * 10,
            scratch_shapes=[
                SMEM(move_cols.shape, i32),
                SMEM(page_table.shape, i32),
                SMEM(lengths.shape, i32),
                VMEM(q.shape, bf16),
                VMEM(kv.shape, bf16),
                pltpu.SemaphoreType.DMA((5,)),
                pltpu.SemaphoreType.DMA((fetches, 2)),
            ],
            compiler_params=pltpu.CompilerParams(vmem_limit_bytes=16 * mib),
            cost_estimate=pl.CostEstimate(flops=2**27, bytes_accessed=2**23, transcendentals=2**18),
            name="list",
        )(*map(in_hbm, (move_cols, page_table, lengths, q, kv, kv_pool)))
        back = pl.pallas_call(
            functools.partial(moved_kernel, links, chunk, far_chunk, steps),
            out_shape=[jax.ShapeDtypeStruct((heads, HD), bf16)] * count,
            in_specs=[smem] * 5 + [vmem] + [vmem] * count,
            out_specs=[vmem] * count,
            scratch_shapes=rows_state(CAP) + work_state(CAP),
            compiler_params=pltpu.CompilerParams(vmem_limit_bytes=16 * mib),
            name="moved",
        )(rank, far_page, far_owner, far_limit, counts, buf, *received)
        ways = [links.backward(which, j) for j in range(count)]
        ways[0] = links.both(ways[0])
        returned = [lax.ppermute(x, "inst", way) for x, way in zip(back, reversed(ways))]
        local = pl.pallas_call(
            functools.partial(stay_kernel, chunk, steps),
            out_shape=staged,
            in_specs=[smem] * 5 + [vmem] * 4 + [anyspace],
            out_specs=vmem,
            scratch_shapes=work_state(rows_inst),
            compiler_params=pltpu.CompilerParams(vmem_limit_bytes=16 * mib),
            cost_estimate=pl.CostEstimate(flops=2**27, bytes_accessed=2**23, transcendentals=2**18),
            name="stay",
        )(slot, page, owner, limit, counts, buf, qbd, fk, fv, back[0])
        out = pl.pallas_call(
            functools.partial(place_kernel, links),
            out_shape=HBM((rows_inst, heads, HD), bf16),
            in_specs=[smem, vmem] + [vmem] * count,
            out_specs=hbm,
            scratch_shapes=[staged, pltpu.SemaphoreType.DMA],
            compiler_params=pltpu.CompilerParams(vmem_limit_bytes=4 * mib),
            name="place",
        )(hidden, local, *returned)
        out = out.reshape(rows_inst, heads_all, steps, HD).transpose(0, 2, 1, 3)
        return out.reshape(rows_inst, steps, width)

    operands = (kv_pool, page_table, lengths, q, kv, move_cols, *packed)
    if links.split:
        return lax.switch(
            branch[0], [functools.partial(rest, k) for k in range(len(links.halves))], *operands
        )
    return rest(0, *operands)


def solution(mesh):
    placed = (
        P(("groups", "inst"), None, None, "tp"),
        P(("groups", "inst"), None),
        P(("groups", "inst")),
        P(("groups", "inst"), None, "tp"),
        P(("groups", "inst"), None, None, "tp"),
        P("groups", None),
    )
    return jax.shard_map(
        body,
        mesh=mesh,
        in_specs=placed,
        out_specs=P(("groups", "inst"), None, "tp"),
        check_vma=False,
    )
```

```python
import functools
import itertools
import math

import jax
import jax.numpy as jnp
from jax import lax
from jax.experimental import pallas as pl
from jax.experimental.pallas import tpu as pltpu
from jax.sharding import PartitionSpec as P

HD = 128
CAP = 2
NEG = -1e30
MAX_SPLITS = 3
SMEM = pltpu.SMEM
VMEM = pltpu.VMEM
HBM = pltpu.HBM


class Links:
    def __init__(self, n):
        self.n = n
        half = n // 2
        self.halves = []
        if n % 2 == 0 and math.comb(n, half) <= 2 * MAX_SPLITS:
            self.halves = [c for c in itertools.combinations(range(n), half) if 0 in c]
        self.split = bool(self.halves)
        self.count = half if self.split else n - 1

    def index(self, busy, a, b):
        n = self.n
        if self.split:
            half = n // 2
            rank_a = sum(jnp.where(k < a, busy[k], 0) for k in range(n))
            rank_b = sum(jnp.where(k < b, 1 - busy[k], 0) for k in range(n))
            shift = jnp.where(busy[0] == 1, rank_b - rank_a, rank_a - rank_b)
            return half - 1 - lax.rem(shift + half, half)
        if n & (n - 1) == 0:
            return (a ^ b) - 1
        return lax.rem(a - b + n, n) - 1

    def branch(self, busy):
        mask = sum(jnp.where(busy[k] == busy[0], 1 << k, 0) for k in range(self.n))
        return sum(
            jnp.where(mask == sum(1 << i for i in half), k, 0) for k, half in enumerate(self.halves)
        )

    def forward(self, which, j):
        n = self.n
        if self.split:
            half = self.halves[which]
            other = [i for i in range(n) if i not in half]
            shift = self.count - 1 - j
            pairs = [(a, other[(k + shift) % len(other)]) for k, a in enumerate(half)]
            return sorted(pairs + [(b, a) for a, b in pairs])
        if n & (n - 1) == 0:
            return [(i, i ^ (j + 1)) for i in range(n)]
        return [(i, (i + j + 1) % n) for i in range(n)]

    def backward(self, which, j):
        return [(b, a) for a, b in self.forward(which, j)]


def find_moves(links, moves, rows_inst, me, hidden=None, rank=None, slot=None):
    n = links.n
    count = links.count
    for j in range(count + 1):
        if hidden is not None:
            hidden[j] = -1
        if rank is not None:
            rank[j] = CAP
    if slot is not None:
        for c in range(CAP + 1):
            slot[c] = -1
    total = moves.shape[1]
    busy = None
    if links.split:
        froms = [moves[0, m] // rows_inst for m in range(total)]
        busy = [
            functools.reduce(jnp.bitwise_or, [(f == k).astype(jnp.int32) for f in froms]) for k in range(n)
        ]

    def step(m, seen):
        cache_slot = moves[0, m]
        hidden_slot = moves[1, m]
        from_inst = cache_slot // rows_inst
        to_inst = hidden_slot // rows_inst
        index = links.index(busy, from_inst, to_inst)
        if hidden is not None:
            hidden[jnp.where(to_inst == me, index, count)] = lax.rem(hidden_slot, rows_inst)
        mine = from_inst == me
        if rank is not None:
            rank[jnp.where(mine, index, count)] = seen
        if slot is not None:
            slot[jnp.where(mine, seen, CAP)] = lax.rem(cache_slot, rows_inst)
        return jnp.where(mine, seen + 1, seen)

    if links.split:
        seen = jnp.int32(0)
        for m in range(total):
            seen = step(m, seen)
    else:
        lax.fori_loop(0, total, step, jnp.int32(0))
    return busy


def pack_kernel(links, moves_hbm, q_hbm, kv_hbm, *refs):
    outs = refs[: links.count]
    branch, hidden, moves, q, kv, sems = refs[links.count :]
    copies = [
        pltpu.make_async_copy(moves_hbm, moves, sems.at[0]),
        pltpu.make_async_copy(q_hbm, q, sems.at[1]),
        pltpu.make_async_copy(kv_hbm, kv, sems.at[2]),
    ]
    for c in copies:
        c.start()
    rows_inst, heads, _ = q.shape
    me = lax.axis_index("inst")
    copies[0].wait()
    busy = find_moves(links, moves, rows_inst, me, hidden=hidden)
    branch[0] = links.branch(busy) if links.split else 0
    copies[1].wait()
    copies[2].wait()
    for j, out in enumerate(outs):
        row = jnp.maximum(hidden[j], 0)
        out[0:heads, :] = q[row]
        out[heads:, :] = kv[row]


def set_row(at, rows, fresh, qbd, fk, fv, groups):
    heads, hd = rows.shape
    per = heads // groups
    zero = jnp.zeros((per, hd), jnp.bfloat16)
    for g in range(groups):
        for k in range(groups):
            qbd[at, g * per : (g + 1) * per, k * hd : (k + 1) * hd] = (
                rows[g * per : (g + 1) * per] if k == g else zero
            )
    if fk is None:
        return
    fresh = fresh.astype(jnp.float32)
    token = lax.broadcasted_iota(jnp.int32, (16, hd), 0)
    for plane, ref in enumerate((fk, fv)):
        for g in range(groups):
            block = jnp.zeros((16, hd), jnp.float32)
            for u in range(fresh.shape[0] // (2 * groups)):
                line = (u * groups + g) * 2 + plane
                block = jnp.where(token == u, fresh[line : line + 1], block)
            ref[at, 0:16, g * hd : (g + 1) * hd] = block.astype(jnp.bfloat16)


def attend_list(rows, ahead, chunk, steps, lists, count, buf, qbd, fk, fv, scores, new, part_max, top, part_sum, acc):
    page, owner, limit = lists
    _, heads, columns = qbd.shape
    hd = acc.shape[2]
    groups = columns // hd
    per = heads // groups
    block = buf.shape[2]
    factor = math.log2(math.e) / math.sqrt(hd)
    loops = lax.div(count - ahead + (chunk - 1), jnp.int32(chunk))
    keys_of = (((1,), (1,)), ((), ()))
    values_of = (((1,), (0,)), ((), ()))
    lane = lax.broadcasted_iota(jnp.int32, (heads, block), 1)
    token = lax.broadcasted_iota(jnp.int32, (heads, hd), 1)
    seen = token <= lax.broadcasted_iota(jnp.int32, (heads, hd), 0) % steps

    def diagonal(o):
        return jnp.concatenate(
            [o[g * per : (g + 1) * per, g * hd : (g + 1) * hd] for g in range(groups)], axis=0
        )

    def first(k):
        r = owner[k]
        s = lax.dot_general(qbd[r], buf[page[k], 0], keys_of, preferred_element_type=jnp.float32)
        s = jnp.where(lane < limit[k], s, NEG)
        scores[k] = s
        m = s[:, 0:hd]
        for c in range(1, block // hd):
            m = jnp.maximum(m, s[:, c * hd : (c + 1) * hd])
        part_max[r] = jnp.maximum(part_max[r], m)

    def second(k):
        r = owner[k]
        m = top[r]
        pieces = []
        total = jnp.zeros((heads, hd), jnp.float32)
        for c in range(block // hd):
            e = jnp.exp2((scores[k, :, c * hd : (c + 1) * hd] - m) * factor)
            total = total + e
            pieces.append(e.astype(jnp.bfloat16))
        o = lax.dot_general(
            jnp.concatenate(pieces, axis=1), buf[page[k], 1], values_of, preferred_element_type=jnp.float32
        )
        part_sum[r] = part_sum[r] + total
        acc[r] = acc[r] + diagonal(o)

    def others(do):
        def step(i, carry):
            for j in range(chunk):
                do(ahead + i * chunk + j)
            return carry

        lax.fori_loop(0, loops, step, 0)

    for r in range(rows):
        s = lax.dot_general(qbd[r], fk[r], keys_of, preferred_element_type=jnp.float32)
        s = jnp.where(seen, s, NEG)
        new[r] = s
        part_max[r] = s
    part_max[rows] = jnp.zeros((heads, hd), jnp.float32)
    for j in range(ahead):
        first(j)
    others(first)

    top[rows] = jnp.zeros((heads, hd), jnp.float32)
    part_sum[rows] = jnp.zeros((heads, hd), jnp.float32)
    acc[rows] = jnp.zeros((heads, hd), jnp.float32)
    for r in range(rows):
        m = jnp.broadcast_to(jnp.max(part_max[r], axis=1, keepdims=True), (heads, hd))
        top[r] = m
        e = jnp.exp2((new[r] - m) * factor)
        part_sum[r] = e
        acc[r] = diagonal(
            lax.dot_general(e.astype(jnp.bfloat16), fv[r], values_of, preferred_element_type=jnp.float32)
        )
    for j in range(ahead):
        second(j)
    others(second)
    for r in range(rows):
        acc[r] = acc[r] / jnp.sum(part_sum[r], axis=1, keepdims=True)


def list_kernel(links, chunk, far_chunk, fetches, moves_hbm, page_hbm, length_hbm, q_hbm, kv_hbm, pool, *refs):
    (
        buf, qbd, fk, fv, hidden, rank, slot,
        page, owner, limit, counts, far_page, far_owner, far_limit,
        moves, page_table, lengths, q, kv, small_sems, sems,
    ) = refs
    rows_inst, heads, hd = q.shape
    slots, _, block, columns = pool.shape
    groups = columns // hd
    me = lax.axis_index("inst")

    small = [
        pltpu.make_async_copy(src, dst, small_sems.at[i])
        for i, (src, dst) in enumerate(
            [(moves_hbm, moves), (page_hbm, page_table), (length_hbm, lengths), (q_hbm, q), (kv_hbm, kv)]
        )
    ]
    for c in small:
        c.start()

    part = slots // fetches

    def fetch(k, plane):
        at = pl.ds(k * part, part)
        return pltpu.make_async_copy(pool.at[at, plane], buf.at[at, plane], sems.at[k, plane])

    for plane in range(2):
        for k in range(fetches):
            fetch(k, plane).start()

    fk[...] = jnp.zeros(fk.shape, fk.dtype)
    fv[...] = jnp.zeros(fv.shape, fv.dtype)
    for c in small:
        c.wait()
    find_moves(links, moves, rows_inst, me, hidden=hidden, rank=rank, slot=slot)

    def row(r, counts):
        near, far = counts
        length = lengths[r]
        which = jnp.int32(CAP)
        for c in range(CAP):
            which = jnp.where(slot[c] == r, c, which)
        moved = which < CAP

        def one(b, counts):
            near, far = counts
            number = page_table[r, b]
            left = length - b * block
            at = jnp.where(moved, slots + far_chunk, near)
            page[at] = number
            owner[at] = r
            limit[at] = left
            at = jnp.where(moved, far, slots + far_chunk)
            far_page[at] = number
            far_owner[at] = which
            far_limit[at] = left
            return jnp.where(moved, near, near + 1), jnp.where(moved, far + 1, far)

        return lax.fori_loop(0, lax.div(length + (block - 1), jnp.int32(block)), one, (near, far))

    near, far = lax.fori_loop(0, rows_inst, row, (jnp.int32(0), jnp.int32(0)))
    counts[0] = near
    counts[1] = far
    for j in range(chunk):
        page[near + j] = 0
        owner[near + j] = rows_inst
        limit[near + j] = 0
    for j in range(far_chunk):
        far_page[far + j] = 0
        far_owner[far + j] = CAP
        far_limit[far + j] = 0

    for r in range(rows_inst):
        set_row(r, q[r], kv[r], qbd, fk, fv, groups)
    set_row(rows_inst, q[0], None, qbd, None, None, groups)

    for plane in range(2):
        for k in range(fetches):
            fetch(k, plane).wait()


def stay_kernel(chunk, steps, slot, page, owner, limit, counts, buf, qbd, fk, fv, order, local, *work):
    rows_inst = local.shape[0]
    attend_list(rows_inst, chunk, chunk, steps, (page, owner, limit), counts[0], buf, qbd, fk, fv, *work)
    acc = work[-1]
    for r in range(rows_inst):
        vacant = functools.reduce(jnp.logical_or, [slot[c] == r for c in range(CAP)])
        local[r] = jnp.where(vacant, 0.0, acc[r]).astype(jnp.bfloat16)


def moved_kernel(links, ahead, chunk, steps, rank, far_page, far_owner, far_limit, counts, buf, *refs):
    recv, back = refs[: links.count], refs[links.count : 2 * links.count]
    qbd, fk, fv, *work = refs[2 * links.count :]
    acc = work[-1]
    heads = qbd.shape[1]
    groups = qbd.shape[2] // acc.shape[2]
    count = counts[1]

    @pl.when(count > 0)
    def _():
        fk[:, 16:, :] = jnp.zeros((CAP, fk.shape[1] - 16, fk.shape[2]), fk.dtype)
        fv[:, 16:, :] = jnp.zeros((CAP, fv.shape[1] - 16, fv.shape[2]), fv.dtype)
        for j in range(links.count):

            def put(j=j):
                set_row(rank[j], recv[j][0:heads, :], recv[j][heads:, :], qbd, fk, fv, groups)

            if links.count == CAP:
                put()
            else:
                pl.when(rank[j] < CAP)(put)
        attend_list(
            CAP, ahead, chunk, steps, (far_page, far_owner, far_limit), count,
            buf, qbd, fk, fv, *work,
        )
        for j in range(links.count):
            back[j][...] = acc[rank[j]].astype(jnp.bfloat16)


def place_kernel(links, hidden, local, *refs):
    back, (out, staged, sem) = refs[: links.count], refs[links.count :]
    staged[...] = local[...]
    for j, ref in enumerate(back):

        def put(ref=ref, j=j):
            staged[hidden[j]] = ref[...]

        pl.when(hidden[j] >= 0)(put)

    write = pltpu.make_async_copy(staged, out, sem)
    write.start()
    write.wait()


def body(kv_pool, page_table, lengths, queries, new_kv, moves):
    links = Links(lax.axis_size("inst"))
    rows_inst, steps, width = queries.shape
    slots, _, block, columns = kv_pool.shape
    groups = columns // HD
    heads_all = width // HD
    heads = steps * heads_all
    fresh_rows = steps * groups * 2
    bf16 = jnp.bfloat16
    f32 = jnp.float32
    i32 = jnp.int32
    q = queries.reshape(rows_inst, steps, heads_all, HD).transpose(0, 2, 1, 3).reshape(rows_inst, heads, HD)
    kv = (
        new_kv.reshape(rows_inst, steps, 2, groups, HD)
        .transpose(0, 1, 3, 2, 4)
        .reshape(rows_inst, fresh_rows, HD)
    )
    smem = pl.BlockSpec(memory_space=SMEM)
    vmem = pl.BlockSpec(memory_space=VMEM)
    hbm = pl.BlockSpec(memory_space=HBM)
    in_hbm = lambda x: pltpu.with_memory_space_constraint(x, HBM)
    move_cols = moves.T
    count = links.count
    chunk = 4
    far_chunk = 6
    fetches = math.gcd(slots, 4)
    mib = 1024 * 1024

    *packed, branch = pl.pallas_call(
        functools.partial(pack_kernel, links),
        out_shape=[jax.ShapeDtypeStruct((heads + fresh_rows, HD), bf16)] * count
        + [SMEM((1,), i32)],
        in_specs=[hbm, hbm, hbm],
        out_specs=[vmem] * count + [smem],
        scratch_shapes=[
            SMEM((count + 1,), i32),
            SMEM(move_cols.shape, i32),
            VMEM(q.shape, bf16),
            VMEM(kv.shape, bf16),
            pltpu.SemaphoreType.DMA((3,)),
        ],
        compiler_params=pltpu.CompilerParams(vmem_limit_bytes=4 * mib),
        name="pack",
    )(in_hbm(move_cols), in_hbm(q), in_hbm(kv))

    def rows_state(rows):
        return [
            VMEM((rows + 1, heads, columns), bf16),
            VMEM((rows, HD, columns), bf16),
            VMEM((rows, HD, columns), bf16),
        ]

    def work_state(rows):
        return [
            VMEM((slots + far_chunk, heads, block), f32),
            VMEM((rows, heads, HD), f32),
        ] + [VMEM((rows + 1, heads, HD), f32)] * 4

    anyspace = pl.BlockSpec(memory_space=pl.ANY)
    blocks = SMEM((slots + far_chunk + 1,), i32)
    staged = VMEM((rows_inst, heads, HD), bf16)

    def rest(which, kv_pool, page_table, lengths, q, kv, move_cols, *packed):
        received = [lax.ppermute(x, "inst", links.forward(which, j)) for j, x in enumerate(packed)]
        (
            buf, qbd, fk, fv, hidden, rank, slot,
            page, owner, limit, counts, far_page, far_owner, far_limit,
        ) = pl.pallas_call(
            functools.partial(list_kernel, links, chunk, far_chunk, fetches),
            out_shape=[VMEM(kv_pool.shape, bf16)]
            + rows_state(rows_inst)
            + [SMEM((count + 1,), i32), SMEM((count + 1,), i32), SMEM((CAP + 1,), i32)]
            + [blocks, blocks, blocks, SMEM((2,), i32), blocks, blocks, blocks],
            in_specs=[hbm] * 6,
            out_specs=[vmem] * 4 + [smem] * 10,
            scratch_shapes=[
                SMEM(move_cols.shape, i32),
                SMEM(page_table.shape, i32),
                SMEM(lengths.shape, i32),
                VMEM(q.shape, bf16),
                VMEM(kv.shape, bf16),
                pltpu.SemaphoreType.DMA((5,)),
                pltpu.SemaphoreType.DMA((fetches, 2)),
            ],
            compiler_params=pltpu.CompilerParams(vmem_limit_bytes=16 * mib),
            cost_estimate=pl.CostEstimate(flops=2**27, bytes_accessed=2**23, transcendentals=2**18),
            name="list",
        )(*map(in_hbm, (move_cols, page_table, lengths, q, kv, kv_pool)))
        back = pl.pallas_call(
            functools.partial(moved_kernel, links, chunk, far_chunk, steps),
            out_shape=[jax.ShapeDtypeStruct((heads, HD), bf16)] * count,
            in_specs=[smem] * 5 + [vmem] + [vmem] * count,
            out_specs=[vmem] * count,
            scratch_shapes=rows_state(CAP) + work_state(CAP),
            compiler_params=pltpu.CompilerParams(vmem_limit_bytes=16 * mib),
            name="moved",
        )(rank, far_page, far_owner, far_limit, counts, buf, *received)
        returned = [lax.ppermute(x, "inst", links.backward(which, j)) for j, x in enumerate(back)]
        local = pl.pallas_call(
            functools.partial(stay_kernel, chunk, steps),
            out_shape=staged,
            in_specs=[smem] * 5 + [vmem] * 4 + [anyspace],
            out_specs=vmem,
            scratch_shapes=work_state(rows_inst),
            compiler_params=pltpu.CompilerParams(vmem_limit_bytes=16 * mib),
            cost_estimate=pl.CostEstimate(flops=2**27, bytes_accessed=2**23, transcendentals=2**18),
            name="stay",
        )(slot, page, owner, limit, counts, buf, qbd, fk, fv, back[0])
        out = pl.pallas_call(
            functools.partial(place_kernel, links),
            out_shape=HBM((rows_inst, heads, HD), bf16),
            in_specs=[smem, vmem] + [vmem] * count,
            out_specs=hbm,
            scratch_shapes=[staged, pltpu.SemaphoreType.DMA],
            compiler_params=pltpu.CompilerParams(vmem_limit_bytes=4 * mib),
            name="place",
        )(hidden, local, *returned)
        out = out.reshape(rows_inst, heads_all, steps, HD).transpose(0, 2, 1, 3)
        return out.reshape(rows_inst, steps, width)

    operands = (kv_pool, page_table, lengths, q, kv, move_cols, *packed)
    if links.split:
        return lax.switch(
            branch[0], [functools.partial(rest, k) for k in range(len(links.halves))], *operands
        )
    return rest(0, *operands)


def solution(mesh):
    placed = (
        P(("groups", "inst"), None, None, "tp"),
        P(("groups", "inst"), None),
        P(("groups", "inst")),
        P(("groups", "inst"), None, "tp"),
        P(("groups", "inst"), None, None, "tp"),
        P("groups", None),
    )
    return jax.shard_map(
        body,
        mesh=mesh,
        in_specs=placed,
        out_specs=P(("groups", "inst"), None, "tp"),
        check_vma=False,
    )
```

```python
import functools
import itertools
import math

import jax
import jax.numpy as jnp
from jax import lax
from jax.experimental import pallas as pl
from jax.experimental.pallas import tpu as pltpu
from jax.sharding import PartitionSpec as P

HD = 128
CAP = 2
NEG = -1e30
MAX_SPLITS = 3
SMEM = pltpu.SMEM
VMEM = pltpu.VMEM
HBM = pltpu.HBM


class Links:
    def __init__(self, n):
        self.n = n
        half = n // 2
        self.halves = []
        if n % 2 == 0 and math.comb(n, half) <= 2 * MAX_SPLITS:
            self.halves = [c for c in itertools.combinations(range(n), half) if 0 in c]
        self.split = bool(self.halves)
        self.count = half if self.split else n - 1

    def index(self, busy, a, b):
        n = self.n
        if self.split:
            half = n // 2
            rank_a = sum(jnp.where(k < a, busy[k], 0) for k in range(n))
            rank_b = sum(jnp.where(k < b, 1 - busy[k], 0) for k in range(n))
            shift = jnp.where(busy[0] == 1, rank_b - rank_a, rank_a - rank_b)
            return half - 1 - lax.rem(shift + half, half)
        if n & (n - 1) == 0:
            return (a ^ b) - 1
        return lax.rem(a - b + n, n) - 1

    def branch(self, busy):
        mask = sum(jnp.where(busy[k] == busy[0], 1 << k, 0) for k in range(self.n))
        return sum(
            jnp.where(mask == sum(1 << i for i in half), k, 0) for k, half in enumerate(self.halves)
        )

    def forward(self, which, j):
        n = self.n
        if self.split:
            half = self.halves[which]
            other = [i for i in range(n) if i not in half]
            shift = self.count - 1 - j
            pairs = [(a, other[(k + shift) % len(other)]) for k, a in enumerate(half)]
            return sorted(pairs + [(b, a) for a, b in pairs])
        if n & (n - 1) == 0:
            return [(i, i ^ (j + 1)) for i in range(n)]
        return [(i, (i + j + 1) % n) for i in range(n)]

    def backward(self, which, j):
        return [(b, a) for a, b in self.forward(which, j)]


def find_moves(links, moves, rows_inst, me, hidden=None, rank=None, slot=None):
    n = links.n
    count = links.count
    for j in range(count + 1):
        if hidden is not None:
            hidden[j] = -1
        if rank is not None:
            rank[j] = CAP
    if slot is not None:
        for c in range(CAP + 1):
            slot[c] = -1
    total = moves.shape[1]
    busy = None
    if links.split:
        froms = [moves[0, m] // rows_inst for m in range(total)]
        busy = [
            functools.reduce(jnp.bitwise_or, [(f == k).astype(jnp.int32) for f in froms]) for k in range(n)
        ]

    def step(m, seen):
        cache_slot = moves[0, m]
        hidden_slot = moves[1, m]
        from_inst = cache_slot // rows_inst
        to_inst = hidden_slot // rows_inst
        index = links.index(busy, from_inst, to_inst)
        if hidden is not None:
            hidden[jnp.where(to_inst == me, index, count)] = lax.rem(hidden_slot, rows_inst)
        mine = from_inst == me
        if rank is not None:
            rank[jnp.where(mine, index, count)] = seen
        if slot is not None:
            slot[jnp.where(mine, seen, CAP)] = lax.rem(cache_slot, rows_inst)
        return jnp.where(mine, seen + 1, seen)

    if links.split:
        seen = jnp.int32(0)
        for m in range(total):
            seen = step(m, seen)
    else:
        lax.fori_loop(0, total, step, jnp.int32(0))
    return busy


def pack_kernel(links, moves_hbm, q_hbm, kv_hbm, *refs):
    outs = refs[: links.count]
    branch, hidden, moves, q, kv, sems = refs[links.count :]
    copies = [
        pltpu.make_async_copy(moves_hbm, moves, sems.at[0]),
        pltpu.make_async_copy(q_hbm, q, sems.at[1]),
        pltpu.make_async_copy(kv_hbm, kv, sems.at[2]),
    ]
    for c in copies:
        c.start()
    rows_inst, heads, _ = q.shape
    me = lax.axis_index("inst")
    copies[0].wait()
    busy = find_moves(links, moves, rows_inst, me, hidden=hidden)
    branch[0] = links.branch(busy) if links.split else 0
    copies[1].wait()
    copies[2].wait()
    for j, out in enumerate(outs):
        row = jnp.maximum(hidden[j], 0)
        out[0:heads, :] = q[row]
        out[heads:, :] = kv[row]


def set_row(at, rows, fresh, qbd, fk, fv, groups):
    heads, hd = rows.shape
    per = heads // groups
    zero = jnp.zeros((per, hd), jnp.bfloat16)
    for g in range(groups):
        for k in range(groups):
            qbd[at, g * per : (g + 1) * per, k * hd : (k + 1) * hd] = (
                rows[g * per : (g + 1) * per] if k == g else zero
            )
    if fk is None:
        return
    fresh = fresh.astype(jnp.float32)
    token = lax.broadcasted_iota(jnp.int32, (16, hd), 0)
    for plane, ref in enumerate((fk, fv)):
        for g in range(groups):
            block = jnp.zeros((16, hd), jnp.float32)
            for u in range(fresh.shape[0] // (2 * groups)):
                line = (u * groups + g) * 2 + plane
                block = jnp.where(token == u, fresh[line : line + 1], block)
            ref[at, 0:16, g * hd : (g + 1) * hd] = block.astype(jnp.bfloat16)


def attend_list(rows, ahead, chunk, steps, lists, count, wait, buf, qbd, fk, fv, scores, new, part_max, top, part_sum, acc):
    owner, limit = lists
    _, heads, columns = qbd.shape
    hd = acc.shape[2]
    groups = columns // hd
    per = heads // groups
    block = buf.shape[2]
    factor = math.log2(math.e) / math.sqrt(hd)
    loops = lax.div(count - ahead + (chunk - 1), jnp.int32(chunk))
    keys_of = (((1,), (1,)), ((), ()))
    values_of = (((1,), (0,)), ((), ()))
    lane = lax.broadcasted_iota(jnp.int32, (heads, block), 1)
    token = lax.broadcasted_iota(jnp.int32, (heads, hd), 1)
    seen = token <= lax.broadcasted_iota(jnp.int32, (heads, hd), 0) % steps

    def diagonal(o):
        return jnp.concatenate(
            [o[g * per : (g + 1) * per, g * hd : (g + 1) * hd] for g in range(groups)], axis=0
        )

    def first(k):
        r = owner[k]
        s = lax.dot_general(qbd[r], buf[k, 0], keys_of, preferred_element_type=jnp.float32)
        s = jnp.where(lane < limit[k], s, NEG)
        scores[k] = s
        m = s[:, 0:hd]
        for c in range(1, block // hd):
            m = jnp.maximum(m, s[:, c * hd : (c + 1) * hd])
        part_max[r] = jnp.maximum(part_max[r], m)

    def second(k):
        r = owner[k]
        m = top[r]
        pieces = []
        total = jnp.zeros((heads, hd), jnp.float32)
        for c in range(block // hd):
            e = jnp.exp2((scores[k, :, c * hd : (c + 1) * hd] - m) * factor)
            total = total + e
            pieces.append(e.astype(jnp.bfloat16))
        o = lax.dot_general(
            jnp.concatenate(pieces, axis=1), buf[k, 1], values_of, preferred_element_type=jnp.float32
        )
        part_sum[r] = part_sum[r] + total
        acc[r] = acc[r] + diagonal(o)

    def several(do, plane, at, number):
        for j in range(number):
            wait(at + j, plane)
        for j in range(number):
            do(at + j)

    def others(do, plane):
        def step(i, carry):
            several(do, plane, ahead + i * chunk, chunk)
            return carry

        lax.fori_loop(0, loops, step, 0)

    for r in range(rows):
        s = lax.dot_general(qbd[r], fk[r], keys_of, preferred_element_type=jnp.float32)
        s = jnp.where(seen, s, NEG)
        new[r] = s
        part_max[r] = s
    part_max[rows] = jnp.zeros((heads, hd), jnp.float32)
    several(first, 0, 0, ahead)
    others(first, 0)

    top[rows] = jnp.zeros((heads, hd), jnp.float32)
    part_sum[rows] = jnp.zeros((heads, hd), jnp.float32)
    acc[rows] = jnp.zeros((heads, hd), jnp.float32)
    for r in range(rows):
        m = jnp.broadcast_to(jnp.max(part_max[r], axis=1, keepdims=True), (heads, hd))
        top[r] = m
        e = jnp.exp2((new[r] - m) * factor)
        part_sum[r] = e
        acc[r] = diagonal(
            lax.dot_general(e.astype(jnp.bfloat16), fv[r], values_of, preferred_element_type=jnp.float32)
        )
    several(second, 1, 0, ahead)
    others(second, 1)
    for r in range(rows):
        acc[r] = acc[r] / jnp.sum(part_sum[r], axis=1, keepdims=True)


def list_kernel(links, chunk, far_chunk, moves_hbm, page_hbm, length_hbm, q_hbm, kv_hbm, pool, *refs):
    (
        buf, qbd, fk, fv, hidden, rank, slot,
        page, owner, limit, counts, far_owner, far_limit,
        moves, page_table, lengths, q, kv, small_sems, sems,
    ) = refs
    rows_inst, heads, hd = q.shape
    slots, _, block, columns = pool.shape
    groups = columns // hd
    me = lax.axis_index("inst")

    small = [
        pltpu.make_async_copy(src, dst, small_sems.at[i])
        for i, (src, dst) in enumerate(
            [(moves_hbm, moves), (page_hbm, page_table), (length_hbm, lengths), (q_hbm, q), (kv_hbm, kv)]
        )
    ]
    for c in small:
        c.start()

    def fetch(number, k):
        return pltpu.make_async_copy(pool.at[number], buf.at[k], sems.at[k])

    fk[...] = jnp.zeros(fk.shape, fk.dtype)
    fv[...] = jnp.zeros(fv.shape, fv.dtype)
    for c in small[:3]:
        c.wait()
    find_moves(links, moves, rows_inst, me, hidden=hidden, rank=rank, slot=slot)

    def row(r, counts):
        near, far = counts
        length = lengths[r]
        which = jnp.int32(CAP)
        for c in range(CAP):
            which = jnp.where(slot[c] == r, c, which)
        moved = which < CAP

        def one(b, counts):
            near, far = counts
            number = page_table[r, b]
            left = length - b * block
            at = jnp.where(moved, slots + far_chunk, near)
            page[at] = number
            owner[at] = r
            limit[at] = left
            at = jnp.where(moved, far, slots + far_chunk)
            far_owner[at] = which
            far_limit[at] = left

            @pl.when(moved)
            def _():
                fetch(number, far).start()

            return jnp.where(moved, near, near + 1), jnp.where(moved, far + 1, far)

        return lax.fori_loop(0, lax.div(length + (block - 1), jnp.int32(block)), one, (near, far))

    near, far = lax.fori_loop(0, rows_inst, row, (jnp.int32(0), jnp.int32(0)))
    counts[0] = near
    counts[1] = far
    for j in range(chunk):
        owner[near + j] = rows_inst
        limit[near + j] = 0
    for j in range(far_chunk):
        far_owner[far + j] = CAP
        far_limit[far + j] = 0

    for c in small[3:]:
        c.wait()
    for r in range(rows_inst):
        set_row(r, q[r], kv[r], qbd, fk, fv, groups)
    set_row(rows_inst, q[0], None, qbd, None, None, groups)


    def arrived(k, carry):
        fetch(0, k).wait()
        return carry

    lax.fori_loop(0, far, arrived, 0)


def stay_kernel(chunk, steps, slot, page, owner, limit, counts, pool, qbd, fk, fv, order, local, buf, sems, *work):
    rows_inst = local.shape[0]
    count = counts[0]

    def fetch(number, k, plane):
        return pltpu.make_async_copy(pool.at[number, plane], buf.at[k, plane], sems.at[k, plane])

    for plane in range(2):

        def start(k, carry, plane=plane):
            fetch(page[k], k, plane).start()
            return carry

        lax.fori_loop(0, count, start, 0)

    def wait(k, plane):
        @pl.when(k < count)
        def _():
            fetch(0, k, plane).wait()

    attend_list(rows_inst, chunk, chunk, steps, (owner, limit), count, wait, buf, qbd, fk, fv, *work)
    acc = work[-1]
    for r in range(rows_inst):
        vacant = functools.reduce(jnp.logical_or, [slot[c] == r for c in range(CAP)])
        local[r] = jnp.where(vacant, 0.0, acc[r]).astype(jnp.bfloat16)


def moved_kernel(links, ahead, chunk, steps, rank, far_owner, far_limit, counts, buf, *refs):
    recv, back = refs[: links.count], refs[links.count : 2 * links.count]
    qbd, fk, fv, *work = refs[2 * links.count :]
    acc = work[-1]
    heads = qbd.shape[1]
    groups = qbd.shape[2] // acc.shape[2]
    count = counts[1]

    @pl.when(count > 0)
    def _():
        fk[:, 16:, :] = jnp.zeros((CAP, fk.shape[1] - 16, fk.shape[2]), fk.dtype)
        fv[:, 16:, :] = jnp.zeros((CAP, fv.shape[1] - 16, fv.shape[2]), fv.dtype)
        for j in range(links.count):

            def put(j=j):
                set_row(rank[j], recv[j][0:heads, :], recv[j][heads:, :], qbd, fk, fv, groups)

            if links.count == CAP:
                put()
            else:
                pl.when(rank[j] < CAP)(put)
        attend_list(
            CAP, ahead, chunk, steps, (far_owner, far_limit), count, lambda k, plane: None,
            buf, qbd, fk, fv, *work,
        )
        for j in range(links.count):
            back[j][...] = acc[rank[j]].astype(jnp.bfloat16)


def place_kernel(links, hidden, local, *refs):
    back, (out, staged, sem) = refs[: links.count], refs[links.count :]
    staged[...] = local[...]
    for j, ref in enumerate(back):

        def put(ref=ref, j=j):
            staged[hidden[j]] = ref[...]

        pl.when(hidden[j] >= 0)(put)

    write = pltpu.make_async_copy(staged, out, sem)
    write.start()
    write.wait()


def body(kv_pool, page_table, lengths, queries, new_kv, moves):
    links = Links(lax.axis_size("inst"))
    rows_inst, steps, width = queries.shape
    slots, _, block, columns = kv_pool.shape
    groups = columns // HD
    heads_all = width // HD
    heads = steps * heads_all
    fresh_rows = steps * groups * 2
    bf16 = jnp.bfloat16
    f32 = jnp.float32
    i32 = jnp.int32
    q = queries.reshape(rows_inst, steps, heads_all, HD).transpose(0, 2, 1, 3).reshape(rows_inst, heads, HD)
    kv = (
        new_kv.reshape(rows_inst, steps, 2, groups, HD)
        .transpose(0, 1, 3, 2, 4)
        .reshape(rows_inst, fresh_rows, HD)
    )
    smem = pl.BlockSpec(memory_space=SMEM)
    vmem = pl.BlockSpec(memory_space=VMEM)
    hbm = pl.BlockSpec(memory_space=HBM)
    in_hbm = lambda x: pltpu.with_memory_space_constraint(x, HBM)
    move_cols = moves.T
    count = links.count
    chunk = 4
    far_chunk = 6
    mib = 1024 * 1024

    *packed, branch = pl.pallas_call(
        functools.partial(pack_kernel, links),
        out_shape=[jax.ShapeDtypeStruct((heads + fresh_rows, HD), bf16)] * count
        + [SMEM((1,), i32)],
        in_specs=[hbm, hbm, hbm],
        out_specs=[vmem] * count + [smem],
        scratch_shapes=[
            SMEM((count + 1,), i32),
            SMEM(move_cols.shape, i32),
            VMEM(q.shape, bf16),
            VMEM(kv.shape, bf16),
            pltpu.SemaphoreType.DMA((3,)),
        ],
        compiler_params=pltpu.CompilerParams(vmem_limit_bytes=4 * mib),
        name="pack",
    )(in_hbm(move_cols), in_hbm(q), in_hbm(kv))

    def rows_state(rows):
        return [
            VMEM((rows + 1, heads, columns), bf16),
            VMEM((rows, HD, columns), bf16),
            VMEM((rows, HD, columns), bf16),
        ]

    def work_state(rows):
        return [
            VMEM((slots + far_chunk, heads, block), f32),
            VMEM((rows, heads, HD), f32),
        ] + [VMEM((rows + 1, heads, HD), f32)] * 4

    anyspace = pl.BlockSpec(memory_space=pl.ANY)
    blocks = SMEM((slots + far_chunk + 1,), i32)
    pool_copy = VMEM((slots + far_chunk,) + kv_pool.shape[1:], bf16)
    staged = VMEM((rows_inst, heads, HD), bf16)

    def rest(which, kv_pool, page_table, lengths, q, kv, move_cols, *packed):
        received = [lax.ppermute(x, "inst", links.forward(which, j)) for j, x in enumerate(packed)]
        (
            buf, qbd, fk, fv, hidden, rank, slot,
            page, owner, limit, counts, far_owner, far_limit,
        ) = pl.pallas_call(
            functools.partial(list_kernel, links, chunk, far_chunk),
            out_shape=[pool_copy]
            + rows_state(rows_inst)
            + [SMEM((count + 1,), i32), SMEM((count + 1,), i32), SMEM((CAP + 1,), i32)]
            + [blocks, blocks, blocks, SMEM((2,), i32), blocks, blocks],
            in_specs=[hbm] * 6,
            out_specs=[vmem] * 4 + [smem] * 9,
            scratch_shapes=[
                SMEM(move_cols.shape, i32),
                SMEM(page_table.shape, i32),
                SMEM(lengths.shape, i32),
                VMEM(q.shape, bf16),
                VMEM(kv.shape, bf16),
                pltpu.SemaphoreType.DMA((5,)),
                pltpu.SemaphoreType.DMA((slots,)),
            ],
            compiler_params=pltpu.CompilerParams(vmem_limit_bytes=16 * mib),
            cost_estimate=pl.CostEstimate(flops=2**27, bytes_accessed=2**23, transcendentals=2**18),
            name="list",
        )(*map(in_hbm, (move_cols, page_table, lengths, q, kv, kv_pool)))
        back = pl.pallas_call(
            functools.partial(moved_kernel, links, chunk, far_chunk, steps),
            out_shape=[jax.ShapeDtypeStruct((heads, HD), bf16)] * count,
            in_specs=[smem] * 4 + [vmem] + [vmem] * count,
            out_specs=[vmem] * count,
            scratch_shapes=rows_state(CAP) + work_state(CAP),
            compiler_params=pltpu.CompilerParams(vmem_limit_bytes=16 * mib),
            name="moved",
        )(rank, far_owner, far_limit, counts, buf, *received)
        returned = [lax.ppermute(x, "inst", links.backward(which, j)) for j, x in enumerate(back)]
        local = pl.pallas_call(
            functools.partial(stay_kernel, chunk, steps),
            out_shape=staged,
            in_specs=[smem] * 5 + [hbm] + [vmem] * 3 + [anyspace],
            out_specs=vmem,
            scratch_shapes=[pool_copy, pltpu.SemaphoreType.DMA((slots, 2))] + work_state(rows_inst),
            compiler_params=pltpu.CompilerParams(vmem_limit_bytes=16 * mib),
            cost_estimate=pl.CostEstimate(flops=2**27, bytes_accessed=2**23, transcendentals=2**18),
            name="stay",
        )(slot, page, owner, limit, counts, in_hbm(kv_pool), qbd, fk, fv, back[0])
        out = pl.pallas_call(
            functools.partial(place_kernel, links),
            out_shape=HBM((rows_inst, heads, HD), bf16),
            in_specs=[smem, vmem] + [vmem] * count,
            out_specs=hbm,
            scratch_shapes=[staged, pltpu.SemaphoreType.DMA],
            compiler_params=pltpu.CompilerParams(vmem_limit_bytes=4 * mib),
            name="place",
        )(hidden, local, *returned)
        out = out.reshape(rows_inst, heads_all, steps, HD).transpose(0, 2, 1, 3)
        return out.reshape(rows_inst, steps, width)

    operands = (kv_pool, page_table, lengths, q, kv, move_cols, *packed)
    if links.split:
        return lax.switch(
            branch[0], [functools.partial(rest, k) for k in range(len(links.halves))], *operands
        )
    return rest(0, *operands)


def solution(mesh):
    placed = (
        P(("groups", "inst"), None, None, "tp"),
        P(("groups", "inst"), None),
        P(("groups", "inst")),
        P(("groups", "inst"), None, "tp"),
        P(("groups", "inst"), None, None, "tp"),
        P("groups", None),
    )
    return jax.shard_map(
        body,
        mesh=mesh,
        in_specs=placed,
        out_specs=P(("groups", "inst"), None, "tp"),
        check_vma=False,
    )
```

```python
import functools
import itertools
import math

import jax
import jax.numpy as jnp
from jax import lax
from jax.experimental import pallas as pl
from jax.experimental.pallas import tpu as pltpu
from jax.sharding import PartitionSpec as P

HD = 128
CAP = 2
NEG = -1e30
MAX_SPLITS = 3
SMEM = pltpu.SMEM
VMEM = pltpu.VMEM
HBM = pltpu.HBM


class Links:
    def __init__(self, n):
        self.n = n
        half = n // 2
        self.halves = []
        if n % 2 == 0 and math.comb(n, half) <= 2 * MAX_SPLITS:
            self.halves = [c for c in itertools.combinations(range(n), half) if 0 in c]
        self.split = bool(self.halves)
        self.count = half if self.split else n - 1

    def index(self, busy, a, b):
        n = self.n
        if self.split:
            half = n // 2
            rank_a = sum(jnp.where(k < a, busy[k], 0) for k in range(n))
            rank_b = sum(jnp.where(k < b, 1 - busy[k], 0) for k in range(n))
            shift = jnp.where(busy[0] == 1, rank_b - rank_a, rank_a - rank_b)
            return half - 1 - lax.rem(shift + half, half)
        if n & (n - 1) == 0:
            return (a ^ b) - 1
        return lax.rem(a - b + n, n) - 1

    def branch(self, busy):
        mask = sum(jnp.where(busy[k] == busy[0], 1 << k, 0) for k in range(self.n))
        return sum(
            jnp.where(mask == sum(1 << i for i in half), k, 0) for k, half in enumerate(self.halves)
        )

    def forward(self, which, j):
        n = self.n
        if self.split:
            half = self.halves[which]
            other = [i for i in range(n) if i not in half]
            shift = self.count - 1 - j
            pairs = [(a, other[(k + shift) % len(other)]) for k, a in enumerate(half)]
            return sorted(pairs + [(b, a) for a, b in pairs])
        if n & (n - 1) == 0:
            return [(i, i ^ (j + 1)) for i in range(n)]
        return [(i, (i + j + 1) % n) for i in range(n)]

    def backward(self, which, j):
        return [(b, a) for a, b in self.forward(which, j)]


def find_moves(links, moves, rows_inst, me, hidden, rank, slot):
    n = links.n
    count = links.count
    for j in range(count + 1):
        hidden[j] = -1
        rank[j] = CAP
    for c in range(CAP + 1):
        slot[c] = -1
    total = moves.shape[1]
    busy = None
    if links.split:
        froms = [moves[0, m] // rows_inst for m in range(total)]
        busy = [
            functools.reduce(jnp.bitwise_or, [(f == k).astype(jnp.int32) for f in froms]) for k in range(n)
        ]

    def step(m, seen):
        cache_slot = moves[0, m]
        hidden_slot = moves[1, m]
        from_inst = cache_slot // rows_inst
        to_inst = hidden_slot // rows_inst
        index = links.index(busy, from_inst, to_inst)
        hidden[jnp.where(to_inst == me, index, count)] = lax.rem(hidden_slot, rows_inst)
        mine = from_inst == me
        rank[jnp.where(mine, index, count)] = seen
        slot[jnp.where(mine, seen, CAP)] = lax.rem(cache_slot, rows_inst)
        return jnp.where(mine, seen + 1, seen)

    if links.split:
        seen = jnp.int32(0)
        for m in range(total):
            seen = step(m, seen)
    else:
        lax.fori_loop(0, total, step, jnp.int32(0))
    return busy


def pack_kernel(links, moves_hbm, page_hbm, length_hbm, q_hbm, kv_hbm, *refs):
    outs = refs[: links.count]
    branch, hidden, rank, slot, page_table, lengths, moves, q, kv, sems = refs[links.count :]
    copies = [
        pltpu.make_async_copy(src, dst, sems.at[i])
        for i, (src, dst) in enumerate(
            [(moves_hbm, moves), (q_hbm, q), (kv_hbm, kv), (page_hbm, page_table), (length_hbm, lengths)]
        )
    ]
    for c in copies:
        c.start()
    rows_inst, heads, _ = q.shape
    me = lax.axis_index("inst")
    copies[0].wait()
    busy = find_moves(links, moves, rows_inst, me, hidden, rank, slot)
    branch[0] = links.branch(busy) if links.split else 0
    copies[1].wait()
    copies[2].wait()
    for j, out in enumerate(outs):
        row = jnp.maximum(hidden[j], 0)
        out[0:heads, :] = q[row]
        out[heads:, :] = kv[row]
    copies[3].wait()
    copies[4].wait()


def set_row(at, rows, fresh, qbd, fk, fv, groups):
    heads, hd = rows.shape
    per = heads // groups
    zero = jnp.zeros((per, hd), jnp.bfloat16)
    for g in range(groups):
        for k in range(groups):
            qbd[at, g * per : (g + 1) * per, k * hd : (k + 1) * hd] = (
                rows[g * per : (g + 1) * per] if k == g else zero
            )
    if fk is None:
        return
    fresh = fresh.astype(jnp.float32)
    token = lax.broadcasted_iota(jnp.int32, (16, hd), 0)
    for plane, ref in enumerate((fk, fv)):
        for g in range(groups):
            block = jnp.zeros((16, hd), jnp.float32)
            for u in range(fresh.shape[0] // (2 * groups)):
                line = (u * groups + g) * 2 + plane
                block = jnp.where(token == u, fresh[line : line + 1], block)
            ref[at, 0:16, g * hd : (g + 1) * hd] = block.astype(jnp.bfloat16)


def attend_list(rows, ahead, chunk, steps, lists, count, wait, buf, qbd, fk, fv, scores, new, part_max, top, part_sum, acc):
    owner, limit = lists
    _, heads, columns = qbd.shape
    hd = acc.shape[2]
    groups = columns // hd
    per = heads // groups
    block = buf.shape[2]
    factor = math.log2(math.e) / math.sqrt(hd)
    loops = lax.div(count - ahead + (chunk - 1), jnp.int32(chunk))
    keys_of = (((1,), (1,)), ((), ()))
    values_of = (((1,), (0,)), ((), ()))
    lane = lax.broadcasted_iota(jnp.int32, (heads, block), 1)
    token = lax.broadcasted_iota(jnp.int32, (heads, hd), 1)
    seen = token <= lax.broadcasted_iota(jnp.int32, (heads, hd), 0) % steps

    def diagonal(o):
        return jnp.concatenate(
            [o[g * per : (g + 1) * per, g * hd : (g + 1) * hd] for g in range(groups)], axis=0
        )

    def first(k):
        r = owner[k]
        s = lax.dot_general(qbd[r], buf[k, 0], keys_of, preferred_element_type=jnp.float32)
        s = jnp.where(lane < limit[k], s, NEG)
        scores[k] = s
        m = s[:, 0:hd]
        for c in range(1, block // hd):
            m = jnp.maximum(m, s[:, c * hd : (c + 1) * hd])
        part_max[r] = jnp.maximum(part_max[r], m)

    def second(k):
        r = owner[k]
        m = top[r]
        pieces = []
        total = jnp.zeros((heads, hd), jnp.float32)
        for c in range(block // hd):
            e = jnp.exp2((scores[k, :, c * hd : (c + 1) * hd] - m) * factor)
            total = total + e
            pieces.append(e.astype(jnp.bfloat16))
        o = lax.dot_general(
            jnp.concatenate(pieces, axis=1), buf[k, 1], values_of, preferred_element_type=jnp.float32
        )
        part_sum[r] = part_sum[r] + total
        acc[r] = acc[r] + diagonal(o)

    def several(do, plane, at, number):
        for j in range(number):
            wait(at + j, plane)
        for j in range(number):
            do(at + j)

    def others(do, plane):
        def step(i, carry):
            several(do, plane, ahead + i * chunk, chunk)
            return carry

        lax.fori_loop(0, loops, step, 0)

    for r in range(rows):
        s = lax.dot_general(qbd[r], fk[r], keys_of, preferred_element_type=jnp.float32)
        s = jnp.where(seen, s, NEG)
        new[r] = s
        part_max[r] = s
    part_max[rows] = jnp.zeros((heads, hd), jnp.float32)
    several(first, 0, 0, ahead)
    others(first, 0)

    top[rows] = jnp.zeros((heads, hd), jnp.float32)
    part_sum[rows] = jnp.zeros((heads, hd), jnp.float32)
    acc[rows] = jnp.zeros((heads, hd), jnp.float32)
    for r in range(rows):
        m = jnp.broadcast_to(jnp.max(part_max[r], axis=1, keepdims=True), (heads, hd))
        top[r] = m
        e = jnp.exp2((new[r] - m) * factor)
        part_sum[r] = e
        acc[r] = diagonal(
            lax.dot_general(e.astype(jnp.bfloat16), fv[r], values_of, preferred_element_type=jnp.float32)
        )
    several(second, 1, 0, ahead)
    others(second, 1)
    for r in range(rows):
        acc[r] = acc[r] / jnp.sum(part_sum[r], axis=1, keepdims=True)


def list_kernel(links, chunk, far_chunk, early, slot, page_table, lengths, q_hbm, kv_hbm, pool, *refs):
    buf, near_buf, qbd, fk, fv, page, owner, limit, counts, far_owner, far_limit, q, kv, small_sems, sems = refs
    rows_inst, heads, hd = q.shape
    slots, _, block, columns = pool.shape
    groups = columns // hd
    small = [
        pltpu.make_async_copy(src, dst, small_sems.at[i])
        for i, (src, dst) in enumerate([(q_hbm, q), (kv_hbm, kv)])
    ]
    for c in small:
        c.start()

    def fetch(number, k):
        return pltpu.make_async_copy(pool.at[number], buf.at[k], sems.at[0, k])

    def fetch_near(number, k):
        return pltpu.make_async_copy(pool.at[number], near_buf.at[k], sems.at[1, k])

    def blocks_of(r):
        return lax.div(lengths[r] + (block - 1), jnp.int32(block))

    far = jnp.int32(0)
    for c in range(CAP):
        r = jnp.maximum(slot[c], 0)

        def one(b, at, r=r, c=c):
            fetch(page_table[r, b], at).start()
            far_owner[at] = c
            far_limit[at] = lengths[r] - b * block
            return at + 1

        far = lax.fori_loop(0, jnp.where(slot[c] >= 0, blocks_of(r), 0), one, far)

    def row(r, near):
        moved = functools.reduce(jnp.logical_or, [slot[c] == r for c in range(CAP)])

        def one(b, at):
            page[at] = page_table[r, b]
            owner[at] = r
            limit[at] = lengths[r] - b * block
            return at + 1

        return lax.fori_loop(0, jnp.where(moved, 0, blocks_of(r)), one, near)

    near = lax.fori_loop(0, rows_inst, row, jnp.int32(0))
    begun = jnp.where(far > 0, jnp.minimum(jnp.maximum(early - far, 0), near), 0)
    counts[0] = near
    counts[1] = far
    counts[2] = begun

    def begin(k, carry):
        fetch_near(page[k], k).start()
        return carry

    lax.fori_loop(0, begun, begin, 0)
    for j in range(chunk):
        owner[near + j] = rows_inst
        limit[near + j] = 0
    for j in range(far_chunk):
        far_owner[far + j] = CAP
        far_limit[far + j] = 0

    fk[...] = jnp.zeros(fk.shape, fk.dtype)
    fv[...] = jnp.zeros(fv.shape, fv.dtype)
    for c in small:
        c.wait()
    for r in range(rows_inst):
        set_row(r, q[r], kv[r], qbd, fk, fv, groups)
    set_row(rows_inst, q[0], None, qbd, None, None, groups)

    def arrived(k, carry):
        fetch(0, k).wait()
        return carry

    def arrived_near(k, carry):
        fetch_near(0, k).wait()
        return carry

    lax.fori_loop(0, far, arrived, 0)
    lax.fori_loop(0, begun, arrived_near, 0)


def stay_kernel(chunk, steps, slot, page, owner, limit, counts, pool, begun_buf, qbd, fk, fv, order, *refs):
    local, buf, sems, *work = refs
    rows_inst = local.shape[0]
    count, begun = counts[0], counts[2]

    def fetch(number, k, plane):
        return pltpu.make_async_copy(pool.at[number, plane], buf.at[k, plane], sems.at[k, plane])

    for plane in range(2):

        def start(k, carry, plane=plane):
            fetch(page[k], k, plane).start()
            return carry

        lax.fori_loop(begun, count, start, 0)

    def wait(k, plane):
        @pl.when((k >= begun) & (k < count))
        def _():
            fetch(0, k, plane).wait()

    attend_list(rows_inst, chunk, chunk, steps, (owner, limit), count, wait, buf, qbd, fk, fv, *work)
    acc = work[-1]
    for r in range(rows_inst):
        vacant = functools.reduce(jnp.logical_or, [slot[c] == r for c in range(CAP)])
        local[r] = jnp.where(vacant, 0.0, acc[r]).astype(jnp.bfloat16)


def moved_kernel(links, ahead, chunk, steps, rank, far_owner, far_limit, counts, buf, *refs):
    recv, back = refs[: links.count], refs[links.count : 2 * links.count]
    qbd, fk, fv, *work = refs[2 * links.count :]
    acc = work[-1]
    heads = qbd.shape[1]
    groups = qbd.shape[2] // acc.shape[2]
    count = counts[1]

    @pl.when(count > 0)
    def _():
        fk[:, 16:, :] = jnp.zeros((CAP, fk.shape[1] - 16, fk.shape[2]), fk.dtype)
        fv[:, 16:, :] = jnp.zeros((CAP, fv.shape[1] - 16, fv.shape[2]), fv.dtype)
        for j in range(links.count):

            def put(j=j):
                set_row(rank[j], recv[j][0:heads, :], recv[j][heads:, :], qbd, fk, fv, groups)

            if links.count == CAP:
                put()
            else:
                pl.when(rank[j] < CAP)(put)
        attend_list(
            CAP, ahead, chunk, steps, (far_owner, far_limit), count, lambda k, plane: None,
            buf, qbd, fk, fv, *work,
        )
        for j in range(links.count):
            back[j][...] = acc[rank[j]].astype(jnp.bfloat16)


def place_kernel(links, hidden, local, *refs):
    back, (out, staged, sem) = refs[: links.count], refs[links.count :]
    staged[...] = local[...]
    for j, ref in enumerate(back):

        def put(ref=ref, j=j):
            staged[hidden[j]] = ref[...]

        pl.when(hidden[j] >= 0)(put)

    write = pltpu.make_async_copy(staged, out, sem)
    write.start()
    write.wait()


def body(kv_pool, page_table, lengths, queries, new_kv, moves):
    links = Links(lax.axis_size("inst"))
    rows_inst, steps, width = queries.shape
    slots, _, block, columns = kv_pool.shape
    groups = columns // HD
    heads_all = width // HD
    heads = steps * heads_all
    fresh_rows = steps * groups * 2
    bf16 = jnp.bfloat16
    f32 = jnp.float32
    i32 = jnp.int32
    q = queries.reshape(rows_inst, steps, heads_all, HD).transpose(0, 2, 1, 3).reshape(rows_inst, heads, HD)
    kv = (
        new_kv.reshape(rows_inst, steps, 2, groups, HD)
        .transpose(0, 1, 3, 2, 4)
        .reshape(rows_inst, fresh_rows, HD)
    )
    smem = pl.BlockSpec(memory_space=SMEM)
    vmem = pl.BlockSpec(memory_space=VMEM)
    hbm = pl.BlockSpec(memory_space=HBM)
    in_hbm = lambda x: pltpu.with_memory_space_constraint(x, HBM)
    move_cols = moves.T
    count = links.count
    chunk = 4
    far_chunk = 6
    mib = 1024 * 1024

    *packed, branch, hidden, rank, slot, pages, sizes = pl.pallas_call(
        functools.partial(pack_kernel, links),
        out_shape=[jax.ShapeDtypeStruct((heads + fresh_rows, HD), bf16)] * count
        + [SMEM((1,), i32), SMEM((count + 1,), i32), SMEM((count + 1,), i32), SMEM((CAP + 1,), i32)]
        + [SMEM(page_table.shape, i32), SMEM(lengths.shape, i32)],
        in_specs=[hbm] * 5,
        out_specs=[vmem] * count + [smem] * 6,
        scratch_shapes=[
            SMEM(move_cols.shape, i32),
            VMEM(q.shape, bf16),
            VMEM(kv.shape, bf16),
            pltpu.SemaphoreType.DMA((5,)),
        ],
        compiler_params=pltpu.CompilerParams(vmem_limit_bytes=4 * mib),
        name="pack",
    )(*map(in_hbm, (move_cols, page_table, lengths, q, kv)))

    def rows_state(rows):
        return [
            VMEM((rows + 1, heads, columns), bf16),
            VMEM((rows, HD, columns), bf16),
            VMEM((rows, HD, columns), bf16),
        ]

    def work_state(rows):
        return [
            VMEM((slots + far_chunk, heads, block), f32),
            VMEM((rows, heads, HD), f32),
        ] + [VMEM((rows + 1, heads, HD), f32)] * 4

    anyspace = pl.BlockSpec(memory_space=pl.ANY)
    blocks = SMEM((slots + far_chunk + 1,), i32)
    pool_copy = VMEM((slots + far_chunk,) + kv_pool.shape[1:], bf16)
    staged = VMEM((rows_inst, heads, HD), bf16)

    def rest(which, kv_pool, q, kv, hidden, rank, slot, pages, sizes, *packed):
        received = [lax.ppermute(x, "inst", links.forward(which, j)) for j, x in enumerate(packed)]
        buf, near_buf, qbd, fk, fv, page, owner, limit, counts, far_owner, far_limit = pl.pallas_call(
            functools.partial(list_kernel, links, chunk, far_chunk, slots // 2),
            out_shape=[pool_copy, pool_copy]
            + rows_state(rows_inst)
            + [blocks, blocks, blocks, SMEM((3,), i32), blocks, blocks],
            in_specs=[smem] * 3 + [hbm] * 3,
            out_specs=[vmem] * 5 + [smem] * 6,
            scratch_shapes=[
                VMEM(q.shape, bf16),
                VMEM(kv.shape, bf16),
                pltpu.SemaphoreType.DMA((2,)),
                pltpu.SemaphoreType.DMA((2, slots)),
            ],
            compiler_params=pltpu.CompilerParams(vmem_limit_bytes=4 * mib),
            cost_estimate=pl.CostEstimate(flops=2**27, bytes_accessed=2**23, transcendentals=2**18),
            name="list",
        )(slot, pages, sizes, *map(in_hbm, (q, kv, kv_pool)))
        back = pl.pallas_call(
            functools.partial(moved_kernel, links, chunk, far_chunk, steps),
            out_shape=[jax.ShapeDtypeStruct((heads, HD), bf16)] * count,
            in_specs=[smem] * 4 + [vmem] + [vmem] * count,
            out_specs=[vmem] * count,
            scratch_shapes=rows_state(CAP) + work_state(CAP),
            compiler_params=pltpu.CompilerParams(vmem_limit_bytes=16 * mib),
            name="moved",
        )(rank, far_owner, far_limit, counts, buf, *received)
        returned = [lax.ppermute(x, "inst", links.backward(which, j)) for j, x in enumerate(back)]
        local, _ = pl.pallas_call(
            functools.partial(stay_kernel, chunk, steps),
            out_shape=[staged, pool_copy],
            in_specs=[smem] * 5 + [hbm] + [vmem] * 4 + [anyspace],
            out_specs=[vmem, vmem],
            input_output_aliases={6: 1},
            scratch_shapes=[pltpu.SemaphoreType.DMA((slots, 2))] + work_state(rows_inst),
            compiler_params=pltpu.CompilerParams(vmem_limit_bytes=16 * mib),
            cost_estimate=pl.CostEstimate(flops=2**27, bytes_accessed=2**23, transcendentals=2**18),
            name="stay",
        )(slot, page, owner, limit, counts, in_hbm(kv_pool), near_buf, qbd, fk, fv, back[-1])
        out = pl.pallas_call(
            functools.partial(place_kernel, links),
            out_shape=HBM((rows_inst, heads, HD), bf16),
            in_specs=[smem, vmem] + [vmem] * count,
            out_specs=hbm,
            scratch_shapes=[staged, pltpu.SemaphoreType.DMA],
            compiler_params=pltpu.CompilerParams(vmem_limit_bytes=4 * mib),
            name="place",
        )(hidden, local, *returned)
        out = out.reshape(rows_inst, heads_all, steps, HD).transpose(0, 2, 1, 3)
        return out.reshape(rows_inst, steps, width)

    operands = (kv_pool, q, kv, hidden, rank, slot, pages, sizes, *packed)
    if links.split:
        return lax.switch(
            branch[0], [functools.partial(rest, k) for k in range(len(links.halves))], *operands
        )
    return rest(0, *operands)


def solution(mesh):
    placed = (
        P(("groups", "inst"), None, None, "tp"),
        P(("groups", "inst"), None),
        P(("groups", "inst")),
        P(("groups", "inst"), None, "tp"),
        P(("groups", "inst"), None, None, "tp"),
        P("groups", None),
    )
    return jax.shard_map(
        body,
        mesh=mesh,
        in_specs=placed,
        out_specs=P(("groups", "inst"), None, "tp"),
        check_vma=False,
    )
```

```python
import functools
import itertools
import math

import jax
import jax.numpy as jnp
from jax import lax
from jax.experimental import pallas as pl
from jax.experimental.pallas import tpu as pltpu
from jax.sharding import PartitionSpec as P

HD = 128
CAP = 2
NEG = -1e30
MAX_SPLITS = 3
SMEM = pltpu.SMEM
VMEM = pltpu.VMEM
HBM = pltpu.HBM


class Links:
    def __init__(self, n):
        self.n = n
        half = n // 2
        self.halves = []
        if n % 2 == 0 and math.comb(n, half) <= 2 * MAX_SPLITS:
            self.halves = [c for c in itertools.combinations(range(n), half) if 0 in c]
        self.split = bool(self.halves)
        self.count = half if self.split else n - 1

    def index(self, busy, a, b):
        n = self.n
        if self.split:
            half = n // 2
            rank_a = sum(jnp.where(k < a, busy[k], 0) for k in range(n))
            rank_b = sum(jnp.where(k < b, 1 - busy[k], 0) for k in range(n))
            shift = jnp.where(busy[0] == 1, rank_b - rank_a, rank_a - rank_b)
            return half - 1 - lax.rem(shift + half, half)
        if n & (n - 1) == 0:
            return (a ^ b) - 1
        return lax.rem(a - b + n, n) - 1

    def branch(self, busy):
        mask = sum(jnp.where(busy[k] == busy[0], 1 << k, 0) for k in range(self.n))
        return sum(
            jnp.where(mask == sum(1 << i for i in half), k, 0) for k, half in enumerate(self.halves)
        )

    def forward(self, which, j):
        n = self.n
        if self.split:
            half = self.halves[which]
            other = [i for i in range(n) if i not in half]
            shift = self.count - 1 - j
            pairs = [(a, other[(k + shift) % len(other)]) for k, a in enumerate(half)]
            return sorted(pairs + [(b, a) for a, b in pairs])
        if n & (n - 1) == 0:
            return [(i, i ^ (j + 1)) for i in range(n)]
        return [(i, (i + j + 1) % n) for i in range(n)]

    def backward(self, which, j):
        return [(b, a) for a, b in self.forward(which, j)]


def find_moves(links, moves, rows_inst, me, hidden, rank, slot):
    n = links.n
    count = links.count
    for j in range(count + 1):
        hidden[j] = -1
        rank[j] = CAP
    for c in range(CAP + 1):
        slot[c] = -1
    total = moves.shape[1]
    busy = None
    if links.split:
        froms = [moves[0, m] // rows_inst for m in range(total)]
        busy = [
            functools.reduce(jnp.bitwise_or, [(f == k).astype(jnp.int32) for f in froms]) for k in range(n)
        ]

    def step(m, seen):
        cache_slot = moves[0, m]
        hidden_slot = moves[1, m]
        from_inst = cache_slot // rows_inst
        to_inst = hidden_slot // rows_inst
        index = links.index(busy, from_inst, to_inst)
        hidden[jnp.where(to_inst == me, index, count)] = lax.rem(hidden_slot, rows_inst)
        mine = from_inst == me
        rank[jnp.where(mine, index, count)] = seen
        slot[jnp.where(mine, seen, CAP)] = lax.rem(cache_slot, rows_inst)
        return jnp.where(mine, seen + 1, seen)

    if links.split:
        seen = jnp.int32(0)
        for m in range(total):
            seen = step(m, seen)
    else:
        lax.fori_loop(0, total, step, jnp.int32(0))
    return busy


def pack_kernel(links, moves_hbm, page_hbm, length_hbm, q_hbm, kv_hbm, *refs):
    outs = refs[: links.count]
    branch, hidden, rank, slot, page_table, lengths, moves, q, kv, sems = refs[links.count :]
    copies = [
        pltpu.make_async_copy(src, dst, sems.at[i])
        for i, (src, dst) in enumerate(
            [(moves_hbm, moves), (q_hbm, q), (kv_hbm, kv), (page_hbm, page_table), (length_hbm, lengths)]
        )
    ]
    for c in copies:
        c.start()
    rows_inst, heads, _ = q.shape
    me = lax.axis_index("inst")
    copies[0].wait()
    busy = find_moves(links, moves, rows_inst, me, hidden, rank, slot)
    branch[0] = links.branch(busy) if links.split else 0
    copies[1].wait()
    copies[2].wait()
    for j, out in enumerate(outs):
        row = jnp.maximum(hidden[j], 0)
        out[0:heads, :] = q[row]
        out[heads:, :] = kv[row]
    copies[3].wait()
    copies[4].wait()


def set_row(at, rows, fresh, qbd, fk, fv, groups):
    heads, hd = rows.shape
    per = heads // groups
    zero = jnp.zeros((per, hd), jnp.bfloat16)
    for g in range(groups):
        for k in range(groups):
            qbd[at, g * per : (g + 1) * per, k * hd : (k + 1) * hd] = (
                rows[g * per : (g + 1) * per] if k == g else zero
            )
    if fk is None:
        return
    fresh = fresh.astype(jnp.float32)
    token = lax.broadcasted_iota(jnp.int32, (16, hd), 0)
    for plane, ref in enumerate((fk, fv)):
        for g in range(groups):
            block = jnp.zeros((16, hd), jnp.float32)
            for u in range(fresh.shape[0] // (2 * groups)):
                line = (u * groups + g) * 2 + plane
                block = jnp.where(token == u, fresh[line : line + 1], block)
            ref[at, 0:16, g * hd : (g + 1) * hd] = block.astype(jnp.bfloat16)


def attend_list(rows, ahead, chunk, steps, lists, count, wait, buf, qbd, fk, fv, scores, new, part_max, top, part_sum, acc):
    owner, limit = lists
    _, heads, columns = qbd.shape
    hd = acc.shape[2]
    groups = columns // hd
    per = heads // groups
    block = buf.shape[2]
    factor = math.log2(math.e) / math.sqrt(hd)
    loops = lax.div(count - ahead + (chunk - 1), jnp.int32(chunk))
    keys_of = (((1,), (1,)), ((), ()))
    values_of = (((1,), (0,)), ((), ()))
    lane = lax.broadcasted_iota(jnp.int32, (heads, block), 1)
    token = lax.broadcasted_iota(jnp.int32, (heads, hd), 1)
    seen = token <= lax.broadcasted_iota(jnp.int32, (heads, hd), 0) % steps

    def diagonal(o):
        return jnp.concatenate(
            [o[g * per : (g + 1) * per, g * hd : (g + 1) * hd] for g in range(groups)], axis=0
        )

    def first(k):
        r = owner[k]
        s = lax.dot_general(qbd[r], buf[k, 0], keys_of, preferred_element_type=jnp.float32)
        s = jnp.where(lane < limit[k], s, NEG)
        scores[k] = s
        m = s[:, 0:hd]
        for c in range(1, block // hd):
            m = jnp.maximum(m, s[:, c * hd : (c + 1) * hd])
        part_max[r] = jnp.maximum(part_max[r], m)

    def second(k):
        r = owner[k]
        m = top[r]
        pieces = []
        total = jnp.zeros((heads, hd), jnp.float32)
        for c in range(block // hd):
            e = jnp.exp2((scores[k, :, c * hd : (c + 1) * hd] - m) * factor)
            total = total + e
            pieces.append(e.astype(jnp.bfloat16))
        o = lax.dot_general(
            jnp.concatenate(pieces, axis=1), buf[k, 1], values_of, preferred_element_type=jnp.float32
        )
        part_sum[r] = part_sum[r] + total
        acc[r] = acc[r] + diagonal(o)

    def several(do, plane, at, number):
        for j in range(number):
            wait(at + j, plane)
        for j in range(number):
            do(at + j)

    def others(do, plane):
        def step(i, carry):
            several(do, plane, ahead + i * chunk, chunk)
            return carry

        lax.fori_loop(0, loops, step, 0)

    for r in range(rows):
        s = lax.dot_general(qbd[r], fk[r], keys_of, preferred_element_type=jnp.float32)
        s = jnp.where(seen, s, NEG)
        new[r] = s
        part_max[r] = s
    part_max[rows] = jnp.zeros((heads, hd), jnp.float32)
    several(first, 0, 0, ahead)
    others(first, 0)

    top[rows] = jnp.zeros((heads, hd), jnp.float32)
    part_sum[rows] = jnp.zeros((heads, hd), jnp.float32)
    acc[rows] = jnp.zeros((heads, hd), jnp.float32)
    for r in range(rows):
        m = jnp.broadcast_to(jnp.max(part_max[r], axis=1, keepdims=True), (heads, hd))
        top[r] = m
        e = jnp.exp2((new[r] - m) * factor)
        part_sum[r] = e
        acc[r] = diagonal(
            lax.dot_general(e.astype(jnp.bfloat16), fv[r], values_of, preferred_element_type=jnp.float32)
        )
    several(second, 1, 0, ahead)
    others(second, 1)
    for r in range(rows):
        acc[r] = acc[r] / jnp.sum(part_sum[r], axis=1, keepdims=True)


def list_kernel(links, chunk, far_chunk, early, slot, page_table, lengths, q_hbm, kv_hbm, pool, *refs):
    buf, near_buf, qbd, fk, fv, page, owner, limit, counts, far_owner, far_limit, q, kv, small_sems, sems = refs
    rows_inst, heads, hd = q.shape
    slots, _, block, columns = pool.shape
    groups = columns // hd
    small = [
        pltpu.make_async_copy(src, dst, small_sems.at[i])
        for i, (src, dst) in enumerate([(q_hbm, q), (kv_hbm, kv)])
    ]
    for c in small:
        c.start()

    def fetch(number, k):
        return pltpu.make_async_copy(pool.at[number], buf.at[k], sems.at[0, k])

    def fetch_near(number, k):
        return pltpu.make_async_copy(pool.at[number], near_buf.at[k], sems.at[1, k])

    def blocks_of(r):
        return lax.div(lengths[r] + (block - 1), jnp.int32(block))

    far = jnp.int32(0)
    for c in range(CAP):
        r = jnp.maximum(slot[c], 0)

        def one(b, at, r=r, c=c):
            fetch(page_table[r, b], at).start()
            far_owner[at] = c
            far_limit[at] = lengths[r] - b * block
            return at + 1

        far = lax.fori_loop(0, jnp.where(slot[c] >= 0, blocks_of(r), 0), one, far)

    def row(r, near):
        moved = functools.reduce(jnp.logical_or, [slot[c] == r for c in range(CAP)])

        def one(b, at):
            page[at] = page_table[r, b]
            owner[at] = r
            limit[at] = lengths[r] - b * block
            return at + 1

        return lax.fori_loop(0, jnp.where(moved, 0, blocks_of(r)), one, near)

    near = lax.fori_loop(0, rows_inst, row, jnp.int32(0))
    begun = jnp.minimum(jnp.maximum(early - far, 0), near)
    counts[0] = near
    counts[1] = far
    counts[2] = begun

    def begin(k, carry):
        fetch_near(page[k], k).start()
        return carry

    lax.fori_loop(0, begun, begin, 0)
    for j in range(chunk):
        owner[near + j] = rows_inst
        limit[near + j] = 0
    for j in range(far_chunk):
        far_owner[far + j] = CAP
        far_limit[far + j] = 0

    fk[...] = jnp.zeros(fk.shape, fk.dtype)
    fv[...] = jnp.zeros(fv.shape, fv.dtype)
    for c in small:
        c.wait()
    for r in range(rows_inst):
        set_row(r, q[r], kv[r], qbd, fk, fv, groups)
    set_row(rows_inst, q[0], None, qbd, None, None, groups)

    def arrived(k, carry):
        fetch(0, k).wait()
        return carry

    def arrived_near(k, carry):
        fetch_near(0, k).wait()
        return carry

    lax.fori_loop(0, far, arrived, 0)
    lax.fori_loop(0, begun, arrived_near, 0)


def stay_kernel(chunk, steps, slot, page, owner, limit, counts, pool, begun_buf, qbd, fk, fv, order, *refs):
    local, buf, sems, *work = refs
    rows_inst = local.shape[0]
    count, begun = counts[0], counts[2]

    def fetch(number, k, plane):
        return pltpu.make_async_copy(pool.at[number, plane], buf.at[k, plane], sems.at[k, plane])

    for plane in range(2):

        def start(k, carry, plane=plane):
            fetch(page[k], k, plane).start()
            return carry

        lax.fori_loop(begun, count, start, 0)

    def wait(k, plane):
        @pl.when((k >= begun) & (k < count))
        def _():
            fetch(0, k, plane).wait()

    attend_list(rows_inst, chunk, chunk, steps, (owner, limit), count, wait, buf, qbd, fk, fv, *work)
    acc = work[-1]
    for r in range(rows_inst):
        vacant = functools.reduce(jnp.logical_or, [slot[c] == r for c in range(CAP)])
        local[r] = jnp.where(vacant, 0.0, acc[r]).astype(jnp.bfloat16)


def moved_kernel(links, ahead, chunk, steps, rank, far_owner, far_limit, counts, buf, *refs):
    recv, back = refs[: links.count], refs[links.count : 2 * links.count]
    qbd, fk, fv, *work = refs[2 * links.count :]
    acc = work[-1]
    heads = qbd.shape[1]
    groups = qbd.shape[2] // acc.shape[2]
    count = counts[1]

    @pl.when(count > 0)
    def _():
        fk[:, 16:, :] = jnp.zeros((CAP, fk.shape[1] - 16, fk.shape[2]), fk.dtype)
        fv[:, 16:, :] = jnp.zeros((CAP, fv.shape[1] - 16, fv.shape[2]), fv.dtype)
        for j in range(links.count):

            def put(j=j):
                set_row(rank[j], recv[j][0:heads, :], recv[j][heads:, :], qbd, fk, fv, groups)

            if links.count == CAP:
                put()
            else:
                pl.when(rank[j] < CAP)(put)
        attend_list(
            CAP, ahead, chunk, steps, (far_owner, far_limit), count, lambda k, plane: None,
            buf, qbd, fk, fv, *work,
        )
        for j in range(links.count):
            back[j][...] = acc[rank[j]].astype(jnp.bfloat16)


def place_kernel(links, hidden, local, *refs):
    back, (out, staged, sem) = refs[: links.count], refs[links.count :]
    staged[...] = local[...]
    for j, ref in enumerate(back):

        def put(ref=ref, j=j):
            staged[hidden[j]] = ref[...]

        pl.when(hidden[j] >= 0)(put)

    write = pltpu.make_async_copy(staged, out, sem)
    write.start()
    write.wait()


def body(kv_pool, page_table, lengths, queries, new_kv, moves):
    links = Links(lax.axis_size("inst"))
    rows_inst, steps, width = queries.shape
    slots, _, block, columns = kv_pool.shape
    groups = columns // HD
    heads_all = width // HD
    heads = steps * heads_all
    fresh_rows = steps * groups * 2
    bf16 = jnp.bfloat16
    f32 = jnp.float32
    i32 = jnp.int32
    q = queries.reshape(rows_inst, steps, heads_all, HD).transpose(0, 2, 1, 3).reshape(rows_inst, heads, HD)
    kv = (
        new_kv.reshape(rows_inst, steps, 2, groups, HD)
        .transpose(0, 1, 3, 2, 4)
        .reshape(rows_inst, fresh_rows, HD)
    )
    smem = pl.BlockSpec(memory_space=SMEM)
    vmem = pl.BlockSpec(memory_space=VMEM)
    hbm = pl.BlockSpec(memory_space=HBM)
    in_hbm = lambda x: pltpu.with_memory_space_constraint(x, HBM)
    move_cols = moves.T
    count = links.count
    chunk = 4
    far_chunk = 6
    mib = 1024 * 1024

    *packed, branch, hidden, rank, slot, pages, sizes = pl.pallas_call(
        functools.partial(pack_kernel, links),
        out_shape=[jax.ShapeDtypeStruct((heads + fresh_rows, HD), bf16)] * count
        + [SMEM((1,), i32), SMEM((count + 1,), i32), SMEM((count + 1,), i32), SMEM((CAP + 1,), i32)]
        + [SMEM(page_table.shape, i32), SMEM(lengths.shape, i32)],
        in_specs=[hbm] * 5,
        out_specs=[vmem] * count + [smem] * 6,
        scratch_shapes=[
            SMEM(move_cols.shape, i32),
            VMEM(q.shape, bf16),
            VMEM(kv.shape, bf16),
            pltpu.SemaphoreType.DMA((5,)),
        ],
        compiler_params=pltpu.CompilerParams(vmem_limit_bytes=4 * mib),
        name="pack",
    )(*map(in_hbm, (move_cols, page_table, lengths, q, kv)))

    def rows_state(rows):
        return [
            VMEM((rows + 1, heads, columns), bf16),
            VMEM((rows, HD, columns), bf16),
            VMEM((rows, HD, columns), bf16),
        ]

    def work_state(rows):
        return [
            VMEM((slots + far_chunk, heads, block), f32),
            VMEM((rows, heads, HD), f32),
        ] + [VMEM((rows + 1, heads, HD), f32)] * 4

    anyspace = pl.BlockSpec(memory_space=pl.ANY)
    blocks = SMEM((slots + far_chunk + 1,), i32)
    pool_copy = VMEM((slots + far_chunk,) + kv_pool.shape[1:], bf16)
    staged = VMEM((rows_inst, heads, HD), bf16)

    def rest(which, kv_pool, q, kv, hidden, rank, slot, pages, sizes, *packed):
        received = [lax.ppermute(x, "inst", links.forward(which, j)) for j, x in enumerate(packed)]
        buf, near_buf, qbd, fk, fv, page, owner, limit, counts, far_owner, far_limit = pl.pallas_call(
            functools.partial(list_kernel, links, chunk, far_chunk, slots // 2),
            out_shape=[pool_copy, pool_copy]
            + rows_state(rows_inst)
            + [blocks, blocks, blocks, SMEM((3,), i32), blocks, blocks],
            in_specs=[smem] * 3 + [hbm] * 3,
            out_specs=[vmem] * 5 + [smem] * 6,
            scratch_shapes=[
                VMEM(q.shape, bf16),
                VMEM(kv.shape, bf16),
                pltpu.SemaphoreType.DMA((2,)),
                pltpu.SemaphoreType.DMA((2, slots)),
            ],
            compiler_params=pltpu.CompilerParams(vmem_limit_bytes=4 * mib),
            cost_estimate=pl.CostEstimate(flops=2**27, bytes_accessed=2**23, transcendentals=2**18),
            name="list",
        )(slot, pages, sizes, *map(in_hbm, (q, kv, kv_pool)))
        back = pl.pallas_call(
            functools.partial(moved_kernel, links, chunk, far_chunk, steps),
            out_shape=[jax.ShapeDtypeStruct((heads, HD), bf16)] * count,
            in_specs=[smem] * 4 + [vmem] + [vmem] * count,
            out_specs=[vmem] * count,
            scratch_shapes=rows_state(CAP) + work_state(CAP),
            compiler_params=pltpu.CompilerParams(vmem_limit_bytes=16 * mib),
            name="moved",
        )(rank, far_owner, far_limit, counts, buf, *received)
        returned = [lax.ppermute(x, "inst", links.backward(which, j)) for j, x in enumerate(back)]
        local, _ = pl.pallas_call(
            functools.partial(stay_kernel, chunk, steps),
            out_shape=[staged, pool_copy],
            in_specs=[smem] * 5 + [hbm] + [vmem] * 4 + [anyspace],
            out_specs=[vmem, vmem],
            input_output_aliases={6: 1},
            scratch_shapes=[pltpu.SemaphoreType.DMA((slots, 2))] + work_state(rows_inst),
            compiler_params=pltpu.CompilerParams(vmem_limit_bytes=16 * mib),
            cost_estimate=pl.CostEstimate(flops=2**27, bytes_accessed=2**23, transcendentals=2**18),
            name="stay",
        )(slot, page, owner, limit, counts, in_hbm(kv_pool), near_buf, qbd, fk, fv, back[-1])
        out = pl.pallas_call(
            functools.partial(place_kernel, links),
            out_shape=HBM((rows_inst, heads, HD), bf16),
            in_specs=[smem, vmem] + [vmem] * count,
            out_specs=hbm,
            scratch_shapes=[staged, pltpu.SemaphoreType.DMA],
            compiler_params=pltpu.CompilerParams(vmem_limit_bytes=4 * mib),
            name="place",
        )(hidden, local, *returned)
        out = out.reshape(rows_inst, heads_all, steps, HD).transpose(0, 2, 1, 3)
        return out.reshape(rows_inst, steps, width)

    operands = (kv_pool, q, kv, hidden, rank, slot, pages, sizes, *packed)
    if links.split:
        return lax.switch(
            branch[0], [functools.partial(rest, k) for k in range(len(links.halves))], *operands
        )
    return rest(0, *operands)


def solution(mesh):
    placed = (
        P(("groups", "inst"), None, None, "tp"),
        P(("groups", "inst"), None),
        P(("groups", "inst")),
        P(("groups", "inst"), None, "tp"),
        P(("groups", "inst"), None, None, "tp"),
        P("groups", None),
    )
    return jax.shard_map(
        body,
        mesh=mesh,
        in_specs=placed,
        out_specs=P(("groups", "inst"), None, "tp"),
        check_vma=False,
    )
```

```python
import functools
import itertools
import math

import jax
import jax.numpy as jnp
from jax import lax
from jax.experimental import pallas as pl
from jax.experimental.pallas import tpu as pltpu
from jax.sharding import PartitionSpec as P

HD = 128
CAP = 2
NEG = -1e30
MAX_SPLITS = 3
SMEM = pltpu.SMEM
VMEM = pltpu.VMEM
HBM = pltpu.HBM


class Links:
    def __init__(self, n):
        self.n = n
        half = n // 2
        self.halves = []
        if n % 2 == 0 and math.comb(n, half) <= 2 * MAX_SPLITS:
            self.halves = [c for c in itertools.combinations(range(n), half) if 0 in c]
        self.split = bool(self.halves)
        self.count = half if self.split else n - 1

    def index(self, busy, a, b):
        n = self.n
        if self.split:
            half = n // 2
            rank_a = sum(jnp.where(k < a, busy[k], 0) for k in range(n))
            rank_b = sum(jnp.where(k < b, 1 - busy[k], 0) for k in range(n))
            shift = jnp.where(busy[0] == 1, rank_b - rank_a, rank_a - rank_b)
            return half - 1 - lax.rem(shift + half, half)
        if n & (n - 1) == 0:
            return (a ^ b) - 1
        return lax.rem(a - b + n, n) - 1

    def branch(self, busy):
        mask = sum(jnp.where(busy[k] == busy[0], 1 << k, 0) for k in range(self.n))
        return sum(
            jnp.where(mask == sum(1 << i for i in half), k, 0) for k, half in enumerate(self.halves)
        )

    def forward(self, which, j):
        n = self.n
        if self.split:
            half = self.halves[which]
            other = [i for i in range(n) if i not in half]
            shift = self.count - 1 - j
            pairs = [(a, other[(k + shift) % len(other)]) for k, a in enumerate(half)]
            return sorted(pairs + [(b, a) for a, b in pairs])
        if n & (n - 1) == 0:
            return [(i, i ^ (j + 1)) for i in range(n)]
        return [(i, (i + j + 1) % n) for i in range(n)]

    def backward(self, which, j):
        return [(b, a) for a, b in self.forward(which, j)]


def find_moves(links, moves, rows_inst, me, hidden, rank, slot):
    n = links.n
    count = links.count
    for j in range(count + 1):
        hidden[j] = -1
        rank[j] = CAP
    for c in range(CAP + 1):
        slot[c] = -1
    total = moves.shape[1]
    busy = None
    if links.split:
        froms = [moves[0, m] // rows_inst for m in range(total)]
        busy = [
            functools.reduce(jnp.bitwise_or, [(f == k).astype(jnp.int32) for f in froms]) for k in range(n)
        ]

    def step(m, seen):
        cache_slot = moves[0, m]
        hidden_slot = moves[1, m]
        from_inst = cache_slot // rows_inst
        to_inst = hidden_slot // rows_inst
        index = links.index(busy, from_inst, to_inst)
        hidden[jnp.where(to_inst == me, index, count)] = lax.rem(hidden_slot, rows_inst)
        mine = from_inst == me
        rank[jnp.where(mine, index, count)] = seen
        slot[jnp.where(mine, seen, CAP)] = lax.rem(cache_slot, rows_inst)
        return jnp.where(mine, seen + 1, seen)

    if links.split:
        seen = jnp.int32(0)
        for m in range(total):
            seen = step(m, seen)
    else:
        lax.fori_loop(0, total, step, jnp.int32(0))
    return busy


def pack_kernel(links, moves_hbm, page_hbm, length_hbm, q_hbm, kv_hbm, *refs):
    outs = refs[: links.count]
    branch, hidden, rank, slot, page_table, lengths, moves, q, kv, sems = refs[links.count :]
    copies = [
        pltpu.make_async_copy(src, dst, sems.at[i])
        for i, (src, dst) in enumerate(
            [(moves_hbm, moves), (q_hbm, q), (kv_hbm, kv), (page_hbm, page_table), (length_hbm, lengths)]
        )
    ]
    for c in copies:
        c.start()
    rows_inst, heads, _ = q.shape
    me = lax.axis_index("inst")
    copies[0].wait()
    busy = find_moves(links, moves, rows_inst, me, hidden, rank, slot)
    branch[0] = links.branch(busy) if links.split else 0
    copies[1].wait()
    copies[2].wait()
    for j, out in enumerate(outs):
        row = jnp.maximum(hidden[j], 0)
        out[0:heads, :] = q[row]
        out[heads:, :] = kv[row]
    copies[3].wait()
    copies[4].wait()


def set_row(at, rows, fresh, qbd, fk, fv, groups):
    heads, hd = rows.shape
    per = heads // groups
    zero = jnp.zeros((per, hd), jnp.bfloat16)
    for g in range(groups):
        for k in range(groups):
            qbd[at, g * per : (g + 1) * per, k * hd : (k + 1) * hd] = (
                rows[g * per : (g + 1) * per] if k == g else zero
            )
    if fk is None:
        return
    fresh = fresh.astype(jnp.float32)
    token = lax.broadcasted_iota(jnp.int32, (16, hd), 0)
    for plane, ref in enumerate((fk, fv)):
        for g in range(groups):
            block = jnp.zeros((16, hd), jnp.float32)
            for u in range(fresh.shape[0] // (2 * groups)):
                line = (u * groups + g) * 2 + plane
                block = jnp.where(token == u, fresh[line : line + 1], block)
            ref[at, 0:16, g * hd : (g + 1) * hd] = block.astype(jnp.bfloat16)


def attend_list(rows, ahead, chunk, steps, lists, count, wait, buf, qbd, fk, fv, scores, new, part_max, top, part_sum, acc):
    owner, limit = lists
    _, heads, columns = qbd.shape
    hd = acc.shape[2]
    groups = columns // hd
    per = heads // groups
    block = buf.shape[2]
    factor = math.log2(math.e) / math.sqrt(hd)
    loops = lax.div(count - ahead + (chunk - 1), jnp.int32(chunk))
    keys_of = (((1,), (1,)), ((), ()))
    values_of = (((1,), (0,)), ((), ()))
    lane = lax.broadcasted_iota(jnp.int32, (heads, block), 1)
    token = lax.broadcasted_iota(jnp.int32, (heads, hd), 1)
    seen = token <= lax.broadcasted_iota(jnp.int32, (heads, hd), 0) % steps

    def diagonal(o):
        return jnp.concatenate(
            [o[g * per : (g + 1) * per, g * hd : (g + 1) * hd] for g in range(groups)], axis=0
        )

    def first(k):
        r = owner[k]
        s = lax.dot_general(qbd[r], buf[k, 0], keys_of, preferred_element_type=jnp.float32)
        s = jnp.where(lane < limit[k], s, NEG)
        scores[k] = s
        m = s[:, 0:hd]
        for c in range(1, block // hd):
            m = jnp.maximum(m, s[:, c * hd : (c + 1) * hd])
        part_max[r] = jnp.maximum(part_max[r], m)

    def second(k):
        r = owner[k]
        m = top[r]
        pieces = []
        total = jnp.zeros((heads, hd), jnp.float32)
        for c in range(block // hd):
            e = jnp.exp2((scores[k, :, c * hd : (c + 1) * hd] - m) * factor)
            total = total + e
            pieces.append(e.astype(jnp.bfloat16))
        o = lax.dot_general(
            jnp.concatenate(pieces, axis=1), buf[k, 1], values_of, preferred_element_type=jnp.float32
        )
        part_sum[r] = part_sum[r] + total
        acc[r] = acc[r] + diagonal(o)

    def several(do, plane, at, number):
        for j in range(number):
            wait(at + j, plane)
        for j in range(number):
            do(at + j)

    def others(do, plane):
        def step(i, carry):
            several(do, plane, ahead + i * chunk, chunk)
            return carry

        lax.fori_loop(0, loops, step, 0)

    for r in range(rows):
        s = lax.dot_general(qbd[r], fk[r], keys_of, preferred_element_type=jnp.float32)
        s = jnp.where(seen, s, NEG)
        new[r] = s
        part_max[r] = s
    part_max[rows] = jnp.zeros((heads, hd), jnp.float32)
    several(first, 0, 0, ahead)
    others(first, 0)

    top[rows] = jnp.zeros((heads, hd), jnp.float32)
    part_sum[rows] = jnp.zeros((heads, hd), jnp.float32)
    acc[rows] = jnp.zeros((heads, hd), jnp.float32)
    for r in range(rows):
        m = jnp.broadcast_to(jnp.max(part_max[r], axis=1, keepdims=True), (heads, hd))
        top[r] = m
        e = jnp.exp2((new[r] - m) * factor)
        part_sum[r] = e
        acc[r] = diagonal(
            lax.dot_general(e.astype(jnp.bfloat16), fv[r], values_of, preferred_element_type=jnp.float32)
        )
    several(second, 1, 0, ahead)
    others(second, 1)
    for r in range(rows):
        acc[r] = acc[r] / jnp.sum(part_sum[r], axis=1, keepdims=True)


def list_kernel(links, chunk, far_chunk, early, slot, page_table, lengths, q_hbm, kv_hbm, pool, *refs):
    buf, near_buf, qbd, fk, fv, page, owner, limit, counts, far_owner, far_limit, q, kv, small_sems, sems = refs
    rows_inst, heads, hd = q.shape
    slots, _, block, columns = pool.shape
    groups = columns // hd
    small = [
        pltpu.make_async_copy(src, dst, small_sems.at[i])
        for i, (src, dst) in enumerate([(q_hbm, q), (kv_hbm, kv)])
    ]
    for c in small:
        c.start()

    def fetch(number, k):
        return pltpu.make_async_copy(pool.at[number], buf.at[k], sems.at[0, k])

    def fetch_near(number, k):
        return pltpu.make_async_copy(pool.at[number], near_buf.at[k], sems.at[1, k])

    def blocks_of(r):
        return lax.div(lengths[r] + (block - 1), jnp.int32(block))

    far = jnp.int32(0)
    for c in range(CAP):
        r = jnp.maximum(slot[c], 0)

        def one(b, at, r=r, c=c):
            fetch(page_table[r, b], at).start()
            far_owner[at] = c
            far_limit[at] = lengths[r] - b * block
            return at + 1

        far = lax.fori_loop(0, jnp.where(slot[c] >= 0, blocks_of(r), 0), one, far)

    def row(r, near):
        moved = functools.reduce(jnp.logical_or, [slot[c] == r for c in range(CAP)])

        def one(b, at):
            page[at] = page_table[r, b]
            owner[at] = r
            limit[at] = lengths[r] - b * block
            return at + 1

        return lax.fori_loop(0, jnp.where(moved, 0, blocks_of(r)), one, near)

    near = lax.fori_loop(0, rows_inst, row, jnp.int32(0))
    begun = jnp.minimum(jnp.maximum(early - 2 * far, 0), near)
    counts[0] = near
    counts[1] = far
    counts[2] = begun

    def begin(k, carry):
        fetch_near(page[k], k).start()
        return carry

    lax.fori_loop(0, begun, begin, 0)
    for j in range(chunk):
        owner[near + j] = rows_inst
        limit[near + j] = 0
    for j in range(far_chunk):
        far_owner[far + j] = CAP
        far_limit[far + j] = 0

    fk[...] = jnp.zeros(fk.shape, fk.dtype)
    fv[...] = jnp.zeros(fv.shape, fv.dtype)
    for c in small:
        c.wait()
    for r in range(rows_inst):
        set_row(r, q[r], kv[r], qbd, fk, fv, groups)
    set_row(rows_inst, q[0], None, qbd, None, None, groups)

    def arrived(k, carry):
        fetch(0, k).wait()
        return carry

    def arrived_near(k, carry):
        fetch_near(0, k).wait()
        return carry

    lax.fori_loop(0, far, arrived, 0)
    lax.fori_loop(0, begun, arrived_near, 0)


def stay_kernel(chunk, steps, slot, page, owner, limit, counts, pool, begun_buf, qbd, fk, fv, order, *refs):
    local, buf, sems, *work = refs
    rows_inst = local.shape[0]
    count, begun = counts[0], counts[2]

    def fetch(number, k, plane):
        return pltpu.make_async_copy(pool.at[number, plane], buf.at[k, plane], sems.at[k, plane])

    for plane in range(2):

        def start(k, carry, plane=plane):
            fetch(page[k], k, plane).start()
            return carry

        lax.fori_loop(begun, count, start, 0)

    def wait(k, plane):
        @pl.when((k >= begun) & (k < count))
        def _():
            fetch(0, k, plane).wait()

    attend_list(rows_inst, chunk, chunk, steps, (owner, limit), count, wait, buf, qbd, fk, fv, *work)
    acc = work[-1]
    for r in range(rows_inst):
        vacant = functools.reduce(jnp.logical_or, [slot[c] == r for c in range(CAP)])
        local[r] = jnp.where(vacant, 0.0, acc[r]).astype(jnp.bfloat16)


def moved_kernel(links, ahead, chunk, steps, rank, far_owner, far_limit, counts, buf, *refs):
    recv, back = refs[: links.count], refs[links.count : 2 * links.count]
    qbd, fk, fv, *work = refs[2 * links.count :]
    acc = work[-1]
    heads = qbd.shape[1]
    groups = qbd.shape[2] // acc.shape[2]
    count = counts[1]

    @pl.when(count > 0)
    def _():
        fk[:, 16:, :] = jnp.zeros((CAP, fk.shape[1] - 16, fk.shape[2]), fk.dtype)
        fv[:, 16:, :] = jnp.zeros((CAP, fv.shape[1] - 16, fv.shape[2]), fv.dtype)
        for j in range(links.count):

            def put(j=j):
                set_row(rank[j], recv[j][0:heads, :], recv[j][heads:, :], qbd, fk, fv, groups)

            if links.count == CAP:
                put()
            else:
                pl.when(rank[j] < CAP)(put)
        attend_list(
            CAP, ahead, chunk, steps, (far_owner, far_limit), count, lambda k, plane: None,
            buf, qbd, fk, fv, *work,
        )
        for j in range(links.count):
            back[j][...] = acc[rank[j]].astype(jnp.bfloat16)


def place_kernel(links, hidden, local, *refs):
    back, (out, staged, sem) = refs[: links.count], refs[links.count :]
    staged[...] = local[...]
    for j, ref in enumerate(back):

        def put(ref=ref, j=j):
            staged[hidden[j]] = ref[...]

        pl.when(hidden[j] >= 0)(put)

    write = pltpu.make_async_copy(staged, out, sem)
    write.start()
    write.wait()


def body(kv_pool, page_table, lengths, queries, new_kv, moves):
    links = Links(lax.axis_size("inst"))
    rows_inst, steps, width = queries.shape
    slots, _, block, columns = kv_pool.shape
    groups = columns // HD
    heads_all = width // HD
    heads = steps * heads_all
    fresh_rows = steps * groups * 2
    bf16 = jnp.bfloat16
    f32 = jnp.float32
    i32 = jnp.int32
    q = queries.reshape(rows_inst, steps, heads_all, HD).transpose(0, 2, 1, 3).reshape(rows_inst, heads, HD)
    kv = (
        new_kv.reshape(rows_inst, steps, 2, groups, HD)
        .transpose(0, 1, 3, 2, 4)
        .reshape(rows_inst, fresh_rows, HD)
    )
    smem = pl.BlockSpec(memory_space=SMEM)
    vmem = pl.BlockSpec(memory_space=VMEM)
    hbm = pl.BlockSpec(memory_space=HBM)
    in_hbm = lambda x: pltpu.with_memory_space_constraint(x, HBM)
    move_cols = moves.T
    count = links.count
    chunk = 4
    far_chunk = 6
    mib = 1024 * 1024

    *packed, branch, hidden, rank, slot, pages, sizes = pl.pallas_call(
        functools.partial(pack_kernel, links),
        out_shape=[jax.ShapeDtypeStruct((heads + fresh_rows, HD), bf16)] * count
        + [SMEM((1,), i32), SMEM((count + 1,), i32), SMEM((count + 1,), i32), SMEM((CAP + 1,), i32)]
        + [SMEM(page_table.shape, i32), SMEM(lengths.shape, i32)],
        in_specs=[hbm] * 5,
        out_specs=[vmem] * count + [smem] * 6,
        scratch_shapes=[
            SMEM(move_cols.shape, i32),
            VMEM(q.shape, bf16),
            VMEM(kv.shape, bf16),
            pltpu.SemaphoreType.DMA((5,)),
        ],
        compiler_params=pltpu.CompilerParams(vmem_limit_bytes=4 * mib),
        name="pack",
    )(*map(in_hbm, (move_cols, page_table, lengths, q, kv)))

    def rows_state(rows):
        return [
            VMEM((rows + 1, heads, columns), bf16),
            VMEM((rows, HD, columns), bf16),
            VMEM((rows, HD, columns), bf16),
        ]

    def work_state(rows):
        return [
            VMEM((slots + far_chunk, heads, block), f32),
            VMEM((rows, heads, HD), f32),
        ] + [VMEM((rows + 1, heads, HD), f32)] * 4

    anyspace = pl.BlockSpec(memory_space=pl.ANY)
    blocks = SMEM((slots + far_chunk + 1,), i32)
    pool_copy = VMEM((slots + far_chunk,) + kv_pool.shape[1:], bf16)
    staged = VMEM((rows_inst, heads, HD), bf16)

    def rest(which, kv_pool, q, kv, hidden, rank, slot, pages, sizes, *packed):
        received = [lax.ppermute(x, "inst", links.forward(which, j)) for j, x in enumerate(packed)]
        buf, near_buf, qbd, fk, fv, page, owner, limit, counts, far_owner, far_limit = pl.pallas_call(
            functools.partial(list_kernel, links, chunk, far_chunk, slots - CAP),
            out_shape=[pool_copy, pool_copy]
            + rows_state(rows_inst)
            + [blocks, blocks, blocks, SMEM((3,), i32), blocks, blocks],
            in_specs=[smem] * 3 + [hbm] * 3,
            out_specs=[vmem] * 5 + [smem] * 6,
            scratch_shapes=[
                VMEM(q.shape, bf16),
                VMEM(kv.shape, bf16),
                pltpu.SemaphoreType.DMA((2,)),
                pltpu.SemaphoreType.DMA((2, slots)),
            ],
            compiler_params=pltpu.CompilerParams(vmem_limit_bytes=4 * mib),
            cost_estimate=pl.CostEstimate(flops=2**27, bytes_accessed=2**23, transcendentals=2**18),
            name="list",
        )(slot, pages, sizes, *map(in_hbm, (q, kv, kv_pool)))
        back = pl.pallas_call(
            functools.partial(moved_kernel, links, chunk, far_chunk, steps),
            out_shape=[jax.ShapeDtypeStruct((heads, HD), bf16)] * count,
            in_specs=[smem] * 4 + [vmem] + [vmem] * count,
            out_specs=[vmem] * count,
            scratch_shapes=rows_state(CAP) + work_state(CAP),
            compiler_params=pltpu.CompilerParams(vmem_limit_bytes=16 * mib),
            name="moved",
        )(rank, far_owner, far_limit, counts, buf, *received)
        returned = [lax.ppermute(x, "inst", links.backward(which, j)) for j, x in enumerate(back)]
        local, _ = pl.pallas_call(
            functools.partial(stay_kernel, chunk, steps),
            out_shape=[staged, pool_copy],
            in_specs=[smem] * 5 + [hbm] + [vmem] * 4 + [anyspace],
            out_specs=[vmem, vmem],
            input_output_aliases={6: 1},
            scratch_shapes=[pltpu.SemaphoreType.DMA((slots, 2))] + work_state(rows_inst),
            compiler_params=pltpu.CompilerParams(vmem_limit_bytes=16 * mib),
            cost_estimate=pl.CostEstimate(flops=2**27, bytes_accessed=2**23, transcendentals=2**18),
            name="stay",
        )(slot, page, owner, limit, counts, in_hbm(kv_pool), near_buf, qbd, fk, fv, back[-1])
        out = pl.pallas_call(
            functools.partial(place_kernel, links),
            out_shape=HBM((rows_inst, heads, HD), bf16),
            in_specs=[smem, vmem] + [vmem] * count,
            out_specs=hbm,
            scratch_shapes=[staged, pltpu.SemaphoreType.DMA],
            compiler_params=pltpu.CompilerParams(vmem_limit_bytes=4 * mib),
            name="place",
        )(hidden, local, *returned)
        out = out.reshape(rows_inst, heads_all, steps, HD).transpose(0, 2, 1, 3)
        return out.reshape(rows_inst, steps, width)

    operands = (kv_pool, q, kv, hidden, rank, slot, pages, sizes, *packed)
    if links.split:
        return lax.switch(
            branch[0], [functools.partial(rest, k) for k in range(len(links.halves))], *operands
        )
    return rest(0, *operands)


def solution(mesh):
    placed = (
        P(("groups", "inst"), None, None, "tp"),
        P(("groups", "inst"), None),
        P(("groups", "inst")),
        P(("groups", "inst"), None, "tp"),
        P(("groups", "inst"), None, None, "tp"),
        P("groups", None),
    )
    return jax.shard_map(
        body,
        mesh=mesh,
        in_specs=placed,
        out_specs=P(("groups", "inst"), None, "tp"),
        check_vma=False,
    )
```
